32 devices in a mesh: dp: 16 (over z, x, core), tensor: 2 (over y).
Axes of the slice: x: 2, y: 2, z: 4, core: 2. Of those that a mesh axis runs over, the one named last changes fastest.
Arguments:
- page_tokens: bfloat16 [16, 708, 768], P('dp'), may hold values from -6 to 6
- patch_counts: int32 [16], P('dp'), may hold values from 49 to 196, as said below
- token_boxes: int32 [16, 2, 708], P('dp'), may hold values from 0 to 511
- text_weight: bfloat16 [3, 3, 768], replicated, may hold values from -1 to 1
- patch_weight: bfloat16 [9, 768], replicated, may hold values from -1.25 to 1.25
- query_weight: bfloat16 [768, 768], P(None, 'tensor'), may hold values from -0.21875 to 0.21875
- query_bias: bfloat16 [768], P('tensor'), may hold values from -1.5 to 1.5
- key_weight: bfloat16 [768, 768], P(None, 'tensor'), may hold values from -0.21875 to 0.21875
- value_weight: bfloat16 [768, 768], P(None, 'tensor'), may hold values from -0.21875 to 0.21875
- value_bias: bfloat16 [768], P('tensor'), may hold values from -1.5 to 1.5
- out_weight: bfloat16 [768, 768], P('tensor'), may hold values from -0.875 to 0.875
- out_bias: bfloat16 [768], replicated, may hold values from -1.5 to 1.5
- line_table: bfloat16 [32, 12], P(None, 'tensor'), may hold values from -3.5 to 3.5
- width_table: bfloat16 [64, 12], P(None, 'tensor'), may hold values from -3.5 to 3.5
- height_table: bfloat16 [64, 12], P(None, 'tensor'), may hold values from -3.5 to 3.5
- norm1_gain: bfloat16 [768], replicated, may hold values from 0.5 to 1.5
- norm1_shift: bfloat16 [768], replicated, may hold values from -1.5 to 1.5
- inner_weight: bfloat16 [768, 3072], P(None, 'tensor'), may hold values from -0.21875 to 0.21875
- inner_bias: bfloat16 [3072], P('tensor'), may hold values from -1.5 to 1.5
- outer_weight: bfloat16 [3072, 768], P('tensor'), may hold values from -0.109375 to 0.109375
- outer_bias: bfloat16 [768], replicated, may hold values from -1.5 to 1.5
- norm2_gain: bfloat16 [768], replicated, may hold values from 0.5 to 1.5
- norm2_shift: bfloat16 [768], replicated, may hold values from -1.5 to 1.5
- cotangent: bfloat16 [16, 708, 768], P('dp'), may hold values from -6 to 6
Outputs:
- layer_output: bfloat16 [16, 708, 768], P('dp')
- input_grad: bfloat16 [16, 708, 768], P('dp')
- grad_text_weight: float32 [3, 3, 768], P(None, None, 'dp')
- grad_patch_weight: float32 [9, 768], P(None, 'dp')
- grad_query_weight: float32 [768, 768], P('dp', 'tensor')
- grad_query_bias: float32 [768], P('tensor')
- grad_key_weight: float32 [768, 768], P('dp', 'tensor')
- grad_value_weight: float32 [768, 768], P('dp', 'tensor')
- grad_value_bias: float32 [768], P('tensor')
- grad_out_weight: float32 [768, 768], P('tensor', 'dp')
- grad_out_bias: float32 [768], P('dp')
- grad_line_table: float32 [32, 12], P(None, 'tensor')
- grad_width_table: float32 [64, 12], P(None, 'tensor')
- grad_height_table: float32 [64, 12], P(None, 'tensor')
- grad_norm1_gain: float32 [768], P('dp')
- grad_norm1_shift: float32 [768], P('dp')
- grad_inner_weight: float32 [768, 3072], P('dp', 'tensor')
- grad_inner_bias: float32 [3072], P('tensor')
- grad_outer_weight: float32 [3072, 768], P('tensor', 'dp')
- grad_outer_bias: float32 [768], P('dp')
- grad_norm2_gain: float32 [768], P('dp')
- grad_norm2_shift: float32 [768], P('dp')
The draws below stay inside these ranges and needn't reach their ends.
Inputs may be any that keep to these rules, and one draw needn't show every extreme that they name: `patch_counts`: each page has 49 or 196 patches; both occur in every draw.
All inputs are finite; a program needn't handle non-finite values.
Results may differ from the reference program's by a relative error of at most 0.014.
The reference program's roundings to bfloat16 on the way count: a program that leaves them out, or rounds other values in their place, can miss the bound.
Values sent between devices are 32-bit elements; how exact they have to be, the bound alone decides.
No kernel may reach another device: no remote copies, remote signals or barrier semaphores. Data moves between devices by JAX's collectives and lax.ppermute only.
A program may use at most 192 MiB of HBM per device.

```python
import jax
import jax.numpy as jnp
from jax import lax

D = 768
HEADS = 12
FF = 3072
TEXT = 512
GRID_SMALL = 7
GRID_LARGE = 14
BINS_1D = 32
BINS_2D = 64
BIN_WIDTH = 8
SEQ = 708
PAGES = 16


def draw_patch_counts(key, part):
    key = jax.random.fold_in(key, 11)
    larger = jax.random.randint(key, (PAGES,), 0, 2)
    larger = larger.at[0].set(1).at[PAGES - 1].set(0)
    return jnp.where(larger == 1, GRID_LARGE * GRID_LARGE, GRID_SMALL * GRID_SMALL).astype(jnp.int32)


def place_ends(values, stream_key, smallest, top_value):
    shape = values.shape
    spot = [jax.random.randint(jax.random.fold_in(stream_key, axis), (), 0, shape[axis]) for axis in range(len(shape))]
    values = values.at[tuple(spot)].set(smallest)
    longest = shape.index(max(shape))
    spot[longest] = (spot[longest] + 1) % shape[longest]
    return values.at[tuple(spot)].set(top_value)


def with_spikes(values, rng, source, target, parts, factor):
    owner, partner = [(jnp.arange(values.shape[dim]) // (values.shape[dim] // parts)).reshape([-1 if axis == dim else 1 for axis in range(values.ndim)]) for dim in (source, target)]
    chosen = jax.random.permutation(rng, parts)[partner]
    strong = (owner == chosen) | (owner == (partner + parts // 2) % parts)
    return jnp.where(strong, factor * values, values)


def shard_levels(own_key, dims, pieces, least, high):
    def one(dim, blocks):
        steps = jax.random.uniform(jax.random.fold_in(jax.random.fold_in(own_key, 6), dim), (blocks,), jnp.float32, least / len(pieces), high / len(pieces))
        return jnp.repeat(jnp.exp(steps), dims[dim] // blocks).reshape((-1,) + (1,) * (len(dims) - dim - 1))

    loudness = one(*pieces[0])
    for cut in pieces[1:]:
        loudness = loudness * one(*cut)
    return loudness


def noise(stream_key, dims, scale, bound, pieces=(), kind=jnp.bfloat16):
    values = scale * jax.random.normal(stream_key, dims, jnp.float32)
    if pieces:
        values = values * shard_levels(stream_key, dims, pieces, -0.22, 0.18)
    return jnp.clip(values, -bound, bound).astype(kind)


def heavy_noise(stream_key, dims, deviation, limit, cuts, heavy, kind=jnp.bfloat16):
    drawn = deviation * jax.random.normal(stream_key, dims, jnp.float32)
    if cuts:
        drawn = drawn * shard_levels(stream_key, dims, cuts, -0.22, 0.18)
    return jnp.clip(with_spikes(drawn, jax.random.fold_in(stream_key, 3), *heavy), -limit, limit).astype(kind)


def setup_inputs(seed: int = 0) -> dict:
    seeds = jax.random.split(jax.random.key(seed), 25)
    return {
        "page_tokens": noise(seeds[0], (PAGES, SEQ, D), 1.0, 6.0, ((0, 16),)),
        "patch_counts": draw_patch_counts(jax.random.fold_in(seeds[24], 71), 0),
        "token_boxes": place_ends(jax.random.randint(seeds[2], (PAGES, 2, SEQ), 0, BIN_WIDTH * BINS_2D), jax.random.fold_in(seeds[2], 1), 0, (BIN_WIDTH * BINS_2D) - 1).astype(jnp.int32),
        "text_weight": noise(seeds[3], (3, 3, D), 0.2, 1.0),
        "patch_weight": noise(seeds[4], (9, D), 0.25, 1.25),
        "query_weight": noise(seeds[5], (D, D), D ** -0.5, 0.21875, ((1, 2),)),
        "query_bias": noise(seeds[6], (D,), 0.3, 1.5, ((0, 2),)),
        "key_weight": noise(seeds[7], (D, D), D ** -0.5, 0.21875, ((1, 2),)),
        "value_weight": noise(seeds[8], (D, D), D ** -0.5, 0.21875, ((1, 2),)),
        "value_bias": noise(seeds[9], (D,), 0.3, 1.5, ((0, 2),)),
        "out_weight": noise(seeds[10], (D, D), (D // 16) ** -0.5, 0.875, ((0, 2),)),
        "out_bias": noise(seeds[11], (D,), 0.3, 1.5),
        "line_table": noise(seeds[12], (BINS_1D, HEADS), 0.7, 3.5, ((1, 2),)),
        "width_table": noise(seeds[13], (BINS_2D, HEADS), 0.7, 3.5, ((1, 2),)),
        "height_table": noise(seeds[14], (BINS_2D, HEADS), 0.7, 3.5, ((1, 2),)),
        "norm1_gain": jnp.clip(1.0 + 0.1 * jax.random.normal(seeds[15], (D,), jnp.float32), 0.5, 1.5).astype(jnp.bfloat16),
        "norm1_shift": noise(seeds[16], (D,), 0.3, 1.5),
        "inner_weight": noise(seeds[17], (D, FF), D ** -0.5, 0.21875, ((1, 2),)),
        "inner_bias": noise(seeds[18], (FF,), 0.3, 1.5, ((0, 2),)),
        "outer_weight": noise(seeds[19], (FF, D), FF ** -0.5, 0.109375, ((0, 2),)),
        "outer_bias": noise(seeds[20], (D,), 0.3, 1.5),
        "norm2_gain": jnp.clip(1.0 + 0.1 * jax.random.normal(seeds[21], (D,), jnp.float32), 0.5, 1.5).astype(jnp.bfloat16),
        "norm2_shift": noise(seeds[22], (D,), 0.3, 1.5),
        "cotangent": heavy_noise(seeds[23], (PAGES, SEQ, D), 1.0, 6.0, ((0, 16),), (0, 2, 16, 2.0)),
    }


eps_norm = 1e-05
neg_fill = -1000000000.0
highest = lax.Precision.HIGHEST

@jax.custom_vjp
def low(v):
    return lax.optimization_barrier(v.astype(jnp.bfloat16)).astype(jnp.float32)

@jax.custom_vjp
def low_back(v):
    return v

def low_keep(v):
    return (low(v), None)

def low_pass(kept, grad):
    return (grad,)

def back_keep(v):
    return (v, None)

def back_low(kept, grad):
    return (low(grad),)
low.defvjp(low_keep, low_pass)
low_back.defvjp(back_keep, back_low)

def matmul(left_side, right_side):
    return jnp.dot(left_side, right_side, precision=highest, preferred_element_type=jnp.float32)

def layer_norm(values, gain_vec, shift_vec):
    centre = values - lax.optimization_barrier(jnp.mean(values, axis=-1, keepdims=True))
    spread = lax.optimization_barrier(jnp.mean(centre * centre, axis=-1, keepdims=True))
    return centre * lax.rsqrt(spread + eps_norm) * gain_vec + shift_vec

def exact_gelu(values):
    return jax.nn.gelu(values, approximate=False)

def patch_matrices(patch_count, patches):
    grid_side = jnp.where(patch_count == GRID_LARGE * GRID_LARGE, GRID_LARGE, GRID_SMALL).astype(jnp.int32)
    patch_index = jnp.arange(patches, dtype=jnp.int32)
    grid_row = patch_index // grid_side
    grid_col = patch_index % grid_side
    tap_list = []
    for step_row in (-1, 0, 1):
        for step_col in (-1, 0, 1):
            inside = (grid_row + step_row >= 0) & (grid_row + step_row < grid_side) & (grid_col + step_col >= 0) & (grid_col + step_col < grid_side) & (patch_index < patch_count)
            target = patch_index + step_row * grid_side + step_col
            selected = (patch_index[None, :] == target[:, None]) & inside[:, None]
            tap_list.append(selected.astype(jnp.float32))
    return jnp.concatenate(tap_list, axis=0)

def position_encoding(page_rows, text_w, patch_w, patch_mats, text_len):
    text_rows = page_rows[:text_len]
    padded = jnp.pad(text_rows, ((3, 3), (0, 0)))
    summed = jnp.zeros_like(text_rows)
    for dilate in range(3):
        for tap_index in range(3):
            offset = (tap_index - 1) * (dilate + 1)
            summed = summed + text_w[dilate, tap_index] * padded[3 + offset:3 + offset + text_len]
    patch_rows = page_rows[text_len:]
    shifted = matmul(patch_mats, patch_rows).reshape(9, patch_rows.shape[0], patch_rows.shape[1])
    patch_part = lax.optimization_barrier(jnp.sum(patch_w[:, None, :] * shifted, axis=0))
    return jnp.concatenate([summed, patch_part], axis=0)

def plane_bucket(coordinate):
    half_plane = BINS_2D // 2
    differ = jnp.floor_divide(coordinate[None, :] - coordinate[:, None], BIN_WIDTH)
    return (jnp.clip(differ, -half_plane, half_plane - 1) + half_plane).astype(jnp.int32)

def bias_buckets(boxes_page, seq_len):
    position = jnp.arange(seq_len, dtype=jnp.int32)
    half_line = BINS_1D // 2
    line_bucket = (jnp.clip(position[None, :] - position[:, None], -half_line, half_line - 1) + half_line).astype(jnp.int32)
    return (line_bucket, plane_bucket(boxes_page[0]), plane_bucket(boxes_page[1]))

def score_bias(buckets, tables):
    summed = 0.0
    for bucket, bias_table in zip(buckets, tables):
        summed = summed + jnp.take(jnp.transpose(bias_table), bucket, axis=1)
    return summed

def page_forward(params, page_rows, patch_count, boxes_page):
    text_w, patch_w, query_w, query_b, key_w, value_w, value_b, out_w, out_b, line_t, width_t, height_t, gain_one, shift_one, inner_w, inner_b, outer_w, outer_b, gain_two, shift_two = params
    seq_len, model_width = page_rows.shape
    head_dim = model_width // HEADS
    scale = head_dim ** (-0.5)
    patch_mats = patch_matrices(patch_count, seq_len - TEXT)
    live_rows = jnp.arange(seq_len) < TEXT + patch_count
    encoded = page_rows + position_encoding(page_rows, text_w, patch_w, patch_mats, TEXT)
    encoded_low = low(encoded)
    queries = low(low_back(matmul(encoded_low, query_w)) + query_b).reshape(seq_len, HEADS, head_dim)
    key_rows = low(low_back(matmul(encoded_low, key_w))).reshape(seq_len, HEADS, head_dim)
    values = low(low_back(matmul(encoded_low, value_w)) + value_b).reshape(seq_len, HEADS, head_dim)
    raw_scores = jnp.einsum('qhd,khd->hqk', queries, key_rows, precision=highest)
    scores = low_back(raw_scores * scale) + score_bias(bias_buckets(boxes_page, seq_len), (line_t, width_t, height_t))
    scores = jnp.where(live_rows[None, None, :], scores, neg_fill)
    row_max = lax.optimization_barrier(jnp.max(scores, axis=-1, keepdims=True))
    exp_scores = jnp.exp(scores - row_max)
    attn_probs = low(exp_scores / lax.optimization_barrier(jnp.sum(exp_scores, axis=-1, keepdims=True)))
    mixture = jnp.einsum('hqk,khd->qhd', attn_probs, values, precision=highest).reshape(seq_len, model_width)
    mixture = low_back(low(mixture))
    attended = low_back(matmul(mixture, out_w)) + out_b
    hidden = layer_norm(encoded + attended, gain_one, shift_one)
    inner_pre = low_back(matmul(low(hidden), inner_w)) + inner_b
    activated = low(exact_gelu(inner_pre))
    outer_out = low_back(matmul(activated, outer_w)) + outer_b
    return layer_norm(hidden + outer_out, gain_two, shift_two) * live_rows[:, None].astype(jnp.float32)

def reference(page_tokens, patch_counts, token_boxes, text_weight, patch_weight, query_weight, query_bias, key_weight, value_weight, value_bias, out_weight, out_bias, line_table, width_table, height_table, norm1_gain, norm1_shift, inner_weight, inner_bias, outer_weight, outer_bias, norm2_gain, norm2_shift, cotangent):
    weights = (text_weight, patch_weight, query_weight, query_bias, key_weight, value_weight, value_bias, out_weight, out_bias, line_table, width_table, height_table, norm1_gain, norm1_shift, inner_weight, inner_bias, outer_weight, outer_bias, norm2_gain, norm2_shift)
    floats = tuple((argument.astype(jnp.float32) for argument in weights))

    def forward(inputs, params):

        def one_page(packed):
            page_rows, patch_count, boxes_page = packed
            return page_forward(params, page_rows, patch_count, boxes_page)
        return lax.map(jax.checkpoint(one_page), (inputs, patch_counts, token_boxes))
    result, pullback = jax.vjp(forward, page_tokens.astype(jnp.float32), floats)
    input_grad, grads = pullback(cotangent.astype(jnp.float32))
    return (result.astype(jnp.bfloat16), input_grad.astype(jnp.bfloat16), grads[0], grads[1], grads[2], grads[3], grads[4], grads[5], grads[6], grads[7], grads[8], grads[9], grads[10], grads[11], grads[12], grads[13], grads[14], grads[15], grads[16], grads[17], grads[18], grads[19])
```

```python
import functools

import jax
import jax.numpy as jnp
from jax import lax
from jax.experimental import pallas as pl
from jax.experimental.pallas import tpu as pltpu
from jax.sharding import PartitionSpec as P

HEADS = 12
TEXT = 512
GRID_SMALL = 7
GRID_LARGE = 14
BINS_1D = 32
BINS_2D = 64
BIN_WIDTH = 8

F32 = jnp.float32
BF16 = jnp.bfloat16
EPS = 1e-05
NEG = -1000000000.0
HIGHEST = lax.Precision.HIGHEST

D = 768
SEQ = 708
ROWS = 720
KEYS = 768
CHUNKS = ((0, 256), (256, 256), (512, 208))
ORDER = (2, 0, 1)
SUB = 128
PAIR = 128
HL = 6
DL = 384
FL = 1536
MARGIN = 16
MIB = 1024 * 1024


def vmem():
    return pl.BlockSpec(memory_space=pltpu.VMEM)


def anywhere():
    return pl.BlockSpec(memory_space=pl.ANY)


def hbm():
    return pl.BlockSpec(memory_space=pltpu.HBM)


def smem():
    return pl.BlockSpec(memory_space=pltpu.SMEM)


def params(mib):
    return pltpu.CompilerParams(vmem_limit_bytes=mib * MIB)


def sds(shape, dtype):
    return jax.ShapeDtypeStruct(shape, dtype)


TOKEN = jax.ShapeDtypeStruct((8, 128), jnp.float32)


class Order:
    def __init__(self):
        self.token = None

    def __call__(
        self, kernel, operands, in_specs, out_shape, out_specs, mib=10, us=1, after=(), **more
    ):
        operands, in_specs = list(operands), list(in_specs)
        count = len(operands)
        operands += list(after)
        in_specs += [anywhere()] * len(after)
        if self.token is not None:
            operands.append(self.token)
            grid = "grid" in more
            in_specs.append(pl.BlockSpec(TOKEN.shape, lambda *i: (0, 0)) if grid else vmem())
        has_token = self.token is not None
        outs = len(out_shape)

        def body(*refs):
            rest = list(refs)
            del rest[count : count + len(after) + has_token]
            at = count + outs
            rest[at][...] = jnp.zeros(TOKEN.shape, F32)
            del rest[at]
            kernel(*rest)

        token_spec = pl.BlockSpec(TOKEN.shape, lambda *i: (0, 0)) if "grid" in more else vmem()
        got = pl.pallas_call(
            body,
            out_shape=tuple(out_shape) + (TOKEN,),
            in_specs=in_specs,
            out_specs=tuple(out_specs) + (token_spec,),
            compiler_params=params(mib),
            cost_estimate=cost(us),
            **more,
        )(*operands)
        self.token = got[-1]
        return got[:-1]


def dot(a, b):
    return lax.dot_general(a, b, (((1,), (0,)), ((), ())), preferred_element_type=F32)


def dot_nt(a, b):
    return lax.dot_general(a, b, (((1,), (1,)), ((), ())), preferred_element_type=F32)


def dot_tn(a, b):
    return lax.dot_general(a, b, (((0,), (0,)), ((), ())), preferred_element_type=F32)


def cost(us):
    return pl.CostEstimate(flops=int(us * 1.0e6), bytes_accessed=int(us * 1.0e3), transcendentals=0)


def iota(shape, dim):
    return lax.broadcasted_iota(jnp.int32, shape, dim)


def first_lanes():
    return iota((1, PAIR), 1) < 64


def start_all(pairs, sems, first=0):
    copies = [
        pltpu.make_async_copy(src, dst, sems.at[first + i]) for i, (src, dst) in enumerate(pairs)
    ]
    for copy in copies:
        copy.start()
    return copies


def tables_kernel(
    where_ref, tab_ref, boxes_hbm, wo_hbm,
    z_ref, m_ref, o_ref, u_ref, r_ref, mine_ref, o_far, ur_far, r_far,
    box_scr, boxes_ref, wo_ref, ur_ref, sems,
):
    half = DL // 2
    rows = pl.ds(pl.multiple_of(where_ref[1] * half, half), half)
    copies = start_all(
        (
            (boxes_hbm, boxes_ref),
            (wo_hbm.at[rows, :], wo_ref),
        ),
        sems,
    )
    for copy in copies:
        copy.wait()
    mine_ref[...] = wo_ref[...].astype(F32)
    lane = iota((BINS_1D, 768), 1)
    bucket = jnp.where(lane < 640, jnp.clip(lane - 256, -16, 15) + 16, 0)
    line_pick = (bucket == iota((BINS_1D, 768), 0)).astype(BF16)
    line_base = dot(tab_ref[:, 0:BINS_1D], line_pick)
    lane = iota((BINS_2D, PAIR), 1)
    bucket = jnp.clip(lane - 64, -32, 31) + 32
    plane_pick = (bucket == iota((BINS_2D, PAIR), 0)).astype(BF16)
    bases = [
        dot(tab_ref[:, BINS_1D + 64 * plane : BINS_1D + 64 * plane + 64], plane_pick)
        for plane in range(2)
    ]
    first = first_lanes()
    zeros = jnp.zeros((64, PAIR), BF16)
    for h in range(HL):
        spread = jnp.broadcast_to(line_base[h : h + 1, :], (SUB, 768))
        rolled = pltpu.roll(spread, 0, 1, stride=1, stride_axis=0)
        z_ref[h] = rolled[:, :640]
        for plane in range(2):
            spread = jnp.broadcast_to(bases[plane][h : h + 1, :], (64, PAIR))
            for below in range(2):
                one = pltpu.roll(spread, 64 + below, 1, stride=1, stride_axis=0)
                both = jnp.where(first, one, pltpu.roll(one, 64, 1)).astype(BF16)
                start = h * 512 + plane * 256 + below * 128
                m_ref[plane * 64 : plane * 64 + 64, start : start + 128] = both
                m_ref[64 - plane * 64 : 128 - plane * 64, start : start + 128] = zeros
    box_scr[...] = jnp.full((8, KEYS), -1, jnp.int32)
    box_scr[0:2, 0:SEQ] = boxes_ref[...]
    row = iota((512, KEYS), 0)
    value = 8 * (row % 64) + row // 64
    for plane in range(2):
        o_ref[plane * 512 : plane * 512 + 512, :] = (
            value == box_scr[plane : plane + 1, :]
        ).astype(F32).astype(BF16)
    turned = jnp.transpose(box_scr[...].astype(F32))[0:ROWS, :].astype(jnp.int32)
    left = jnp.broadcast_to(turned[:, 0:1], (ROWS, PAIR))
    right = jnp.broadcast_to(turned[:, 1:2], (ROWS, PAIR))
    lane = iota((ROWS, PAIR), 1)
    both = jnp.where(lane < 64, left, right)
    r_ref[0] = left & 7
    r_ref[1] = right & 7
    upper = lax.shift_right_logical(both, 3)
    inner = lane & 63
    u_ref[...] = (upper == inner).astype(F32).astype(BF16)
    ur_ref[...] = (63 - upper == inner).astype(F32).astype(BF16)
    for copy in start_all(((o_ref, o_far), (ur_ref, ur_far), (r_ref, r_far)), sems):
        copy.wait()


def make_tables(order, where, tab, boxes, wo):
    return order(
        tables_kernel,
        (where, tab, boxes, wo),
        [smem(), vmem()] + [hbm()] * 2,
        (
            sds((HL, SUB, 640), F32),
            sds((128, HL * 512), BF16),
            sds((1024, KEYS), BF16),
            sds((ROWS, PAIR), BF16),
            sds((2, ROWS, PAIR), jnp.int32),
            sds((DL // 2, D), F32),
            sds((1024, KEYS), BF16),
            sds((ROWS, PAIR), BF16),
            sds((2, ROWS, PAIR), jnp.int32),
        ),
        [vmem()] * 6 + [hbm()] * 3,
        us=20000,
        scratch_shapes=[
            pltpu.VMEM((8, KEYS), jnp.int32),
            pltpu.VMEM(boxes.shape, jnp.int32),
            pltpu.VMEM((DL // 2, D), BF16),
            pltpu.VMEM((ROWS, PAIR), BF16),
            pltpu.SemaphoreType.DMA((5,)),
        ],
        name="bias_tables",
    )


def copy_kernel(src, dst, scr, sems):
    for pair in ((src, scr), (scr, dst)):
        copy = pltpu.make_async_copy(*pair, sems.at[0])
        copy.start()
        copy.wait()


def pass_on(order, x):
    return order(
        copy_kernel,
        (x,),
        [anywhere()],
        (sds(x.shape, x.dtype),),
        [anywhere()],
        scratch_shapes=[pltpu.VMEM(x.shape, x.dtype), pltpu.SemaphoreType.DMA((1,))],
        name="pass_on",
    )[0]


def text_taps(text_ref, cols):
    taps = {}
    for dilate in range(3):
        for tap in range(3):
            shift = (tap - 1) * (dilate + 1)
            row = text_ref[dilate, tap : tap + 1, cols].astype(F32)
            taps[shift] = row if shift not in taps else taps[shift] + row
    return taps


def text_conv_block(win, taps, sign):
    total = win[8:40] * (taps[0] + 1.0)
    for shift in (-3, -2, -1, 1, 2, 3):
        start = 8 + sign * shift
        total = total + win[start : start + 32] * taps[shift]
    return total


def grid_masks(side):
    place = iota((208, PAIR), 0)
    row = jnp.floor((place.astype(F32) + 0.5) * (1.0 / side)).astype(jnp.int32)
    col = place - row * side
    return (place < side * side, col >= 1, col <= side - 2)


def patch_conv_cols(win, patch_ref, cols, side, sign):
    live, has_left, has_right = grid_masks(side)
    total = None
    for ds in (-1, 0, 1):
        part = None
        for dr in (-1, 0, 1):
            tap = 3 * (dr + 1) + ds + 1
            start = MARGIN + sign * (dr * side + ds)
            term = win[start : start + 208] * patch_ref[tap : tap + 1, cols].astype(F32)
            part = term if part is None else part + term
        if ds * sign == -1:
            part = jnp.where(has_left, part, 0.0)
        if ds * sign == 1:
            part = jnp.where(has_right, part, 0.0)
        total = part if total is None else total + part
    return jnp.where(live, total, 0.0)


def fill_patches(patch_scr, source, count):
    zero = jnp.zeros((MARGIN, D), F32)
    patch_scr[0:MARGIN, :] = zero
    patch_scr[MARGIN + 208 : MARGIN + 208 + MARGIN, :] = zero
    live = iota((208, PAIR), 0) < count
    for c in range(D // PAIR):
        cols = slice(c * PAIR, c * PAIR + PAIR)
        patch_scr[MARGIN : MARGIN + 208, cols] = jnp.where(live, source(cols), 0.0)


def load_page(x_ref, count, text_scr, patch_scr, raw_scr):
    zero8 = jnp.zeros((8, D), F32)
    text_scr[0:8, :] = zero8
    text_scr[520:528, :] = zero8
    for b in range(TEXT // 64):
        text_scr[8 + 64 * b : 72 + 64 * b, :] = x_ref[64 * b : 64 * b + 64, :].astype(F32)
    raw_scr[...] = jnp.zeros((208, D), F32)
    raw_scr[0 : SEQ - TEXT, :] = x_ref[TEXT:SEQ, :].astype(F32)
    fill_patches(patch_scr, lambda cols: raw_scr[:, cols], count)


PAGE_SCRATCH = [
    pltpu.VMEM((528, D), F32),
    pltpu.VMEM((208 + 2 * MARGIN, D), F32),
    pltpu.VMEM((208, D), F32),
]


def by_grid(count, patches):
    large = count == GRID_LARGE * GRID_LARGE

    @pl.when(large)
    def _():
        patches(GRID_LARGE)

    @pl.when(jnp.logical_not(large))
    def _():
        patches(GRID_SMALL)


def encode_kernel(
    count_ref, x_hbm, text_ref, patch_ref, bias_ref, wq_hbm, wk_hbm, wv_hbm,
    q0, q1, q2, k_ref, v_ref,
    e0_far, e1_far, e2_far, l0_far, l1_far, l2_far, q0_far, q1_far, q2_far, k_far, v_far,
    text_scr, patch_scr, raw_scr, x_ref, wq_ref, wk_ref, wv_ref,
    e0, e1, e2, l0, l1, l2, sems,
):
    copies = start_all(
        ((x_hbm, x_ref), (wq_hbm, wq_ref), (wk_hbm, wk_ref), (wv_hbm, wv_ref)), sems
    )
    count = count_ref[0]
    copies[0].wait()
    load_page(x_ref, count, text_scr, patch_scr, raw_scr)

    for c in range(2):
        cols = slice(c * 384, c * 384 + 384)
        taps = text_taps(text_ref, cols)

        def one(b, carry, cols=cols, taps=taps, out=None, first=0):
            base = pl.multiple_of(b * 32, 32)
            win = text_scr[pl.ds(first + base, 48), cols]
            out[pl.ds(base, 32), cols] = text_conv_block(win, taps, 1)
            return carry

        lax.fori_loop(0, 8, functools.partial(one, out=e0, first=0), 0)
        lax.fori_loop(0, 8, functools.partial(one, out=e1, first=256), 0)

    def patches(side):
        for c in range(D // PAIR):
            cols = slice(c * PAIR, c * PAIR + PAIR)
            e2[:, cols] = raw_scr[:, cols] + patch_conv_cols(
                patch_scr[:, cols], patch_ref, cols, side, 1
            )

    by_grid(count, patches)
    far = start_all(((e0, e0_far), (e1, e1_far), (e2, e2_far)), sems, 4)
    for copy in copies[1:]:
        copy.wait()
    for i, ((start, rows), e, low, low_far, q, q_far) in enumerate(
        zip(
            CHUNKS, (e0, e1, e2), (l0, l1, l2), (l0_far, l1_far, l2_far), (q0, q1, q2),
            (q0_far, q1_far, q2_far),
        )
    ):
        enc = e[...].astype(BF16)
        low[...] = enc
        query = (dot(enc, wq_ref[...]) + bias_ref[0:1, :]).astype(BF16)
        q[...] = query * jnp.asarray(0.125, BF16)
        k_ref[start : start + rows, :] = dot(enc, wk_ref[...]).astype(BF16)
        value = dot(enc, wv_ref[...]) + bias_ref[1:2, :]
        v_ref[start : start + rows, :] = value.astype(BF16)
        far += start_all(((low, low_far), (q, q_far)), sems, 7 + 2 * i)
    k_ref[ROWS:KEYS, :] = jnp.zeros((KEYS - ROWS, DL), BF16)
    v_ref[ROWS:KEYS, :] = jnp.zeros((KEYS - ROWS, DL), BF16)
    far += start_all(((k_ref, k_far), (v_ref, v_far)), sems, 13)
    for copy in far:
        copy.wait()


def encode(order, count, x, text, patch, bias, wq, wk, wv):
    chunk = lambda width, dtype: tuple(sds((rows, width), dtype) for _, rows in CHUNKS)
    scratch = lambda width, dtype: [pltpu.VMEM((rows, width), dtype) for _, rows in CHUNKS]
    keys = (sds((KEYS, DL), BF16), sds((KEYS, DL), BF16))
    out = order(
        encode_kernel,
        (count, x, text, patch, bias, wq, wk, wv),
        [smem(), hbm()] + [vmem()] * 3 + [hbm()] * 3,
        chunk(DL, BF16) + keys + chunk(D, F32) + chunk(D, BF16) + chunk(DL, BF16) + keys,
        [vmem()] * 5 + [hbm()] * 11,
        scratch_shapes=PAGE_SCRATCH
        + [pltpu.VMEM((SEQ, D), BF16)]
        + [pltpu.VMEM((D, DL), BF16)] * 3
        + scratch(D, F32)
        + scratch(D, BF16)
        + [pltpu.SemaphoreType.DMA((15,))],
        mib=18,
        us=8000,
        name="encode_project",
    )
    return out[0:5], out[5:8], out[8:11], out[11:]


def bias_rows(e, r_col, k, rows):
    step = 2 * k + (iota((rows, PAIR), 1) >= 64).astype(jnp.int32)
    return jnp.where(step >= r_col, e[0], e[1]).astype(BF16)


def line_rows(z_ref, h, sub, rows):
    groups = [min(max(g - sub + 2, 0), 4) for g in range(KEYS // SUB)]
    return jnp.concatenate([z_ref[h, 0:rows, g * 128 : g * 128 + 128] for g in groups], axis=1)


def attend_kernel(
    start, rows, count_ref, q_ref, k_ref, v_ref, u_ref, r_ref, m_ref, o_ref, z_ref,
    p_hbm, mix_ref, low_far, p_scr, low_scr, sems,
):
    live = iota((1, KEYS), 1) < TEXT + count_ref[0]
    first = first_lanes()
    r_w = r_ref[0, start : start + rows, :]
    r_h = r_ref[1, start : start + rows, :]
    copies = []
    u = u_ref[start : start + rows, :]
    for pair in range(HL // 2):
        cols = slice(pair * PAIR, pair * PAIR + PAIR)
        q = q_ref[:, cols]
        k = k_ref[:, cols]
        v = v_ref[:, cols]
        mixed = []
        for half in range(2):
            h = 2 * pair + half
            mine = first if half == 0 else jnp.logical_not(first)
            qm = jnp.where(mine, q, jnp.zeros_like(q))
            e = dot(u, m_ref[:, h * 512 : h * 512 + 512])
            parts = [bias_rows((e[:, 0:128], e[:, 128:256]), r_w, kk, rows) for kk in range(4)]
            parts += [bias_rows((e[:, 256:384], e[:, 384:512]), r_h, kk, rows) for kk in range(4)]
            picked = jnp.concatenate(parts, axis=1)
            s = dot(picked, o_ref[...]) + dot_nt(qm, k)
            pieces = []
            for at in range(0, rows, SUB):
                size = min(SUB, rows - at)
                pieces.append(line_rows(z_ref, h, (start + at) // SUB, size))
            s = s + jnp.concatenate(pieces, axis=0)
            s = jnp.where(live, s, NEG)
            top = jnp.max(s, axis=1, keepdims=True)
            ex = jnp.exp(s - top)
            total = jnp.sum(ex, axis=1, keepdims=True)
            prob = (ex * (1.0 / total)).astype(BF16)
            p_scr[h] = prob
            copies.append(pltpu.make_async_copy(p_scr.at[h], p_hbm.at[h], sems.at[h]))
            copies[-1].start()
            mixed.append(dot(prob, v))
        low = jnp.where(first, mixed[0], mixed[1]).astype(BF16)
        low_scr[:, cols] = low
        mix_ref[:, cols] = low.astype(F32)
    copies.append(pltpu.make_async_copy(low_scr, low_far, sems.at[HL]))
    copies[-1].start()
    for copy in copies:
        copy.wait()


def attend(order, c, count, q, k, v, u, r, m, o, z):
    start, rows = CHUNKS[c]
    return order(
        functools.partial(attend_kernel, start, rows),
        (count, q, k, v, u, r, m, o, z),
        [smem()] + [vmem()] * 8,
        (sds((HL, rows, KEYS), BF16), sds((rows, DL), F32), sds((rows, DL), BF16)),
        (hbm(), vmem(), hbm()),
        scratch_shapes=[
            pltpu.VMEM((HL, rows, KEYS), BF16),
            pltpu.VMEM((rows, DL), BF16),
            pltpu.SemaphoreType.DMA((HL + 1,)),
        ],
        mib=14,
        name=f"attend_{c}",
    )


def feed_kernel(
    where_ref, own_ref, other_ref, enc_hbm, vec_ref, wo_ref, wo_a_ref, wo_b_ref, wi_ref, bi_ref,
    w2_ref, xhat_ref, rstd_ref, hlow_ref, act_ref, slope_ref, part_ref, enc_ref, sems,
):
    (copy,) = start_all(((enc_hbm, enc_ref),), sems)
    half = where_ref[0]
    core = where_ref[1]
    own = dot(own_ref[...].astype(BF16), wo_ref[...])
    other = other_ref[...].astype(BF16)
    low = jnp.where(core == 0, wo_a_ref[...], wo_b_ref[...]).astype(BF16)
    high = jnp.where(core == 0, wo_b_ref[...], wo_a_ref[...]).astype(BF16)
    other = dot(other, jnp.concatenate([low, high], axis=0))
    attended = jnp.where(half == 0, own, other) + jnp.where(half == 0, other, own)
    copy.wait()
    v = enc_ref[...] + (attended + vec_ref[0:1, :])
    centre = v - jnp.mean(v, axis=1, keepdims=True)
    rstd = lax.rsqrt(jnp.mean(centre * centre, axis=1, keepdims=True) + EPS)
    xhat = centre * rstd
    xhat_ref[...] = xhat
    rstd_ref[...] = jnp.broadcast_to(rstd, rstd_ref.shape)
    hlow = (xhat * vec_ref[1:2, :] + vec_ref[2:3, :]).astype(BF16)
    hlow_ref[...] = hlow
    total = None
    for n in range(FL // 512):
        cols = slice(n * 512, n * 512 + 512)
        pre = dot(hlow, wi_ref[:, cols]) + bi_ref[0:1, cols]
        gate = 0.5 + 0.5 * lax.erf(pre * 0.7071067811865476)
        slope_ref[:, cols] = gate + pre * (0.3989422804014327 * jnp.exp(-0.5 * pre * pre))
        act = (pre * gate).astype(BF16)
        act_ref[:, cols] = act
        term = dot(act, w2_ref[cols, :])
        total = term if total is None else total + term
    part_ref[...] = total


def feed(order, c, where, own, other, enc, vec, wo, wo_a, wo_b, wi, bi, w2):
    _, rows = CHUNKS[c]
    return order(
        feed_kernel,
        (where, own, other, enc, vec, wo, wo_a, wo_b, wi, bi, w2),
        [smem()] + [vmem()] * 2 + [hbm()] + [vmem()] * 7,
        (
            sds((rows, D), F32),
            sds((rows, 128), F32),
            sds((rows, D), BF16),
            sds((rows, FL), BF16),
            sds((rows, FL), F32),
            sds((rows, D), F32),
        ),
        [vmem()] * 6,
        scratch_shapes=[pltpu.VMEM((rows, D), F32), pltpu.SemaphoreType.DMA((1,))],
        name=f"feed_{c}",
    )


def norm_back(dy, xhat, rstd, gain):
    dxh = dy * gain
    return rstd * (
        dxh
        - jnp.mean(dxh, axis=1, keepdims=True)
        - xhat * jnp.mean(dxh * xhat, axis=1, keepdims=True)
    )


def col_sum(x):
    return jnp.sum(x, axis=0, keepdims=True)


def feed_back_kernel(
    start, rows, first, count_ref, own_ref, other_ref, xhat1_ref, cot_ref, vec_ref, w2_ref,
    slope_ref, wi_ref, *rest,
):
    if not first:
        rest = rest[1:]
    out_ref, dres_ref, g2_ref, g1_ref, part_ref, sums_ref = rest
    place = start + iota((rows, 1), 0)
    live = place < TEXT + count_ref[0]
    hidden = xhat1_ref[...] * vec_ref[1:2, :] + vec_ref[2:3, :]
    v = hidden + ((own_ref[...] + other_ref[...]) + vec_ref[3:4, :])
    centre = v - jnp.mean(v, axis=1, keepdims=True)
    rstd = lax.rsqrt(jnp.mean(centre * centre, axis=1, keepdims=True) + EPS)
    xhat = centre * rstd
    y = xhat * vec_ref[4:5, :] + vec_ref[5:6, :]
    out_ref[0:rows, :] = jnp.where(live, y, 0.0).astype(BF16)
    dy = jnp.where(live, cot_ref[0:rows, :].astype(F32), 0.0)
    sums_ref[...] = jnp.zeros(sums_ref.shape, F32)
    sums_ref[2:3, 0:D] = col_sum(dy * xhat)
    sums_ref[3:4, 0:D] = col_sum(dy)
    dres = norm_back(dy, xhat, rstd, vec_ref[4:5, :])
    dres_ref[...] = dres
    sums_ref[1:2, 0:D] = col_sum(dres)
    g2 = dres.astype(BF16)
    g2_ref[...] = g2
    total = None
    for n in range(FL // 512):
        cols = slice(n * 512, n * 512 + 512)
        d_inner = dot_nt(g2, w2_ref[cols, :]) * slope_ref[:, cols]
        sums_ref[0:1, cols] = col_sum(d_inner)
        g1 = d_inner.astype(BF16)
        g1_ref[:, cols] = g1
        term = dot_nt(g1, wi_ref[:, cols])
        total = term if total is None else total + term
    part_ref[...] = total


def feed_back(order, c, count, own, other, xhat1, cot, vec, w2, slope, wi, out_so_far):
    start, rows = CHUNKS[c]
    block = pl.BlockSpec((256, D), lambda i: (start // 256, 0))
    whole = lambda a: pl.BlockSpec(a.shape, lambda i: (0, 0))
    shapes = (
        sds((SEQ, D), BF16),
        sds((rows, D), F32),
        sds((rows, D), BF16),
        sds((rows, FL), BF16),
        sds((rows, D), F32),
        sds((8, FL), F32),
    )
    operands = [count, own, other, xhat1, cot, vec, w2, slope, wi]
    specs = [smem()] + [vmem()] * 3 + [block] + [vmem()] * 4
    aliases = {}
    if out_so_far is not None:
        operands.append(out_so_far)
        specs.append(anywhere())
        aliases = {9: 0}
    return order(
        functools.partial(feed_back_kernel, start, rows, out_so_far is None),
        operands,
        specs,
        shapes,
        [block] + [vmem()] * 5,
        grid=(1,),
        input_output_aliases=aliases,
        us=15000 if c == ORDER[0] else 1,
        name=f"feed_back_{c}",
    )


def store_slabs(slab, core, grad, keep_ref, send_ref):
    for i in range(D // (2 * slab)):
        even = grad[2 * i * slab : (2 * i + 1) * slab]
        odd = grad[(2 * i + 1) * slab : (2 * i + 2) * slab]
        keep_ref[i * slab : (i + 1) * slab, :] = jnp.where(core == 0, even, odd)
        send_ref[i * slab : (i + 1) * slab, :] = jnp.where(core == 0, odd, even)


def tn_sum(lefts, rights):
    total = None
    for left, right in zip(lefts, rights):
        term = dot_tn(left[...], right[...].astype(BF16))
        total = term if total is None else total + term
    return total


def put_grads(slab, where_ref, grad, outs):
    if slab is None:
        outs[0][...] = grad
    else:
        store_slabs(slab, where_ref[1], grad, *outs)


def chunk_grads_kernel(slab, has_total, where_ref, left_ref, right_ref, *refs):
    grad = dot_tn(left_ref[...], right_ref[...])
    if has_total:
        grad = refs[0][...] + grad
    put_grads(slab, where_ref, grad, refs[has_total:])


def chunk_grads(order, slab, where, left, right, total, last, name):
    width = right.shape[1]
    block = 512
    piece = lambda rows: pl.BlockSpec((rows, block), lambda i: (0, i))
    whole = pl.BlockSpec(left.shape, lambda i: (0, 0))
    apart = last and slab is not None
    rows, count = (D // 2, 2) if apart else (D, 1)
    operands, specs, aliases = [where, left, right], [smem(), whole, piece(right.shape[0])], {}
    if total is not None:
        operands.append(total)
        specs.append(piece(D))
        if not apart:
            aliases = {3: 0}
    return order(
        functools.partial(chunk_grads_kernel, slab if apart else None, total is not None),
        operands,
        specs,
        (sds((rows, width), F32),) * count,
        [piece(rows)] * count,
        grid=(width // block,),
        input_output_aliases=aliases,
        mib=16,
        name=name,
    )


def attention_grads_kernel(slab, where_ref, *refs):
    low, dq, (dk_ref, dv_ref), g0, mix = refs[0:3], refs[3:6], refs[6:8], refs[8:11], refs[11:14]
    outs = refs[14:]
    half = len(outs) // 2
    step = pl.program_id(0)
    chunks = lambda ref: [ref.at[start : start + rows] for start, rows in CHUNKS]
    todo = (
        (low, dq, outs[:half]),
        (low, chunks(dk_ref), outs[:half]),
        (low, chunks(dv_ref), outs[half:]),
        (g0, mix, outs[half:]),
    )
    for i, (lefts, rights, out) in enumerate(todo):

        @pl.when(step == i)
        def _(lefts=lefts, rights=rights, out=out):
            put_grads(slab, where_ref, tn_sum(lefts, rights), out)


def attention_grads(order, slab, where, enc_low, dq, dk, dv, g0, mix):
    operands = [*enc_low, *dq, dk, dv, *g0, *mix]
    rows, count = (D, 1) if slab is None else (D // 2, 2)
    return order(
        functools.partial(attention_grads_kernel, slab),
        (where, *operands),
        [smem()] + [pl.BlockSpec(a.shape, lambda i: (0, 0)) for a in operands],
        (sds((rows, D), F32),) * (2 * count),
        [pl.BlockSpec((rows, DL), lambda i: (0, jnp.minimum(i, 1)))] * count
        + [pl.BlockSpec((rows, DL), lambda i: (0, jnp.maximum(i - 2, 0)))] * count,
        grid=(4,),
        mib=24,
        name="attention_grads",
    )


SMALL = 40


def halve_kernel(slabs, high, where_bit, extra, where_ref, *refs):
    small_ref = None
    if extra == "first":
        small_ref, *refs = refs
    *pairs, own_ref, out_ref = refs
    mine = where_ref[where_bit]
    total = pairs[0].shape[0] - (SMALL if extra == "more" else 0)
    run = high * (total // slabs)
    at = 0
    for a_ref, b_ref in zip(pairs[0::2], pairs[1::2]):
        cols = slice(at, at + a_ref.shape[1])
        at += a_ref.shape[1]
        for i in range(slabs // (2 * high)):
            for ref, which in ((own_ref, mine), (out_ref, 1 - mine)):
                rows = pl.ds(pl.multiple_of((2 * i + which) * run, 8), run)
                ref[i * run : (i + 1) * run, cols] = a_ref[rows, :] + b_ref[rows, :]
    if extra is not None:
        small = small_ref[...] if extra == "first" else pairs[0][total:] + pairs[1][total:]
        own_ref[total // 2 :, :] = small
        out_ref[total // 2 :, :] = small


def halve(order, where, pairs, slabs, high, where_bit, first, width, name, small=None, extra=None):
    rows = pairs[0][0].shape[0]
    out_rows = rows // 2
    operands, specs = [where], [smem()]
    if extra == "first":
        out_rows = rows // 2 + SMALL
        operands.append(small)
        specs.append(vmem())
    if extra == "more":
        out_rows = (rows - SMALL) // 2 + SMALL
    if len(pairs) == 1 and extra is None:
        block = 512 if width % 512 == 0 and first % 512 == 0 else 384
        at = first // block
        specs += [pl.BlockSpec((rows, block), lambda i: (0, at + i))] * 2
        grid = (width // block,)
    else:
        block = width
        specs += [pl.BlockSpec(a.shape, lambda i: (0, 0)) for pair in pairs for a in pair]
        grid = (1,)
    half = pl.BlockSpec((out_rows, block), lambda i: (0, i))
    return order(
        functools.partial(halve_kernel, slabs, high, where_bit, extra),
        operands + [a for pair in pairs for a in pair],
        specs,
        (sds((out_rows, width), F32),) * 2,
        [half, half],
        grid=grid,
        mib=12,
        name=name,
    )


def norm_back_kernel(
    dres2_ref, own_ref, other_ref, xhat_ref, rstd_ref, vec_ref, wo_ref,
    dres1_far, g0_ref, dmix_ref, sums_ref, dres1_ref, sems,
):
    dhid = dres2_ref[...] + (own_ref[...] + other_ref[...])
    xhat = xhat_ref[...]
    sums_ref[...] = jnp.zeros(sums_ref.shape, F32)
    sums_ref[1:2, :] = col_sum(dhid * xhat)
    sums_ref[2:3, :] = col_sum(dhid)
    dres1 = norm_back(dhid, xhat, rstd_ref[:, 0:1], vec_ref[1:2, :])
    dres1_ref[...] = dres1
    (copy,) = start_all(((dres1_ref, dres1_far),), sems)
    sums_ref[0:1, :] = col_sum(dres1)
    g0 = dres1.astype(BF16)
    g0_ref[...] = g0
    dmix_ref[...] = dot_nt(g0, wo_ref[...]).astype(BF16)
    copy.wait()


def norm_one_back(order, c, dres2, own, other, xhat, rstd, vec, wo):
    _, rows = CHUNKS[c]
    return order(
        norm_back_kernel,
        (dres2, own, other, xhat, rstd, vec, wo),
        [vmem()] * 7,
        (sds((rows, D), F32), sds((rows, D), BF16), sds((rows, DL), BF16), sds((8, D), F32)),
        [hbm()] + [vmem()] * 3,
        scratch_shapes=[pltpu.VMEM((rows, D), F32), pltpu.SemaphoreType.DMA((1,))],
        us=20000 if c == ORDER[0] else 1,
        name=f"norm_back_{c}",
    )


def attend_back_kernel(
    start, rows, first, dmix_ref, p_hbm, q_ref, k_ref, v_ref, ur_ref, r_ref, o_ref, *rest,
):
    if not first:
        dk_in, dv_in, dm_in, dz_in = rest[:4]
        rest = rest[4:]
    dq_ref, dk_ref, dv_ref, dm_ref, dz_ref, p_scr, sems = rest
    copies = [pltpu.make_async_copy(p_hbm.at[h], p_scr.at[h], sems.at[h]) for h in range(HL)]
    for copy in copies:
        copy.start()
    if first:
        dz_ref[...] = jnp.zeros(dz_ref.shape, F32)
    else:
        dz_ref[...] = dz_in[...]

    lanes = first_lanes()
    r_w = r_ref[0, start : start + rows, :]
    r_h = r_ref[1, start : start + rows, :]
    upper = (iota((rows, PAIR), 1) >= 64).astype(jnp.int32)
    ur = ur_ref[start : start + rows, :]
    for pair in range(HL // 2):
        cols = slice(pair * PAIR, pair * PAIR + PAIR)
        q = q_ref[:, cols]
        k = k_ref[:, cols]
        v = v_ref[:, cols]
        dmix = dmix_ref[:, cols]
        dq_total = None
        dk_total = None if first else dk_in[:, cols]
        dv_total = None if first else dv_in[:, cols]
        for half in range(2):
            h = 2 * pair + half
            mine = lanes if half == 0 else jnp.logical_not(lanes)
            pick = lambda a: jnp.where(mine, a, jnp.zeros_like(a))
            dmix_m = pick(dmix)
            copies[h].wait()
            prob = p_scr[h]
            dprob = dot_nt(dmix_m, v)
            prob_f = prob.astype(F32)
            both = prob_f * dprob
            ds = both - prob_f * jnp.sum(both, axis=1, keepdims=True)
            low = ds.astype(BF16)
            dq = dot(low, pick(k))
            dk = dot_tn(low, pick(q))
            dv = dot_tn(prob, dmix_m)
            dq_total = dq if dq_total is None else dq_total + dq
            dk_total = dk if dk_total is None else dk_total + dk
            dv_total = dv if dv_total is None else dv_total + dv
            for at in range(0, rows, SUB):
                size = min(SUB, rows - at)
                sub = (start + at) // SUB
                sums = {}
                for g in range(KEYS // SUB):
                    group = min(max(g - sub + 2, 0), 4)
                    piece = ds[at : at + size, g * 128 : g * 128 + 128]
                    sums[group] = piece if group not in sums else sums[group] + piece
                for group, piece in sums.items():
                    dz_ref[h, 0:size, group * 128 : group * 128 + 128] += piece
            dbias = dot_nt(low, o_ref[...])
            parts = []
            for plane, r_col in ((0, r_w), (1, r_h)):
                same = None
                under = None
                for kk in range(4):
                    base = plane * 512 + kk * 128
                    piece = dbias[:, base : base + 128]
                    ok = (2 * kk + upper) >= r_col
                    yes = jnp.where(ok, piece, 0.0)
                    no = jnp.where(ok, 0.0, piece)
                    same = yes if same is None else same + yes
                    under = no if under is None else under + no
                parts += [same, under]
            dm = dot_tn(ur, jnp.concatenate(parts, axis=1).astype(BF16))
            at = slice(h * 512, h * 512 + 512)
            dm_ref[:, at] = dm if first else dm_in[:, at] + dm
        dq_ref[:, cols] = dq_total * 0.125
        dk_ref[:, cols] = dk_total
        dv_ref[:, cols] = dv_total


def attend_back(order, c, dmix, p, q, k, v, ur, r, o, carry):
    start, rows = CHUNKS[c]
    operands = [dmix, p, q, k, v, ur, r, o]
    aliases = {}
    if carry is not None:
        operands += list(carry)
        aliases = {8 + i: 1 + i for i in range(4)}
    return order(
        functools.partial(attend_back_kernel, start, rows, carry is None),
        operands,
        [vmem(), hbm()] + [vmem()] * (len(operands) - 2),
        (
            sds((rows, DL), F32),
            sds((KEYS, DL), F32),
            sds((KEYS, DL), F32),
            sds((128, HL * 512), F32),
            sds((HL, SUB, 640), F32),
        ),
        [vmem()] * 5,
        scratch_shapes=[pltpu.VMEM((HL, rows, KEYS), BF16), pltpu.SemaphoreType.DMA((HL,))],
        input_output_aliases=aliases,
        mib=14,
        name=f"attend_back_{c}",
    )


def table_sums_kernel(dm_ref, dz_ref, out_ref):
    lane = iota((PAIR, BINS_2D), 0)
    plane_bin = jnp.clip(lane - 64, -32, 31) + 32
    plane_pick = (plane_bin == iota((PAIR, BINS_2D), 1)).astype(F32)
    lane = iota((512, BINS_1D), 0)
    line_bin = jnp.clip(lane - 256, -16, 15) + 16
    line_pick = (line_bin == iota((512, BINS_1D), 1)).astype(F32)
    first = first_lanes()
    flip = (iota((SUB, SUB), 0) + iota((SUB, SUB), 1) == SUB - 1).astype(F32)
    bin_id = iota((1, BINS_1D), 1)
    exact = functools.partial(
        lax.dot_general,
        dimension_numbers=(((1,), (0,)), ((), ())),
        precision=HIGHEST,
        preferred_element_type=F32,
    )
    out_ref[...] = jnp.zeros(out_ref.shape, F32)
    for h in range(HL):
        z = dz_ref[h]
        left = jnp.sum(z[:, 0:128])
        right = jnp.sum(z[:, 512:640])
        band = jnp.concatenate([z[:, 128:512], jnp.zeros((SUB, 128), F32)], axis=1)
        band = pltpu.roll(exact(flip, band), 512 - 127 + 128, 1, stride=1, stride_axis=0)
        line = exact(col_sum(band), line_pick)
        line = line + jnp.where(bin_id == 0, left, 0.0) + jnp.where(bin_id == 31, right, 0.0)
        out_ref[h : h + 1, 0:BINS_1D] = line
        for plane in range(2):
            total = None
            for below in range(2):
                at = h * 512 + plane * 256 + below * 128
                g = dm_ref[plane * 64 : plane * 64 + 64, at : at + 128]
                g = jnp.where(first, g + pltpu.roll(g, 64, 1), 0.0)
                g = pltpu.roll(g, 1 - below, 1, stride=1, stride_axis=0)
                total = g if total is None else total + g
            summed = exact(col_sum(total), plane_pick)
            at = BINS_1D + plane * 64
            out_ref[h : h + 1, at : at + 64] = summed


def table_sums(order, dm, dz):
    return order(
        table_sums_kernel,
        (dm, dz),
        [vmem()] * 2,
        (sds((8, 256), F32),),
        [vmem()],
        name="table_sums",
    )[0]


def project_back_kernel(
    q0, q1, q2, dk_ref, dv_ref, wq_hbm, wk_hbm, wv_hbm, part_ref, bias_ref,
    wq_ref, wk_ref, wv_ref, sems,
):
    copies = [
        pltpu.make_async_copy(src, dst, sems.at[i])
        for i, (src, dst) in enumerate(
            zip((wq_hbm, wk_hbm, wv_hbm), (wq_ref, wk_ref, wv_ref))
        )
    ]
    for copy in copies:
        copy.start()
    sum_q = None
    sum_v = None
    for i, ((start, rows), dq) in enumerate(zip(CHUNKS, (q0, q1, q2))):
        query = dq[...]
        value = dv_ref[start : start + rows, :]
        sum_q = col_sum(query) if sum_q is None else sum_q + col_sum(query)
        sum_v = col_sum(value) if sum_v is None else sum_v + col_sum(value)
        query = query.astype(BF16)
        key = dk_ref[start : start + rows, :].astype(BF16)
        value = value.astype(BF16)
        if i == 0:
            for copy in copies:
                copy.wait()
        part_ref[start : start + rows, :] = (
            dot_nt(query, wq_ref[...]) + dot_nt(key, wk_ref[...]) + dot_nt(value, wv_ref[...])
        )
    bias_ref[...] = jnp.zeros(bias_ref.shape, F32)
    bias_ref[0:1, 0:DL] = sum_q
    bias_ref[0:1, DL:D] = sum_v


def project_back(order, dq, dk, dv, wq, wk, wv):
    return order(
        project_back_kernel,
        (*dq, dk, dv, wq, wk, wv),
        [vmem()] * 5 + [hbm()] * 3,
        (sds((ROWS, D), F32), sds((8, D), F32)),
        [vmem()] * 2,
        scratch_shapes=[pltpu.VMEM((D, DL), BF16)] * 3 + [pltpu.SemaphoreType.DMA((3,))],
        name="project_back",
    )


def taps_kernel(
    count_ref, x_hbm, pt, r0_far, r1_far, r2_far, out_ref,
    text_scr, patch_scr, raw_scr, x_ref, r0, r1, r2, sems,
):
    count = count_ref[0]
    copies = start_all(((x_hbm, x_ref), (r0_far, r0), (r1_far, r1), (r2_far, r2)), sems)
    copies[0].wait()
    load_page(x_ref, count, text_scr, patch_scr, raw_scr)
    for copy in copies[1:]:
        copy.wait()
    out_ref[...] = jnp.zeros(out_ref.shape, F32)
    shifts = tuple(range(-3, 4))
    for c in range(2):
        cols = slice(c * 384, c * 384 + 384)

        def one(b, sums, cols=cols, res=None, first=0):
            base = pl.multiple_of(b * 32, 32)
            win = text_scr[pl.ds(first + base, 48), cols]
            grad = pt[pl.ds(first + base, 32), cols] + 0.5 * res[pl.ds(base, 32), cols]
            out = []
            for shift, total in zip(shifts, sums):
                prod = grad * win[8 + shift : 40 + shift]
                out.append(total + jnp.sum(prod.reshape(4, 8, 384), axis=0))
            return tuple(out)

        sums = tuple(jnp.zeros((8, 384), F32) for _ in shifts)
        sums = lax.fori_loop(0, 8, functools.partial(one, res=r0, first=0), sums)
        sums = lax.fori_loop(0, 8, functools.partial(one, res=r1, first=256), sums)
        for dilate in range(3):
            for tap in range(3):
                row = 3 * dilate + tap
                total = sums[3 + (tap - 1) * (dilate + 1)]
                out_ref[row : row + 1, cols] = col_sum(total)

    def patches(side):
        live, has_left, has_right = grid_masks(side)
        for c in range(D // PAIR):
            cols = slice(c * PAIR, c * PAIR + PAIR)
            win = patch_scr[:, cols]
            grad = jnp.where(live, pt[TEXT:ROWS, cols] + 0.5 * r2[:, cols], 0.0)
            for ds in (-1, 0, 1):
                masked = grad
                if ds == -1:
                    masked = jnp.where(has_left, grad, 0.0)
                if ds == 1:
                    masked = jnp.where(has_right, grad, 0.0)
                for dr in (-1, 0, 1):
                    row = 9 + 3 * (dr + 1) + ds + 1
                    at = MARGIN + dr * side + ds
                    out_ref[row : row + 1, cols] = col_sum(masked * win[at : at + 208])

    by_grid(count, patches)


def tap_sums(order, count, x, part, res):
    return order(
        taps_kernel,
        (count, x, part, *res),
        [smem(), hbm(), vmem()] + [hbm()] * 3,
        (sds((24, D), F32),),
        [vmem()],
        scratch_shapes=PAGE_SCRATCH
        + [pltpu.VMEM((SEQ, D), BF16)]
        + [pltpu.VMEM((rows, D), F32) for _, rows in CHUNKS]
        + [pltpu.SemaphoreType.DMA((4,))],
        mib=14,
        name="tap_sums",
    )[0]


def decode_text_kernel(text_ref, p, s, r0, r1, out_ref, text_scr):
    zero8 = jnp.zeros((8, D), F32)
    text_scr[0:8, :] = zero8
    text_scr[520:528, :] = zero8
    for r, at in ((r0, 0), (r1, 256)):
        for b in range(4):
            res = r[64 * b : 64 * b + 64, :]
            rows = slice(at + 64 * b, at + 64 * b + 64)
            text_scr[8 + at + 64 * b : 72 + at + 64 * b, :] = res + (p[rows, :] + s[rows, :])
    for c in range(2):
        cols = slice(c * 384, c * 384 + 384)
        taps = text_taps(text_ref, cols)

        def one(b, carry, cols=cols, taps=taps):
            base = pl.multiple_of(b * 32, 32)
            win = text_scr[pl.ds(base, 48), cols]
            out_ref[pl.ds(base, 32), cols] = text_conv_block(win, taps, -1).astype(BF16)
            return carry

        lax.fori_loop(0, TEXT // 32, one, 0)


def decode_kernel(
    count_ref, text_ref, patch_ref, p, s, r0_far, r1_far, r2_far, out_ref,
    text_scr, patch_scr, raw_scr, r0, r1, r2, sems,
):
    for copy in start_all(((r0_far, r0), (r1_far, r1), (r2_far, r2)), sems):
        copy.wait()
    decode_text_kernel(text_ref, p, s, r0, r1, out_ref, text_scr)
    count = count_ref[0]
    raw_scr[...] = r2[...] + (p[TEXT:ROWS, :] + s[TEXT:ROWS, :])
    fill_patches(patch_scr, lambda cols: raw_scr[:, cols], count)

    def patches(side):
        for c in range(D // PAIR):
            cols = slice(c * PAIR, c * PAIR + PAIR)
            total = raw_scr[:, cols] + patch_conv_cols(patch_scr[:, cols], patch_ref, cols, side, -1)
            out_ref[TEXT:SEQ, cols] = total[0 : SEQ - TEXT].astype(BF16)

    by_grid(count, patches)


def decode(order, count, text_w, patch_w, part, other, res):
    return order(
        decode_kernel,
        (count, text_w, patch_w, part, other, *res),
        [smem()] + [vmem()] * 4 + [hbm()] * 3,
        (sds((SEQ, D), BF16),),
        [vmem()],
        scratch_shapes=PAGE_SCRATCH
        + [pltpu.VMEM((rows, D), F32) for _, rows in CHUNKS]
        + [pltpu.SemaphoreType.DMA((3,))],
        mib=14,
        name="decode",
    )[0]


def swap_tensor(x):
    return lax.ppermute(x, "tensor", [(0, 1), (1, 0)])


def swap_dp(x, bit, dp):
    return lax.ppermute(x, "dp", [(i, i ^ bit) for i in range(dp)])


def swap_core(parts, dp):
    return (parts[0], swap_dp(parts[1], 1, dp)) if len(parts) == 2 else parts


class Scatter:
    def __init__(self, order, dp, where, pair, bits, name, first, width):
        self.order, self.dp, self.where, self.bits, self.name = order, dp, where, bits, name
        self.window = (first, width)
        self.pairs = [pair]
        self.left = list(range(1, dp.bit_length() - 1))

    def join(self, other):
        self.pairs += other.pairs
        self.window = (self.window[0], self.window[1] + other.window[1])

    def step(self, small=None, extra=None):
        if len(self.pairs[0]) == 1:
            return
        bit = self.bits[0]
        self.bits = self.bits[1:]
        at = self.left.index(bit)
        own, out = halve(
            self.order, self.where, self.pairs, 2 ** len(self.left), 2**at, 1 + bit, *self.window,
            f"{self.name}_{bit}", small, extra,
        )
        self.window = (0, self.window[1])
        self.left.remove(bit)
        self.pairs = [(own, swap_dp(out, 2**bit, self.dp))]

    def total(self):
        if len(self.pairs[0]) == 1:
            first, width = self.window
            whole = self.pairs[0][0][:, first : first + width]
            return lax.psum_scatter(whole, "dp", scatter_dimension=0, tiled=True)
        return self.pairs[0][0] + self.pairs[0][1]


def total_kernel(turned, a0, a1, out):
    both = a0[...] + a1[...]
    out[...] = jnp.transpose(both) if turned else both


def total_of(order, part, turned, name):
    pair = part.pairs[0]
    shape = pair[0].shape[::-1] if turned else pair[0].shape
    return order(
        functools.partial(total_kernel, turned), pair, [vmem()] * 2, (sds(shape, F32),), [vmem()],
        name=name,
    )[0]


def attention_totals_kernel(a0, a1, b0, b1, q_ref, k_ref, v_ref, o_ref, small_ref):
    both = a0[...] + a1[...]
    slab = q_ref.shape[0]
    q_ref[...] = both[0:slab, 0:DL]
    k_ref[...] = both[0:slab, DL:D]
    small_ref[...] = both[slab:]
    both = b0[...] + b1[...]
    v_ref[...] = both[:, 0:DL]
    o_ref[...] = jnp.transpose(both[:, DL:D])


def attention_totals(order, query_key, value_out, slab):
    pairs = [a for part in (query_key, value_out) for a in part.pairs[0]]
    plain = sds((slab, DL), F32)
    return order(
        attention_totals_kernel, pairs, [vmem()] * 4,
        (plain, plain, plain, sds((DL, slab), F32), sds((SMALL, D), F32)), [vmem()] * 5,
        name="attention_totals",
    )


def gather_small_kernel(taps, a0, a1, a2, f0, f1, f2, bias, tab, out):
    out[...] = jnp.zeros(out.shape, F32)
    out[0:18, :] = taps[0:18, :]
    out[18:21, :] = (a0[...] + a1[...] + a2[...])[0:3]
    feed_sums = f0[...] + f1[...] + f2[...]
    out[21:24, :] = feed_sums[1:4, 0:D]
    out[24:25, :] = bias[0:1, :]
    out[25:26, :] = feed_sums[0:1, 0:D]
    out[26:27, :] = feed_sums[0:1, D:]
    out[27 : 27 + HL, 0:256] = tab[0:HL, :]


def gather_small(order, *rest):
    return order(
        gather_small_kernel, rest, [vmem()] * 9, (sds((SMALL, D), F32),), [vmem()],
        name="gather_small",
    )[0]


def finish_kernel(
    place_ref, own, core, other, both,
    text, patch, out_b, gain1, shift1, outer_b, gain2, shift2,
    query_b, value_b, inner_b, line, width, height,
):
    small = own[...] + core[...]
    slab = patch.shape[1]
    turn = lambda a: pltpu.roll(a, lax.rem(D - place_ref[0] * slab, D), 1)[:, 0:slab]
    shard = turn(small[0:24])
    taps = shard + turn(other[...] + both[...])
    for i in range(3):
        text[i] = taps[3 * i : 3 * i + 3]
    patch[...] = taps[9:18]
    for i, ref in enumerate((out_b, gain1, shift1, outer_b, gain2, shift2)):
        ref[...] = shard[18 + i]
    query_b[...] = small[24, 0:DL]
    value_b[...] = small[24, DL:D]
    inner_b[0:D] = small[25]
    inner_b[D:FL] = small[26]
    tables = jnp.transpose(small[24:40, 0:256])
    line[...] = tables[0:32, 3 : 3 + HL]
    width[...] = tables[32:96, 3 : 3 + HL]
    height[...] = tables[96:160, 3 : 3 + HL]


def finish(order, place, own, core, other, both, slab):
    f = lambda *shape: sds(shape, F32)
    shapes = (f(3, 3, slab), f(9, slab)) + (f(slab),) * 6
    shapes += (f(DL), f(DL), f(FL), f(32, HL), f(64, HL), f(64, HL))
    return order(
        finish_kernel, (place, own, core, other, both), [smem()] + [vmem()] * 4, shapes,
        [vmem()] * 14, name="finish",
    )


def swap_both(x, dp):
    pairs = [(2 * i + t, 2 * (i ^ 1) + (t ^ 1)) for i in range(dp) for t in range(2)]
    return lax.ppermute(x, ("dp", "tensor"), pairs)


def per_device(
    dp,
    page_tokens,
    patch_counts,
    token_boxes,
    text_weight,
    patch_weight,
    query_weight,
    query_bias,
    key_weight,
    value_weight,
    value_bias,
    out_weight,
    out_bias,
    line_table,
    width_table,
    height_table,
    norm1_gain,
    norm1_shift,
    inner_weight,
    inner_bias,
    outer_weight,
    outer_bias,
    norm2_gain,
    norm2_shift,
    cotangent,
):
    place = lax.axis_index("dp")
    half = lax.axis_index("tensor")
    core = place % 2
    bits = [(place // 2**i) % 2 for i in range(4)]
    where = jnp.stack([half] + bits).astype(jnp.int32)
    x = page_tokens.reshape(SEQ, D)
    cot = cotangent.reshape(SEQ, D)
    slab = D // dp if dp == 16 else None
    order = Order()

    z, m, o, u, r, wo_mine, o_far, ur_far, r_far = make_tables(
        order,
        where,
        jnp.concatenate([jnp.transpose(a) for a in (line_table, width_table, height_table)], axis=1),
        token_boxes.reshape(2, SEQ),
        out_weight,
    )
    wo_a = swap_tensor(wo_mine)
    row = lax.broadcasted_iota(jnp.int32, (8, 1), 0)
    bias = jnp.where(row == 0, query_bias[None, :], value_bias[None, :]).astype(F32)
    (q0, q1, q2, k, v), enc, enc_low, far = encode(
        order, patch_counts, x, text_weight, patch_weight, bias,
        query_weight, key_weight, value_weight,
    )
    q = (q0, q1, q2)
    q_far, k_far, v_far = far[0:3], far[3], far[4]

    vec = jnp.zeros((8, 1), F32)
    for i, a in enumerate(
        (out_bias, norm1_gain, norm1_shift, outer_bias, norm2_gain, norm2_shift)
    ):
        vec = jnp.where(row == i, a[None, :].astype(F32), vec)
    bi = jnp.broadcast_to(inner_bias[None, :].astype(F32), (8, FL))
    probs, mix, mix_low, mix_other = ([None] * 3 for _ in range(4))
    xhat, rstd, hlow, act, slope, outer, outer_other = ([None] * 3 for _ in range(7))

    def attention_of(c):
        p, a, low = attend(order, c, patch_counts, q[c], k, v, u, r, m, o, z)
        probs[c], mix[c], mix_low[c], mix_other[c] = p, a, low, swap_tensor(a)

    def feed_of(c):
        got = feed(
            order, c, where, mix[c], mix_other[c], enc[c], vec, out_weight, wo_a, wo_b,
            inner_weight, bi, outer_weight,
        )
        for keep, a in zip((xhat, rstd, hlow, act, slope, outer), got):
            keep[c] = a
        outer_other[c] = swap_tensor(got[5])

    attention_of(ORDER[0])
    wo_a = pass_on(order, wo_a)
    wo_b = swap_dp(wo_a, 1, dp)
    attention_of(ORDER[1])
    feed_of(ORDER[0])
    attention_of(ORDER[2])
    feed_of(ORDER[1])
    feed_of(ORDER[2])
    layer_out, inner_grad, outer_grad = None, None, None
    dres2, g2, g1, dhid, dhid_other, sums2 = ([None] * 3 for _ in range(6))
    for c in ORDER:
        got = feed_back(
            order, c, patch_counts, outer[c], outer_other[c], xhat[c], cot, vec, outer_weight,
            slope[c], inner_weight, layer_out,
        )
        layer_out = got[0]
        for keep, a in zip((dres2, g2, g1, dhid, sums2), got[1:]):
            keep[c] = a
        dhid_other[c] = swap_tensor(got[4])
        last = c == ORDER[2]
        inner_grad = chunk_grads(
            order, slab, where, hlow[c], g1[c], inner_grad, last, f"inner_grads_{c}"
        )
        outer_grad = chunk_grads(
            order, slab, where, g2[c], act[c], outer_grad, last, f"outer_grads_{c}"
        )
        if not last:
            inner_grad, outer_grad = inner_grad[0], outer_grad[0]
    scatter = functools.partial(Scatter, order, dp, where)
    x_first, z_first = (1, 2, 3), (2, 3, 1)
    inner_pair, outer_pair = swap_core(inner_grad, dp), swap_core(outer_grad, dp)
    inner = scatter(inner_pair, x_first, "inner", 0, D)
    inner_b = scatter(inner_pair, x_first, "inner_b", D, D)
    outer_a = scatter(outer_pair, x_first, "outer_a", 0, 512)
    outer_b = scatter(outer_pair, z_first, "outer_b", 512, 1024)
    carry = None
    dres1, g0, dq, sums1 = ([None] * 3 for _ in range(4))
    for c in ORDER:
        got = norm_one_back(
            order, c, dres2[c], dhid[c], dhid_other[c], xhat[c], rstd[c], vec, out_weight
        )
        dres1[c], g0[c], _, sums1[c] = got
        if c == ORDER[0]:
            inner.step()
            outer_b.step()
            inner_b.step()
        if c == ORDER[1]:
            outer_a.step()
            inner.step()
            outer_b.step()
        if c == ORDER[2]:
            inner_b.step()
            inner.step()
            outer_b.step()
        dq[c], *carry = attend_back(
            order, c, got[2], probs[c], q_far[c], k_far, v_far, ur_far, r_far, o_far, carry
        )
    dk, dv, dm, dz = carry
    outer_a.step()
    inner_b.step()
    if dp == 16:
        total_inner = total_of(order, inner, False, "inner_total")
        total_outer_b = total_of(order, outer_b, True, "outer_b_total")
    got = attention_grads(order, slab, where, enc_low, dq, dk, dv, g0, mix_low)
    half_way = len(got) // 2
    query_key = scatter(swap_core(got[:half_way], dp), x_first, "query_key", 0, D)
    value_out = scatter(swap_core(got[half_way:], dp), z_first, "value_out", 0, D)
    part, bias_sums = project_back(order, dq, dk, dv, query_weight, key_weight, value_weight)
    part_other = swap_tensor(part)
    tables = table_sums(order, dm, dz)
    taps = tap_sums(order, patch_counts, x, part, dres1)
    small = gather_small(order, taps, *sums1, *sums2, bias_sums, tables)
    outer_a.step()
    if dp == 16:
        total_inner_b = total_of(order, inner_b, False, "inner_b_total")
    query_key.step(small, "first")
    value_out.step()
    query_key.step(None, "more")
    value_out.step()
    if dp == 16:
        total_outer_a = total_of(order, outer_a, True, "outer_a_total")
    query_key.step(None, "more")
    value_out.step()
    input_grad = decode(order, patch_counts, text_weight, patch_weight, part, part_other, dres1)
    if dp == 16:
        inner_total = jnp.concatenate([total_inner, total_inner_b], axis=1)
        sum_outer = jnp.concatenate([total_outer_a, total_outer_b], axis=0)
        grad_q, grad_k, grad_v, grad_o, small = attention_totals(
            order, query_key, value_out, slab
        )
    else:
        grad_q, grad_k = jnp.split(query_key.total(), 2, axis=1)
        grad_v, grad_o = jnp.split(value_out.total(), 2, axis=1)
        grad_o = jnp.transpose(grad_o)
        inner_total = jnp.concatenate([inner.total(), inner_b.total()], axis=1)
        sum_outer = jnp.concatenate([outer_a.total(), outer_b.total()], axis=1)
        sum_outer = jnp.transpose(sum_outer)
        bit = 2
        while bit < dp:
            small = small + swap_dp(small, bit, dp)
            bit *= 2
    small = finish(
        order, jnp.reshape(place, (1,)).astype(jnp.int32), small, swap_dp(small, 1, dp),
        swap_tensor(small[0:24]), swap_both(small[0:24], dp), D // dp,
    )
    text, patch, out_b, gain1, shift1, outer_b, gain2, shift2 = small[:8]
    query_b, value_b, inner_b, line, width, height = small[8:]
    return (
        layer_out.reshape(1, SEQ, D),
        input_grad.reshape(1, SEQ, D),
        text,
        patch,
        grad_q,
        query_b,
        grad_k,
        grad_v,
        value_b,
        grad_o,
        out_b,
        line,
        width,
        height,
        gain1,
        shift1,
        inner_total,
        inner_b,
        sum_outer,
        outer_b,
        gain2,
        shift2,
    )


def solution(mesh):
    placed = (
        P("dp", None, None),
        P("dp"),
        P("dp", None, None),
        P(),
        P(),
        P(None, "tensor"),
        P("tensor"),
        P(None, "tensor"),
        P(None, "tensor"),
        P("tensor"),
        P("tensor", None),
        P(),
        P(None, "tensor"),
        P(None, "tensor"),
        P(None, "tensor"),
        P(),
        P(),
        P(None, "tensor"),
        P("tensor"),
        P("tensor", None),
        P(),
        P(),
        P(),
        P("dp", None, None),
    )
    return jax.shard_map(
        functools.partial(per_device, mesh.shape["dp"]),
        mesh=mesh,
        in_specs=placed,
        out_specs=(
            P("dp", None, None),
            P("dp", None, None),
            P(None, None, "dp"),
            P(None, "dp"),
            P("dp", "tensor"),
            P("tensor"),
            P("dp", "tensor"),
            P("dp", "tensor"),
            P("tensor"),
            P("tensor", "dp"),
            P("dp"),
            P(None, "tensor"),
            P(None, "tensor"),
            P(None, "tensor"),
            P("dp"),
            P("dp"),
            P("dp", "tensor"),
            P("tensor"),
            P("tensor", "dp"),
            P("dp"),
            P("dp"),
            P("dp"),
        ),
        check_vma=False,
    )
```

```python
import functools

import jax
import jax.numpy as jnp
from jax import lax
from jax.experimental import pallas as pl
from jax.experimental.pallas import tpu as pltpu
from jax.sharding import PartitionSpec as P

HEADS = 12
TEXT = 512
GRID_SMALL = 7
GRID_LARGE = 14
BINS_1D = 32
BINS_2D = 64
BIN_WIDTH = 8

F32 = jnp.float32
BF16 = jnp.bfloat16
EPS = 1e-05
NEG = -1000000000.0
HIGHEST = lax.Precision.HIGHEST

D = 768
SEQ = 708
ROWS = 720
KEYS = 768
CHUNKS = ((0, 256), (256, 256), (512, 208))
ORDER = (2, 0, 1)
SUB = 128
PAIR = 128
HL = 6
DL = 384
FL = 1536
MARGIN = 16
MIB = 1024 * 1024


def vmem():
    return pl.BlockSpec(memory_space=pltpu.VMEM)


def anywhere():
    return pl.BlockSpec(memory_space=pl.ANY)


def hbm():
    return pl.BlockSpec(memory_space=pltpu.HBM)


def smem():
    return pl.BlockSpec(memory_space=pltpu.SMEM)


def params(mib):
    return pltpu.CompilerParams(vmem_limit_bytes=mib * MIB)


def sds(shape, dtype):
    return jax.ShapeDtypeStruct(shape, dtype)


TOKEN = jax.ShapeDtypeStruct((8, 128), jnp.float32)


class Order:
    def __init__(self):
        self.token = None

    def __call__(
        self, kernel, operands, in_specs, out_shape, out_specs, mib=10, us=1, out=(), into=(),
        scratch_shapes=(), **more,
    ):
        operands, in_specs = list(operands), list(in_specs)
        count, outs, moved = len(operands), len(out_shape), len(out) + len(into)
        operands += [*out, *into]
        in_specs += [vmem()] * len(out) + [hbm()] * len(into)
        has_token = self.token is not None
        grid = "grid" in more
        token_spec = pl.BlockSpec(TOKEN.shape, lambda *i: (0, 0)) if grid else vmem()
        if has_token:
            operands.append(self.token)
            in_specs.append(token_spec)
        shapes = [sds(a.shape, a.dtype) for a in (*out, *into)]
        specs = [hbm()] * len(out) + [vmem()] * len(into)
        scratch_shapes = list(scratch_shapes)
        if moved:
            scratch_shapes.append(pltpu.SemaphoreType.DMA((moved,)))

        def body(*refs):
            rest = list(refs)
            sources = rest[count : count + moved]
            del rest[count : count + moved + has_token]
            at = count + outs
            targets = rest[at : at + moved]
            rest[at + moved][...] = jnp.zeros(TOKEN.shape, F32)
            del rest[at : at + moved + 1]
            copies = start_all(zip(sources, targets), rest.pop()) if moved else []
            kernel(*rest)
            for copy in copies:
                copy.wait()

        got = pl.pallas_call(
            body,
            out_shape=tuple(out_shape) + tuple(shapes) + (TOKEN,),
            in_specs=in_specs,
            out_specs=tuple(out_specs) + tuple(specs) + (token_spec,),
            scratch_shapes=scratch_shapes,
            compiler_params=params(mib),
            cost_estimate=cost(us),
            **more,
        )(*operands)
        self.token = got[-1]
        if moved:
            return got[:outs], got[outs:-1]
        return got[:-1]


def start_all(pairs, sems, first=0):
    copies = [
        pltpu.make_async_copy(src, dst, sems.at[first + i]) for i, (src, dst) in enumerate(pairs)
    ]
    for copy in copies:
        copy.start()
    return copies


def dot(a, b):
    return lax.dot_general(a, b, (((1,), (0,)), ((), ())), preferred_element_type=F32)


def dot_nt(a, b):
    return lax.dot_general(a, b, (((1,), (1,)), ((), ())), preferred_element_type=F32)


def dot_tn(a, b):
    return lax.dot_general(a, b, (((0,), (0,)), ((), ())), preferred_element_type=F32)


def cost(us):
    return pl.CostEstimate(flops=int(us * 1.0e6), bytes_accessed=int(us * 1.0e3), transcendentals=0)


def iota(shape, dim):
    return lax.broadcasted_iota(jnp.int32, shape, dim)


def first_lanes():
    return iota((1, PAIR), 1) < 64


def tables_kernel(
    where_ref, tab_ref, boxes_hbm, wo_hbm,
    z_ref, m_ref, o_ref, u_ref, r_ref, mine_ref, ur_ref,
    box_scr, boxes_ref, wo_ref, sems,
):
    half = DL // 2
    rows = pl.ds(pl.multiple_of(where_ref[1] * half, half), half)
    copies = start_all(
        (
            (boxes_hbm, boxes_ref),
            (wo_hbm.at[rows, :], wo_ref),
        ),
        sems,
    )
    for copy in copies:
        copy.wait()
    mine_ref[...] = wo_ref[...].astype(F32)
    lane = iota((BINS_1D, 768), 1)
    bucket = jnp.where(lane < 640, jnp.clip(lane - 256, -16, 15) + 16, 0)
    line_pick = (bucket == iota((BINS_1D, 768), 0)).astype(BF16)
    line_base = dot(tab_ref[:, 0:BINS_1D], line_pick)
    lane = iota((BINS_2D, PAIR), 1)
    bucket = jnp.clip(lane - 64, -32, 31) + 32
    plane_pick = (bucket == iota((BINS_2D, PAIR), 0)).astype(BF16)
    bases = [
        dot(tab_ref[:, BINS_1D + 64 * plane : BINS_1D + 64 * plane + 64], plane_pick)
        for plane in range(2)
    ]
    first = first_lanes()
    zeros = jnp.zeros((64, PAIR), BF16)
    for h in range(HL):
        spread = jnp.broadcast_to(line_base[h : h + 1, :], (SUB, 768))
        rolled = pltpu.roll(spread, 0, 1, stride=1, stride_axis=0)
        z_ref[h] = rolled[:, :640]
        for plane in range(2):
            spread = jnp.broadcast_to(bases[plane][h : h + 1, :], (64, PAIR))
            for below in range(2):
                one = pltpu.roll(spread, 64 + below, 1, stride=1, stride_axis=0)
                both = jnp.where(first, one, pltpu.roll(one, 64, 1)).astype(BF16)
                start = h * 512 + plane * 256 + below * 128
                m_ref[plane * 64 : plane * 64 + 64, start : start + 128] = both
                m_ref[64 - plane * 64 : 128 - plane * 64, start : start + 128] = zeros
    box_scr[...] = jnp.full((8, KEYS), -1, jnp.int32)
    box_scr[0:2, 0:SEQ] = boxes_ref[...]
    row = iota((512, KEYS), 0)
    value = 8 * (row % 64) + row // 64
    for plane in range(2):
        o_ref[plane * 512 : plane * 512 + 512, :] = (
            value == box_scr[plane : plane + 1, :]
        ).astype(F32).astype(BF16)
    turned = jnp.transpose(box_scr[...].astype(F32))[0:ROWS, :].astype(jnp.int32)
    left = jnp.broadcast_to(turned[:, 0:1], (ROWS, PAIR))
    right = jnp.broadcast_to(turned[:, 1:2], (ROWS, PAIR))
    lane = iota((ROWS, PAIR), 1)
    both = jnp.where(lane < 64, left, right)
    r_ref[0] = left & 7
    r_ref[1] = right & 7
    upper = lax.shift_right_logical(both, 3)
    inner = lane & 63
    u_ref[...] = (upper == inner).astype(F32).astype(BF16)
    ur_ref[...] = (63 - upper == inner).astype(F32).astype(BF16)


def make_tables(order, where, tab, boxes, wo):
    return order(
        tables_kernel,
        (where, tab, boxes, wo),
        [smem(), vmem()] + [hbm()] * 2,
        (
            sds((HL, SUB, 640), F32),
            sds((128, HL * 512), BF16),
            sds((1024, KEYS), BF16),
            sds((ROWS, PAIR), BF16),
            sds((2, ROWS, PAIR), jnp.int32),
            sds((DL // 2, D), F32),
            sds((ROWS, PAIR), BF16),
        ),
        [vmem()] * 7,
        us=20000,
        scratch_shapes=[
            pltpu.VMEM((8, KEYS), jnp.int32),
            pltpu.VMEM(boxes.shape, jnp.int32),
            pltpu.VMEM((DL // 2, D), BF16),
            pltpu.SemaphoreType.DMA((2,)),
        ],
        name="bias_tables",
    )


def copy_kernel(src, dst, scr, sems):
    for pair in ((src, scr), (scr, dst)):
        copy = pltpu.make_async_copy(*pair, sems.at[0])
        copy.start()
        copy.wait()


def pass_on(order, x):
    return order(
        copy_kernel,
        (x,),
        [anywhere()],
        (sds(x.shape, x.dtype),),
        [anywhere()],
        scratch_shapes=[pltpu.VMEM(x.shape, x.dtype), pltpu.SemaphoreType.DMA((1,))],
        name="pass_on",
    )[0]


def text_taps(text_ref, cols):
    taps = {}
    for dilate in range(3):
        for tap in range(3):
            shift = (tap - 1) * (dilate + 1)
            row = text_ref[dilate, tap : tap + 1, cols].astype(F32)
            taps[shift] = row if shift not in taps else taps[shift] + row
    return taps


def text_conv_block(win, taps, sign):
    total = win[8:40] * (taps[0] + 1.0)
    for shift in (-3, -2, -1, 1, 2, 3):
        start = 8 + sign * shift
        total = total + win[start : start + 32] * taps[shift]
    return total


def grid_masks(side):
    place = iota((208, PAIR), 0)
    row = jnp.floor((place.astype(F32) + 0.5) * (1.0 / side)).astype(jnp.int32)
    col = place - row * side
    return (place < side * side, col >= 1, col <= side - 2)


def patch_conv_cols(win, patch_ref, cols, side, sign):
    live, has_left, has_right = grid_masks(side)
    total = None
    for ds in (-1, 0, 1):
        part = None
        for dr in (-1, 0, 1):
            tap = 3 * (dr + 1) + ds + 1
            start = MARGIN + sign * (dr * side + ds)
            term = win[start : start + 208] * patch_ref[tap : tap + 1, cols].astype(F32)
            part = term if part is None else part + term
        if ds * sign == -1:
            part = jnp.where(has_left, part, 0.0)
        if ds * sign == 1:
            part = jnp.where(has_right, part, 0.0)
        total = part if total is None else total + part
    return jnp.where(live, total, 0.0)


def fill_patches(patch_scr, source, count):
    zero = jnp.zeros((MARGIN, D), F32)
    patch_scr[0:MARGIN, :] = zero
    patch_scr[MARGIN + 208 : MARGIN + 208 + MARGIN, :] = zero
    live = iota((208, PAIR), 0) < count
    for c in range(D // PAIR):
        cols = slice(c * PAIR, c * PAIR + PAIR)
        patch_scr[MARGIN : MARGIN + 208, cols] = jnp.where(live, source(cols), 0.0)


def load_page(x_ref, count, text_scr, patch_scr, raw_scr):
    zero8 = jnp.zeros((8, D), F32)
    text_scr[0:8, :] = zero8
    text_scr[520:528, :] = zero8
    for b in range(TEXT // 64):
        text_scr[8 + 64 * b : 72 + 64 * b, :] = x_ref[64 * b : 64 * b + 64, :].astype(F32)
    raw_scr[...] = jnp.zeros((208, D), F32)
    raw_scr[0 : SEQ - TEXT, :] = x_ref[TEXT:SEQ, :].astype(F32)
    fill_patches(patch_scr, lambda cols: raw_scr[:, cols], count)


PAGE_SCRATCH = [
    pltpu.VMEM((528, D), F32),
    pltpu.VMEM((208 + 2 * MARGIN, D), F32),
    pltpu.VMEM((208, D), F32),
]


def by_grid(count, patches):
    large = count == GRID_LARGE * GRID_LARGE

    @pl.when(large)
    def _():
        patches(GRID_LARGE)

    @pl.when(jnp.logical_not(large))
    def _():
        patches(GRID_SMALL)


def encode_kernel(
    count_ref, x_hbm, text_ref, patch_ref, bias_ref, wq_hbm, wk_hbm, wv_hbm,
    q0, q1, q2, k_ref, v_ref, e0, e1, e2, l0, l1, l2,
    text_scr, patch_scr, raw_scr, x_ref, wq_ref, wk_ref, wv_ref, sems,
):
    copies = start_all(
        ((x_hbm, x_ref), (wq_hbm, wq_ref), (wk_hbm, wk_ref), (wv_hbm, wv_ref)), sems
    )
    count = count_ref[0]
    copies[0].wait()
    load_page(x_ref, count, text_scr, patch_scr, raw_scr)

    for c in range(2):
        cols = slice(c * 384, c * 384 + 384)
        taps = text_taps(text_ref, cols)

        def one(b, carry, cols=cols, taps=taps, out=None, first=0):
            base = pl.multiple_of(b * 32, 32)
            win = text_scr[pl.ds(first + base, 48), cols]
            out[pl.ds(base, 32), cols] = text_conv_block(win, taps, 1)
            return carry

        for (first, rows), out in zip(CHUNKS, (e0, e1)):
            lax.fori_loop(0, rows // 32, functools.partial(one, out=out, first=first), 0)

    def patches(side):
        for c in range(D // PAIR):
            cols = slice(c * PAIR, c * PAIR + PAIR)
            e2[:, cols] = raw_scr[:, cols] + patch_conv_cols(
                patch_scr[:, cols], patch_ref, cols, side, 1
            )

    by_grid(count, patches)
    for copy in copies[1:]:
        copy.wait()
    for (start, rows), e, low, q in zip(CHUNKS, (e0, e1, e2), (l0, l1, l2), (q0, q1, q2)):
        enc = e[...].astype(BF16)
        low[...] = enc
        query = (dot(enc, wq_ref[...]) + bias_ref[0:1, :]).astype(BF16)
        q[...] = query * jnp.asarray(0.125, BF16)
        k_ref[start : start + rows, :] = dot(enc, wk_ref[...]).astype(BF16)
        value = dot(enc, wv_ref[...]) + bias_ref[1:2, :]
        v_ref[start : start + rows, :] = value.astype(BF16)
    k_ref[ROWS:KEYS, :] = jnp.zeros((KEYS - ROWS, DL), BF16)
    v_ref[ROWS:KEYS, :] = jnp.zeros((KEYS - ROWS, DL), BF16)


def encode(order, count, x, text, patch, bias, wq, wk, wv, out):
    chunk = lambda width, dtype: tuple(sds((rows, width), dtype) for _, rows in CHUNKS)
    keys = (sds((KEYS, DL), BF16), sds((KEYS, DL), BF16))
    got, far = order(
        encode_kernel,
        (count, x, text, patch, bias, wq, wk, wv),
        [smem(), hbm()] + [vmem()] * 3 + [hbm()] * 3,
        chunk(DL, BF16) + keys + chunk(D, F32) + chunk(D, BF16),
        [vmem()] * 11,
        scratch_shapes=PAGE_SCRATCH
        + [pltpu.VMEM((SEQ, D), BF16)]
        + [pltpu.VMEM((D, DL), BF16)] * 3
        + [pltpu.SemaphoreType.DMA((4,))],
        mib=12,
        us=8000,
        out=out,
        name="encode_project",
    )
    return got[0:5], got[5:8], got[8:11], far


def bias_rows(e, r_col, k, rows):
    step = 2 * k + (iota((rows, PAIR), 1) >= 64).astype(jnp.int32)
    return jnp.where(step >= r_col, e[0], e[1]).astype(BF16)


def line_rows(z_ref, h, sub, rows):
    groups = [min(max(g - sub + 2, 0), 4) for g in range(KEYS // SUB)]
    return jnp.concatenate([z_ref[h, 0:rows, g * 128 : g * 128 + 128] for g in groups], axis=1)


def attend_kernel(
    start, rows, count_ref, q_ref, k_ref, v_ref, u_ref, r_ref, m_ref, o_ref, z_ref,
    p_ref, mix_ref, low_ref,
):
    live = iota((1, KEYS), 1) < TEXT + count_ref[0]
    first = first_lanes()
    r_w = r_ref[0, start : start + rows, :]
    r_h = r_ref[1, start : start + rows, :]
    u = u_ref[start : start + rows, :]
    for pair in range(HL // 2):
        cols = slice(pair * PAIR, pair * PAIR + PAIR)
        q = q_ref[:, cols]
        k = k_ref[:, cols]
        v = v_ref[:, cols]
        mixed = []
        for half in range(2):
            h = 2 * pair + half
            mine = first if half == 0 else jnp.logical_not(first)
            qm = jnp.where(mine, q, jnp.zeros_like(q))
            e = dot(u, m_ref[:, h * 512 : h * 512 + 512])
            parts = [bias_rows((e[:, 0:128], e[:, 128:256]), r_w, kk, rows) for kk in range(4)]
            parts += [bias_rows((e[:, 256:384], e[:, 384:512]), r_h, kk, rows) for kk in range(4)]
            picked = jnp.concatenate(parts, axis=1)
            s = dot(picked, o_ref[...]) + dot_nt(qm, k)
            pieces = []
            for at in range(0, rows, SUB):
                size = min(SUB, rows - at)
                pieces.append(line_rows(z_ref, h, (start + at) // SUB, size))
            s = s + jnp.concatenate(pieces, axis=0)
            s = jnp.where(live, s, NEG)
            top = jnp.max(s, axis=1, keepdims=True)
            ex = jnp.exp(s - top)
            total = jnp.sum(ex, axis=1, keepdims=True)
            prob = (ex * (1.0 / total)).astype(BF16)
            p_ref[h] = prob
            mixed.append(dot(prob, v))
        low = jnp.where(first, mixed[0], mixed[1]).astype(BF16)
        low_ref[:, cols] = low
        mix_ref[:, cols] = low.astype(F32)


def attend(order, c, count, q, k, v, u, r, m, o, z, out):
    start, rows = CHUNKS[c]
    return order(
        functools.partial(attend_kernel, start, rows),
        (count, q, k, v, u, r, m, o, z),
        [smem()] + [vmem()] * 8,
        (sds((HL, rows, KEYS), BF16), sds((rows, DL), F32), sds((rows, DL), BF16)),
        [vmem()] * 3,
        out=out,
        name=f"attend_{c}",
    )


def feed_kernel(
    where_ref, own_ref, other_ref, enc_hbm, vec_ref, wo_ref, wo_a_ref, wo_b_ref, wi_ref, bi_ref,
    w2_ref, xhat_ref, rstd_ref, hlow_ref, act_ref, slope_ref, part_ref, enc_ref, sems,
):
    (copy,) = start_all(((enc_hbm, enc_ref),), sems)
    half = where_ref[0]
    core = where_ref[1]
    own = dot(own_ref[...].astype(BF16), wo_ref[...])
    other = other_ref[...].astype(BF16)
    low = jnp.where(core == 0, wo_a_ref[...], wo_b_ref[...]).astype(BF16)
    high = jnp.where(core == 0, wo_b_ref[...], wo_a_ref[...]).astype(BF16)
    other = dot(other, jnp.concatenate([low, high], axis=0))
    attended = jnp.where(half == 0, own, other) + jnp.where(half == 0, other, own)
    copy.wait()
    v = enc_ref[...] + (attended + vec_ref[0:1, :])
    centre = v - jnp.mean(v, axis=1, keepdims=True)
    rstd = lax.rsqrt(jnp.mean(centre * centre, axis=1, keepdims=True) + EPS)
    xhat = centre * rstd
    xhat_ref[...] = xhat
    rstd_ref[...] = jnp.broadcast_to(rstd, rstd_ref.shape)
    hlow = (xhat * vec_ref[1:2, :] + vec_ref[2:3, :]).astype(BF16)
    hlow_ref[...] = hlow
    total = None
    for n in range(FL // 512):
        cols = slice(n * 512, n * 512 + 512)
        pre = dot(hlow, wi_ref[:, cols]) + bi_ref[0:1, cols]
        gate = 0.5 + 0.5 * lax.erf(pre * 0.7071067811865476)
        slope_ref[:, cols] = gate + pre * (0.3989422804014327 * jnp.exp(-0.5 * pre * pre))
        act = (pre * gate).astype(BF16)
        act_ref[:, cols] = act
        term = dot(act, w2_ref[cols, :])
        total = term if total is None else total + term
    part_ref[...] = total


def feed(order, c, where, own, other, enc, vec, wo, wo_a, wo_b, wi, bi, w2, out):
    _, rows = CHUNKS[c]
    return order(
        feed_kernel,
        (where, own, other, enc, vec, wo, wo_a, wo_b, wi, bi, w2),
        [smem()] + [vmem()] * 2 + [hbm()] + [vmem()] * 7,
        (
            sds((rows, D), F32),
            sds((rows, 128), F32),
            sds((rows, D), BF16),
            sds((rows, FL), BF16),
            sds((rows, FL), F32),
            sds((rows, D), F32),
        ),
        [vmem()] * 6,
        scratch_shapes=[pltpu.VMEM((rows, D), F32), pltpu.SemaphoreType.DMA((1,))],
        out=out,
        name=f"feed_{c}",
    )


def norm_back(dy, xhat, rstd, gain):
    dxh = dy * gain
    return rstd * (
        dxh
        - jnp.mean(dxh, axis=1, keepdims=True)
        - xhat * jnp.mean(dxh * xhat, axis=1, keepdims=True)
    )


def col_sum(x):
    return jnp.sum(x, axis=0, keepdims=True)


def feed_back_kernel(
    start, rows, first, count_ref, own_ref, other_ref, xhat1_ref, cot_ref, vec_ref, w2_ref,
    slope_ref, wi_ref, *rest,
):
    if not first:
        rest = rest[1:]
    out_ref, dres_ref, g2_ref, g1_ref, part_ref, sums_ref = rest
    place = start + iota((rows, 1), 0)
    live = place < TEXT + count_ref[0]
    hidden = xhat1_ref[...] * vec_ref[1:2, :] + vec_ref[2:3, :]
    v = hidden + ((own_ref[...] + other_ref[...]) + vec_ref[3:4, :])
    centre = v - jnp.mean(v, axis=1, keepdims=True)
    rstd = lax.rsqrt(jnp.mean(centre * centre, axis=1, keepdims=True) + EPS)
    xhat = centre * rstd
    y = xhat * vec_ref[4:5, :] + vec_ref[5:6, :]
    out_ref[0:rows, :] = jnp.where(live, y, 0.0).astype(BF16)
    dy = jnp.where(live, cot_ref[0:rows, :].astype(F32), 0.0)
    sums_ref[...] = jnp.zeros(sums_ref.shape, F32)
    sums_ref[2:3, 0:D] = col_sum(dy * xhat)
    sums_ref[3:4, 0:D] = col_sum(dy)
    dres = norm_back(dy, xhat, rstd, vec_ref[4:5, :])
    dres_ref[...] = dres
    sums_ref[1:2, 0:D] = col_sum(dres)
    g2 = dres.astype(BF16)
    g2_ref[...] = g2
    total = None
    for n in range(FL // 512):
        cols = slice(n * 512, n * 512 + 512)
        d_inner = dot_nt(g2, w2_ref[cols, :]) * slope_ref[:, cols]
        sums_ref[0:1, cols] = col_sum(d_inner)
        g1 = d_inner.astype(BF16)
        g1_ref[:, cols] = g1
        term = dot_nt(g1, wi_ref[:, cols])
        total = term if total is None else total + term
    part_ref[...] = total


def feed_back(order, c, count, own, other, xhat1, cot, vec, w2, slope, wi, out_so_far):
    start, rows = CHUNKS[c]
    high = 256 if start == TEXT else rows
    block = pl.BlockSpec((high, D), lambda i: (start // high, 0))
    whole = lambda a: pl.BlockSpec(a.shape, lambda i: (0, 0))
    shapes = (
        sds((SEQ, D), BF16),
        sds((rows, D), F32),
        sds((rows, D), BF16),
        sds((rows, FL), BF16),
        sds((rows, D), F32),
        sds((8, FL), F32),
    )
    operands = [count, own, other, xhat1, cot, vec, w2, slope, wi]
    specs = [smem()] + [vmem()] * 3 + [block] + [vmem()] * 4
    aliases = {}
    if out_so_far is not None:
        operands.append(out_so_far)
        specs.append(anywhere())
        aliases = {9: 0}
    return order(
        functools.partial(feed_back_kernel, start, rows, out_so_far is None),
        operands,
        specs,
        shapes,
        [block] + [vmem()] * 5,
        grid=(1,),
        input_output_aliases=aliases,
        us=15000 if c == ORDER[0] else 1,
        name=f"feed_back_{c}",
    )


def store_slabs(slab, core, grad, keep_ref, send_ref):
    for i in range(D // (2 * slab)):
        even = grad[2 * i * slab : (2 * i + 1) * slab]
        odd = grad[(2 * i + 1) * slab : (2 * i + 2) * slab]
        keep_ref[i * slab : (i + 1) * slab, :] = jnp.where(core == 0, even, odd)
        send_ref[i * slab : (i + 1) * slab, :] = jnp.where(core == 0, odd, even)


def tn_sum(lefts, rights):
    total = None
    for left, right in zip(lefts, rights):
        term = dot_tn(left[...], right[...].astype(BF16))
        total = term if total is None else total + term
    return total


def put_grads(slab, where_ref, grad, outs):
    if slab is None:
        outs[0][...] = grad
    else:
        store_slabs(slab, where_ref[1], grad, *outs)


def chunk_grads_kernel(slab, has_total, where_ref, left_ref, right_ref, *refs):
    grad = dot_tn(left_ref[...], right_ref[...])
    if has_total:
        grad = refs[0][...] + grad
    put_grads(slab, where_ref, grad, refs[has_total:])


def chunk_grads(order, slab, where, left, right, total, last, name):
    width = right.shape[1]
    block = 512
    piece = lambda rows: pl.BlockSpec((rows, block), lambda i: (0, i))
    whole = pl.BlockSpec(left.shape, lambda i: (0, 0))
    apart = last and slab is not None
    rows, count = (D // 2, 2) if apart else (D, 1)
    operands, specs, aliases = [where, left, right], [smem(), whole, piece(right.shape[0])], {}
    if total is not None:
        operands.append(total)
        specs.append(piece(D))
        if not apart:
            aliases = {3: 0}
    return order(
        functools.partial(chunk_grads_kernel, slab if apart else None, total is not None),
        operands,
        specs,
        (sds((rows, width), F32),) * count,
        [piece(rows)] * count,
        grid=(width // block,),
        input_output_aliases=aliases,
        mib=16,
        name=name,
    )


SPLIT = 1024


def attention_grads_kernel(slab, where_ref, *refs):
    low, dq, (dk_ref, dv_ref), g0, mix = refs[0:3], refs[3:6], refs[6:8], refs[8:11], refs[11:14]
    chunks = lambda ref: [ref.at[start : start + rows] for start, rows in CHUNKS]
    todo = ((low, dq), (low, chunks(dk_ref)), (low, chunks(dv_ref)), (g0, mix))
    for i, (lefts, rights) in enumerate(todo):
        grad = tn_sum(lefts, rights)
        first, last = i * DL, i * DL + DL
        for part, (low_end, high_end) in enumerate(((0, SPLIT), (SPLIT, 4 * DL))):
            begin, end = max(first, low_end), min(last, high_end)
            if begin < end:
                cols = slice(begin - low_end, end - low_end)
                outs = [ref.at[:, cols] for ref in refs[14 + 2 * part : 16 + 2 * part]]
                store_slabs(slab, where_ref[1], grad[:, begin - first : end - first], *outs)


def attention_grads(order, slab, where, enc_low, dq, dk, dv, g0, mix):
    operands = [*enc_low, *dq, dk, dv, *g0, *mix]
    widths = (SPLIT, SPLIT, 4 * DL - SPLIT, 4 * DL - SPLIT)
    return order(
        functools.partial(attention_grads_kernel, slab),
        (where, *operands),
        [smem()] + [vmem()] * len(operands),
        [sds((D // 2, width), F32) for width in widths],
        [vmem()] * 4,
        name="attention_grads",
    )


def plain_grads_kernel(*refs):
    low, dq, (dk_ref, dv_ref), g0, mix = refs[0:3], refs[3:6], refs[6:8], refs[8:11], refs[11:14]
    chunks = lambda ref: [ref.at[start : start + rows] for start, rows in CHUNKS]
    todo = ((low, dq), (low, chunks(dk_ref)), (low, chunks(dv_ref)), (g0, mix))
    for i, (lefts, rights) in enumerate(todo):
        refs[14][:, i * DL : i * DL + DL] = tn_sum(lefts, rights)


def plain_grads(order, enc_low, dq, dk, dv, g0, mix):
    operands = [*enc_low, *dq, dk, dv, *g0, *mix]
    return order(
        plain_grads_kernel, operands, [vmem()] * len(operands), (sds((D, 4 * DL), F32),), [vmem()],
        name="plain_grads",
    )


def halve_kernel(slabs, high, where_bit, count, extra, where_ref, *refs):
    *smalls, a_ref, b_ref, own_ref, out_ref = refs
    mine = where_ref[where_bit]
    total = a_ref.shape[0] - (extra if count == 0 else 0)
    run = high * (total // slabs)
    for i in range(slabs // (2 * high)):
        for ref, which in ((own_ref, mine), (out_ref, 1 - mine)):
            rows = pl.ds(pl.multiple_of((2 * i + which) * run, 8), run)
            ref[i * run : (i + 1) * run, :] = a_ref[rows, :] + b_ref[rows, :]
    if extra == 0:
        return
    width = D
    small = a_ref[total:, 0:width] + b_ref[total:, 0:width] if count == 0 else smalls[0][...]
    for ref in smalls[1:]:
        small = small + ref[...]
    for ref in (own_ref, out_ref):
        ref[total // 2 :, 0:width] = small
        if ref.shape[1] > width:
            rest = (extra, ref.shape[1] - width)
            ref[total // 2 :, width:] = jnp.zeros(rest, F32)


def halve(order, where, pair, slabs, high, where_bit, first, width, name, smalls=(), extra=0):
    rows = pair[0].shape[0]
    total = rows - (0 if smalls else extra)
    if extra == 0:
        block = 512 if width % 512 == 0 and first % 512 == 0 else 384
    else:
        block = width
    at = first // block
    out_rows = total // 2 + extra
    half = pl.BlockSpec((out_rows, block), lambda i: (0, i))
    return order(
        functools.partial(halve_kernel, slabs, high, where_bit, len(smalls), extra),
        [where, *smalls, *pair],
        [smem()]
        + [pl.BlockSpec(a.shape, lambda i: (0, 0)) for a in smalls]
        + [pl.BlockSpec((rows, block), lambda i: (0, at + i))] * 2,
        (sds((out_rows, width), F32),) * 2,
        [half, half],
        grid=(width // block,),
        mib=12,
        name=name,
    )


def norm_back_kernel(
    dres2_ref, own_ref, other_ref, xhat_ref, rstd_ref, vec_ref, wo_ref,
    dres1_far, g0_ref, dmix_ref, sums_ref, dres1_ref, sems,
):
    dhid = dres2_ref[...] + (own_ref[...] + other_ref[...])
    xhat = xhat_ref[...]
    sums_ref[...] = jnp.zeros(sums_ref.shape, F32)
    sums_ref[1:2, :] = col_sum(dhid * xhat)
    sums_ref[2:3, :] = col_sum(dhid)
    dres1 = norm_back(dhid, xhat, rstd_ref[:, 0:1], vec_ref[1:2, :])
    dres1_ref[...] = dres1
    (copy,) = start_all(((dres1_ref, dres1_far),), sems)
    sums_ref[0:1, :] = col_sum(dres1)
    g0 = dres1.astype(BF16)
    g0_ref[...] = g0
    dmix_ref[...] = dot_nt(g0, wo_ref[...]).astype(BF16)
    copy.wait()


def norm_one_back(order, c, dres2, own, other, xhat, rstd, vec, wo):
    _, rows = CHUNKS[c]
    return order(
        norm_back_kernel,
        (dres2, own, other, xhat, rstd, vec, wo),
        [vmem()] * 7,
        (sds((rows, D), F32), sds((rows, D), BF16), sds((rows, DL), BF16), sds((8, D), F32)),
        [hbm()] + [vmem()] * 3,
        scratch_shapes=[pltpu.VMEM((rows, D), F32), pltpu.SemaphoreType.DMA((1,))],
        us=20000 if c == ORDER[0] else 1,
        name=f"norm_back_{c}",
    )


def attend_back_kernel(
    start, rows, first, dmix_ref, p_ref, q_ref, k_ref, v_ref, ur_ref, r_ref, o_ref, *rest,
):
    if not first:
        dk_in, dv_in, dm_in, dz_in = rest[:4]
        rest = rest[4:]
    dq_ref, dk_ref, dv_ref, dm_ref, dz_ref = rest
    if first:
        dz_ref[...] = jnp.zeros(dz_ref.shape, F32)
    else:
        dz_ref[...] = dz_in[...]

    lanes = first_lanes()
    r_w = r_ref[0, start : start + rows, :]
    r_h = r_ref[1, start : start + rows, :]
    upper = (iota((rows, PAIR), 1) >= 64).astype(jnp.int32)
    ur = ur_ref[start : start + rows, :]
    pick = lambda h, a: jnp.where(
        lanes if h % 2 == 0 else jnp.logical_not(lanes), a, jnp.zeros_like(a)
    )
    pair_cols = lambda h: slice(h // 2 * PAIR, h // 2 * PAIR + PAIR)

    def dprob_of(h):
        return dot_nt(pick(h, dmix_ref[:, pair_cols(h)]), v_ref[:, pair_cols(h)])

    def back_of(h, dprob):
        cols = pair_cols(h)
        prob = p_ref[h]
        prob_f = prob.astype(F32)
        both = prob_f * dprob
        ds = both - prob_f * jnp.sum(both, axis=1, keepdims=True)
        low = ds.astype(BF16)
        dq = dot(low, pick(h, k_ref[:, cols]))
        dk = dot_tn(low, pick(h, q_ref[:, cols]))
        dv = dot_tn(prob, pick(h, dmix_ref[:, cols]))
        dbias = dot_nt(low, o_ref[...])
        for at in range(0, rows, SUB):
            size = min(SUB, rows - at)
            sub = (start + at) // SUB
            sums = {}
            for g in range(KEYS // SUB):
                group = min(max(g - sub + 2, 0), 4)
                piece = ds[at : at + size, g * 128 : g * 128 + 128]
                sums[group] = piece if group not in sums else sums[group] + piece
            for group, piece in sums.items():
                dz_ref[h, 0:size, group * 128 : group * 128 + 128] += piece
        return dq, dk, dv, dbias

    def table_of(h, dbias):
        parts = []
        for plane, r_col in ((0, r_w), (1, r_h)):
            same = None
            under = None
            for kk in range(4):
                base = plane * 512 + kk * 128
                piece = dbias[:, base : base + 128]
                ok = (2 * kk + upper) >= r_col
                yes = jnp.where(ok, piece, 0.0)
                no = jnp.where(ok, 0.0, piece)
                same = yes if same is None else same + yes
                under = no if under is None else under + no
            parts += [same, under]
        dm = dot_tn(ur, jnp.concatenate(parts, axis=1).astype(BF16))
        at = slice(h * 512, h * 512 + 512)
        dm_ref[:, at] = dm if first else dm_in[:, at] + dm

    dprob = dprob_of(0)
    totals = None
    for h in range(HL):
        following = dprob_of(h + 1) if h + 1 < HL else None
        dq, dk, dv, dbias = back_of(h, dprob)
        dprob = following
        cols = pair_cols(h)
        if h % 2 == 0:
            totals = (dq, dk, dv)
        else:
            dq_ref[:, cols] = (totals[0] + dq) * 0.125
            dk = totals[1] + dk
            dv = totals[2] + dv
            dk_ref[:, cols] = dk if first else dk_in[:, cols] + dk
            dv_ref[:, cols] = dv if first else dv_in[:, cols] + dv
        table_of(h, dbias)


def attend_back(order, c, dmix, p, q, k, v, ur, r, o, carry, into):
    start, rows = CHUNKS[c]
    operands = [dmix, p, q, k, v, ur, r, o]
    aliases = {}
    if carry is not None:
        operands += list(carry)
        aliases = {8 + i: 1 + i for i in range(4)}
    return order(
        functools.partial(attend_back_kernel, start, rows, carry is None),
        operands,
        [vmem()] * len(operands),
        (
            sds((rows, DL), F32),
            sds((KEYS, DL), F32),
            sds((KEYS, DL), F32),
            sds((128, HL * 512), F32),
            sds((HL, SUB, 640), F32),
        ),
        [vmem()] * 5,
        input_output_aliases=aliases,
        into=into,
        name=f"attend_back_{c}",
    )


def table_sums_kernel(dm_ref, dz_ref, out_ref):
    lane = iota((PAIR, BINS_2D), 0)
    plane_bin = jnp.clip(lane - 64, -32, 31) + 32
    plane_pick = (plane_bin == iota((PAIR, BINS_2D), 1)).astype(F32)
    lane = iota((512, BINS_1D), 0)
    line_bin = jnp.clip(lane - 256, -16, 15) + 16
    line_pick = (line_bin == iota((512, BINS_1D), 1)).astype(F32)
    first = first_lanes()
    flip = (iota((SUB, SUB), 0) + iota((SUB, SUB), 1) == SUB - 1).astype(F32)
    bin_id = iota((1, BINS_1D), 1)
    exact = functools.partial(
        lax.dot_general,
        dimension_numbers=(((1,), (0,)), ((), ())),
        precision=HIGHEST,
        preferred_element_type=F32,
    )
    out_ref[...] = jnp.zeros(out_ref.shape, F32)
    for h in range(HL):
        z = dz_ref[h]
        left = jnp.sum(z[:, 0:128])
        right = jnp.sum(z[:, 512:640])
        band = jnp.concatenate([z[:, 128:512], jnp.zeros((SUB, 128), F32)], axis=1)
        band = pltpu.roll(exact(flip, band), 512 - 127 + 128, 1, stride=1, stride_axis=0)
        line = exact(col_sum(band), line_pick)
        line = line + jnp.where(bin_id == 0, left, 0.0) + jnp.where(bin_id == 31, right, 0.0)
        out_ref[h : h + 1, 0:BINS_1D] = line
        for plane in range(2):
            total = None
            for below in range(2):
                at = h * 512 + plane * 256 + below * 128
                g = dm_ref[plane * 64 : plane * 64 + 64, at : at + 128]
                g = jnp.where(first, g + pltpu.roll(g, 64, 1), 0.0)
                g = pltpu.roll(g, 1 - below, 1, stride=1, stride_axis=0)
                total = g if total is None else total + g
            summed = exact(col_sum(total), plane_pick)
            at = BINS_1D + plane * 64
            out_ref[h : h + 1, at : at + 64] = summed


def table_sums(order, dm, dz):
    return order(
        table_sums_kernel,
        (dm, dz),
        [vmem()] * 2,
        (sds((8, 256), F32),),
        [vmem()],
        name="table_sums",
    )[0]


def project_back_kernel(
    q0, q1, q2, dk_ref, dv_ref, wq_hbm, wk_hbm, wv_hbm, part_ref, bias_ref,
    wq_ref, wk_ref, wv_ref, sems,
):
    copies = [
        pltpu.make_async_copy(src, dst, sems.at[i])
        for i, (src, dst) in enumerate(
            zip((wq_hbm, wk_hbm, wv_hbm), (wq_ref, wk_ref, wv_ref))
        )
    ]
    for copy in copies:
        copy.start()
    sum_q = None
    sum_v = None
    for i, ((start, rows), dq) in enumerate(zip(CHUNKS, (q0, q1, q2))):
        query = dq[...]
        value = dv_ref[start : start + rows, :]
        sum_q = col_sum(query) if sum_q is None else sum_q + col_sum(query)
        sum_v = col_sum(value) if sum_v is None else sum_v + col_sum(value)
        query = query.astype(BF16)
        key = dk_ref[start : start + rows, :].astype(BF16)
        value = value.astype(BF16)
        if i == 0:
            for copy in copies:
                copy.wait()
        part_ref[start : start + rows, :] = (
            dot_nt(query, wq_ref[...]) + dot_nt(key, wk_ref[...]) + dot_nt(value, wv_ref[...])
        )
    bias_ref[...] = jnp.zeros(bias_ref.shape, F32)
    bias_ref[0:1, 0:DL] = sum_q
    bias_ref[0:1, DL:D] = sum_v


def project_back(order, dq, dk, dv, wq, wk, wv):
    return order(
        project_back_kernel,
        (*dq, dk, dv, wq, wk, wv),
        [vmem()] * 5 + [hbm()] * 3,
        (sds((ROWS, D), F32), sds((8, D), F32)),
        [vmem()] * 2,
        scratch_shapes=[pltpu.VMEM((D, DL), BF16)] * 3 + [pltpu.SemaphoreType.DMA((3,))],
        us=15000,
        name="project_back",
    )


def taps_kernel(
    count_ref, x_hbm, pt, r0_far, r1_far, r2_far, out_ref,
    text_scr, patch_scr, raw_scr, x_ref, r0, r1, r2, sems,
):
    count = count_ref[0]
    copies = start_all(((x_hbm, x_ref), (r0_far, r0), (r1_far, r1), (r2_far, r2)), sems)
    copies[0].wait()
    load_page(x_ref, count, text_scr, patch_scr, raw_scr)
    for copy in copies[1:]:
        copy.wait()
    out_ref[...] = jnp.zeros(out_ref.shape, F32)
    shifts = tuple(range(-3, 4))
    for c in range(2):
        cols = slice(c * 384, c * 384 + 384)

        def one(b, sums, cols=cols, res=None, first=0):
            base = pl.multiple_of(b * 32, 32)
            win = text_scr[pl.ds(first + base, 48), cols]
            grad = pt[pl.ds(first + base, 32), cols] + 0.5 * res[pl.ds(base, 32), cols]
            out = []
            for shift, total in zip(shifts, sums):
                prod = grad * win[8 + shift : 40 + shift]
                out.append(total + jnp.sum(prod.reshape(4, 8, 384), axis=0))
            return tuple(out)

        sums = tuple(jnp.zeros((8, 384), F32) for _ in shifts)
        for (first, rows), res in zip(CHUNKS, (r0, r1)):
            sums = lax.fori_loop(
                0, rows // 32, functools.partial(one, res=res, first=first), sums
            )
        for row, total in enumerate(sums):
            out_ref[row : row + 1, cols] = col_sum(total)

    def patches(side):
        live, has_left, has_right = grid_masks(side)
        for c in range(D // PAIR):
            cols = slice(c * PAIR, c * PAIR + PAIR)
            win = patch_scr[:, cols]
            grad = jnp.where(live, pt[TEXT:ROWS, cols] + 0.5 * r2[:, cols], 0.0)
            for ds in (-1, 0, 1):
                masked = grad
                if ds == -1:
                    masked = jnp.where(has_left, grad, 0.0)
                if ds == 1:
                    masked = jnp.where(has_right, grad, 0.0)
                for dr in (-1, 0, 1):
                    row = 7 + 3 * (dr + 1) + ds + 1
                    at = MARGIN + dr * side + ds
                    out_ref[row : row + 1, cols] = col_sum(masked * win[at : at + 208])

    by_grid(count, patches)


def tap_sums(order, count, x, part, res):
    return order(
        taps_kernel,
        (count, x, part, *res),
        [smem(), hbm(), vmem()] + [hbm()] * 3,
        (sds((16, D), F32),),
        [vmem()],
        scratch_shapes=PAGE_SCRATCH
        + [pltpu.VMEM((SEQ, D), BF16)]
        + [pltpu.VMEM((rows, D), F32) for _, rows in CHUNKS]
        + [pltpu.SemaphoreType.DMA((4,))],
        mib=14,
        name="tap_sums",
    )[0]


def decode_text_kernel(text_ref, p, s, r0, r1, out_ref, text_scr):
    zero8 = jnp.zeros((8, D), F32)
    text_scr[0:8, :] = zero8
    text_scr[520:528, :] = zero8
    for r, (at, rows) in zip((r0, r1), CHUNKS):
        for b in range(rows // 64):
            res = r[64 * b : 64 * b + 64, :]
            here = slice(at + 64 * b, at + 64 * b + 64)
            text_scr[8 + at + 64 * b : 72 + at + 64 * b, :] = res + (p[here, :] + s[here, :])
    for c in range(2):
        cols = slice(c * 384, c * 384 + 384)
        taps = text_taps(text_ref, cols)

        def one(b, carry, cols=cols, taps=taps):
            base = pl.multiple_of(b * 32, 32)
            win = text_scr[pl.ds(base, 48), cols]
            out_ref[pl.ds(base, 32), cols] = text_conv_block(win, taps, -1).astype(BF16)
            return carry

        lax.fori_loop(0, TEXT // 32, one, 0)


def decode_kernel(
    count_ref, text_ref, patch_ref, p_far, s_far, r0_far, r1_far, r2_far, out_ref,
    text_scr, patch_scr, raw_scr, p, s, r0, r1, r2, sems,
):
    pairs = ((p_far, p), (s_far, s), (r0_far, r0), (r1_far, r1), (r2_far, r2))
    for copy in start_all(pairs, sems):
        copy.wait()
    decode_text_kernel(text_ref, p, s, r0, r1, out_ref, text_scr)
    count = count_ref[0]
    raw_scr[...] = r2[...] + (p[TEXT:ROWS, :] + s[TEXT:ROWS, :])
    fill_patches(patch_scr, lambda cols: raw_scr[:, cols], count)

    def patches(side):
        for c in range(D // PAIR):
            cols = slice(c * PAIR, c * PAIR + PAIR)
            total = raw_scr[:, cols] + patch_conv_cols(patch_scr[:, cols], patch_ref, cols, side, -1)
            out_ref[TEXT:SEQ, cols] = total[0 : SEQ - TEXT].astype(BF16)

    by_grid(count, patches)


def decode(order, count, text_w, patch_w, part, other, res):
    return order(
        decode_kernel,
        (count, text_w, patch_w, part, other, *res),
        [smem()] + [vmem()] * 2 + [hbm()] * 5,
        (sds((SEQ, D), BF16),),
        whole_blocks((sds((SEQ, D), BF16),)),
        grid=(1,),
        scratch_shapes=PAGE_SCRATCH
        + [pltpu.VMEM((ROWS, D), F32)] * 2
        + [pltpu.VMEM((rows, D), F32) for _, rows in CHUNKS]
        + [pltpu.SemaphoreType.DMA((5,))],
        mib=18,
        name="decode",
    )[0]


def swap_tensor(x):
    return lax.ppermute(x, "tensor", [(0, 1), (1, 0)])


def swap_dp(x, bit, dp):
    return lax.ppermute(x, "dp", [(i, i ^ bit) for i in range(dp)])


def swap_core(parts, dp):
    return (parts[0], swap_dp(parts[1], 1, dp)) if len(parts) == 2 else parts


class Scatter:
    def __init__(self, order, dp, where, pair, bits, name, first, width):
        self.order, self.dp, self.where, self.bits, self.name = order, dp, where, bits, name
        self.window = (first, width)
        self.pair = pair
        self.left = list(range(1, dp.bit_length() - 1))
        self.extra = 0

    def step(self, *smalls):
        if len(self.pair) == 1:
            return
        bit = self.bits[0]
        self.bits = self.bits[1:]
        at = self.left.index(bit)
        if smalls:
            self.extra = smalls[0].shape[0]
        own, out = halve(
            self.order, self.where, self.pair, 2 ** len(self.left), 2**at, 1 + bit, *self.window,
            f"{self.name}_{bit}", smalls, self.extra,
        )
        self.window = (0, self.window[1])
        self.left.remove(bit)
        self.pair = (own, swap_dp(out, 2**bit, self.dp))

    def total(self):
        first, width = self.window
        whole = self.pair[0][:, first : first + width]
        return lax.psum_scatter(whole, "dp", scatter_dimension=0, tiled=True)


def whole_blocks(shapes):
    return [pl.BlockSpec(a.shape, lambda i, n=len(a.shape): (0,) * n) for a in shapes]


EARLY = 8
LATE = 24


def total_of(order, part, name):
    pair = part.pair
    shapes = (sds(pair[0].shape, F32),)
    return order(
        add_kernel, pair, whole_blocks(pair), shapes, whole_blocks(shapes), grid=(1,), name=name
    )[0]


def add_kernel(a, b, out):
    out[...] = a[...] + b[...]


def add_here(order, a, b, name):
    return order(
        add_kernel, (a, b), [vmem()] * 2, (sds(a.shape, F32),), [vmem()], name=name
    )[0]


def last_totals_kernel(
    a0, a1, b0, b1, oa, ob, ia, ib, late, late_other,
    q_ref, k_ref, v_ref, o_ref, outer_ref, inner_ref, small_ref,
):
    slab = q_ref.shape[0]
    both = a0[...] + a1[...]
    q_ref[...] = both[0:slab, 0:DL]
    k_ref[...] = both[0:slab, DL:D]
    v_ref[:, 0 : SPLIT - D] = both[0:slab, D:SPLIT]
    small_ref[0:LATE, :] = late[...] + late_other[...]
    both = b0[...] + b1[...]
    v_ref[:, SPLIT - D : DL] = both[:, 0 : D + DL - SPLIT]
    o_ref[...] = both[:, D + DL - SPLIT :]
    outer_ref[:, 0:D] = oa[0:slab, :]
    outer_ref[:, D:FL] = ob[...]
    inner_ref[:, 0:D] = ia[...]
    inner_ref[:, D:FL] = ib[...]
    small_ref[LATE : LATE + EARLY, :] = oa[slab:, :]


def last_totals(order, part_a, part_b, *rest):
    *rest, slab = rest
    operands = [*part_a.pair, *part_b.pair, *rest]
    plain = sds((slab, DL), F32)
    wide = sds((slab, FL), F32)
    shapes = (plain,) * 4 + (wide, wide, sds((LATE + EARLY, D), F32))
    return order(
        last_totals_kernel, operands, whole_blocks(operands), shapes, whole_blocks(shapes),
        grid=(1,), name="last_totals",
    )


def gather_early_kernel(f0, f1, f2, out):
    sums = f0[...] + f1[...] + f2[...]
    out[...] = jnp.zeros(out.shape, F32)
    out[0:1, :] = sums[0:1, 0:D]
    out[1:2, :] = sums[0:1, D:FL]
    out[2:5, :] = sums[1:4, 0:D]


def gather_early(order, sums, into):
    (early,), moved = order(
        gather_early_kernel, sums, [vmem()] * 3, (sds((EARLY, D), F32),), [vmem()], into=into,
        name="gather_early",
    )
    return early, moved


def gather_late_kernel(taps, a0, a1, a2, bias, tab, out):
    out[...] = jnp.zeros(out.shape, F32)
    out[0:16, :] = taps[0:16, :]
    out[16:19, :] = (a0[...] + a1[...] + a2[...])[0:3]
    out[19:20, :] = bias[0:1, :]
    for h in range(HL):
        at = 256 * (h % 3)
        out[20 + h // 3 : 21 + h // 3, at : at + 256] = tab[h : h + 1, :]


def gather_late(order, *rest):
    return order(
        gather_late_kernel, rest, [vmem()] * 6, (sds((LATE, D), F32),), [vmem()],
        name="gather_late",
    )[0]


def finish_kernel(
    place_ref, own, core, other, both,
    text, patch, out_b, gain1, shift1, outer_b, gain2, shift2,
    query_b, value_b, inner_b, line, width, height,
):
    small = own[...] + core[...]
    slab = patch.shape[1]
    turn = lambda a: pltpu.roll(a, lax.rem(D - place_ref[0] * slab, D), 1)[:, 0:slab]
    shard = turn(small)
    taps = shard[0:16] + turn(other[...] + both[...])
    for dilate in range(3):
        for tap in range(3):
            text[dilate, tap] = taps[3 + (tap - 1) * (dilate + 1)]
    patch[...] = taps[7:16]
    rows = (16, 17, 18, LATE + 2, LATE + 3, LATE + 4)
    for i, ref in zip(rows, (out_b, gain1, shift1, outer_b, gain2, shift2)):
        ref[...] = shard[i]
    query_b[...] = small[19, 0:DL]
    value_b[...] = small[19, DL:D]
    inner_b[0:D] = small[LATE]
    inner_b[D:FL] = small[LATE + 1]
    for h in range(HL):
        row, at = 20 + h // 3, 256 * (h % 3)
        line[h : h + 1, :] = small[row : row + 1, at : at + 32]
        width[h : h + 1, :] = small[row : row + 1, at + 32 : at + 96]
        height[h : h + 1, :] = small[row : row + 1, at + 96 : at + 160]


def finish(order, place, own, core, other, both, slab):
    f = lambda *shape: sds(shape, F32)
    shapes = (f(3, 3, slab), f(9, slab)) + (f(slab),) * 6
    shapes += (f(DL), f(DL), f(FL), f(HL, 32), f(HL, 64), f(HL, 64))
    return order(
        finish_kernel, (place, own, core, other, both),
        [smem()] + whole_blocks((own, core, other, both)), shapes, whole_blocks(shapes), grid=(1,),
        name="finish",
    )


def swap_both(x, dp):
    pairs = [(2 * i + t, 2 * (i ^ 1) + (t ^ 1)) for i in range(dp) for t in range(2)]
    return lax.ppermute(x, ("dp", "tensor"), pairs)


def per_device(
    dp,
    page_tokens,
    patch_counts,
    token_boxes,
    text_weight,
    patch_weight,
    query_weight,
    query_bias,
    key_weight,
    value_weight,
    value_bias,
    out_weight,
    out_bias,
    line_table,
    width_table,
    height_table,
    norm1_gain,
    norm1_shift,
    inner_weight,
    inner_bias,
    outer_weight,
    outer_bias,
    norm2_gain,
    norm2_shift,
    cotangent,
):
    place = lax.axis_index("dp")
    half = lax.axis_index("tensor")
    core = place % 2
    bits = [(place // 2**i) % 2 for i in range(4)]
    where = jnp.stack([half] + bits).astype(jnp.int32)
    x = page_tokens.reshape(SEQ, D)
    cot = cotangent.reshape(SEQ, D)
    slab = D // dp if dp == 16 else None
    order = Order()

    z, m, o, u, r, wo_mine, ur = make_tables(
        order,
        where,
        jnp.concatenate([jnp.transpose(a) for a in (line_table, width_table, height_table)], axis=1),
        token_boxes.reshape(2, SEQ),
        out_weight,
    )
    wo_a = swap_tensor(wo_mine)
    row = lax.broadcasted_iota(jnp.int32, (8, 1), 0)
    bias = jnp.where(row == 0, query_bias[None, :], value_bias[None, :]).astype(F32)
    (q0, q1, q2, k, v), enc, enc_low, (o_far, ur_far, r_far) = encode(
        order, patch_counts, x, text_weight, patch_weight, bias,
        query_weight, key_weight, value_weight, (o, ur, r),
    )
    q = (q0, q1, q2)

    vec = jnp.zeros((8, 1), F32)
    for i, a in enumerate(
        (out_bias, norm1_gain, norm1_shift, outer_bias, norm2_gain, norm2_shift)
    ):
        vec = jnp.where(row == i, a[None, :].astype(F32), vec)
    bi = jnp.broadcast_to(inner_bias[None, :].astype(F32), (8, FL))
    probs, mix, mix_low, mix_other = ([None] * 3 for _ in range(4))
    xhat, rstd, hlow, act, slope, outer, outer_other = ([None] * 3 for _ in range(7))

    def attention_of(c, out):
        (p, a, low), far = attend(order, c, patch_counts, q[c], k, v, u, r, m, o, z, out)
        mix[c], mix_other[c] = a, swap_tensor(a)
        return (p, low), far

    def feed_of(c, out=()):
        got = feed(
            order, c, where, mix[c], mix_other[c], enc[c], vec, out_weight, wo_a, wo_b,
            inner_weight, bi, outer_weight, out,
        )
        far = None
        if out:
            got, far = got
        for keep, a in zip((xhat, rstd, hlow, act, slope, outer), got):
            keep[c] = a
        outer_other[c] = swap_tensor(got[5])
        return far

    near, far = attention_of(ORDER[0], (*enc, *enc_low, q0, q1, q2, k, v))
    enc, enc_low, q_far, k_far, v_far = far[0:3], far[3:6], far[6:9], far[9], far[10]
    wo_a = pass_on(order, wo_a)
    wo_b = swap_dp(wo_a, 1, dp)
    near, (probs[ORDER[0]], mix_low[ORDER[0]]) = attention_of(ORDER[1], near)
    feed_of(ORDER[0])
    near, (probs[ORDER[1]], mix_low[ORDER[1]]) = attention_of(ORDER[2], near)
    probs[ORDER[2]], mix_low[ORDER[2]] = feed_of(ORDER[1], near)
    feed_of(ORDER[2])
    layer_out, inner_grad, outer_grad = None, None, None
    dres2, g2, g1, dhid, dhid_other, sums2 = ([None] * 3 for _ in range(6))
    for c in ORDER:
        got = feed_back(
            order, c, patch_counts, outer[c], outer_other[c], xhat[c], cot, vec, outer_weight,
            slope[c], inner_weight, layer_out,
        )
        layer_out = got[0]
        for keep, a in zip((dres2, g2, g1, dhid, sums2), got[1:]):
            keep[c] = a
        dhid_other[c] = swap_tensor(got[4])
        last = c == ORDER[2]
        inner_grad = chunk_grads(
            order, slab, where, hlow[c], g1[c], inner_grad, last, f"inner_grads_{c}"
        )
        outer_grad = chunk_grads(
            order, slab, where, g2[c], act[c], outer_grad, last, f"outer_grads_{c}"
        )
        if not last:
            inner_grad, outer_grad = inner_grad[0], outer_grad[0]
    scatter = functools.partial(Scatter, order, dp, where)
    x_first, z_first = (1, 2, 3), (2, 3, 1)
    inner_pair, outer_pair = swap_core(inner_grad, dp), swap_core(outer_grad, dp)
    inner = scatter(inner_pair, x_first, "inner", 0, D)
    inner_b = scatter(inner_pair, x_first, "inner_b", D, D)
    outer_a = scatter(outer_pair, x_first, "outer_a", 0, D)
    outer_b = scatter(outer_pair, z_first, "outer_b", D, D)
    early, (prob,) = gather_early(order, sums2, (probs[ORDER[0]],))
    carry = None
    dres1, g0, dq, sums1 = ([None] * 3 for _ in range(4))
    for c in ORDER:
        got = norm_one_back(
            order, c, dres2[c], dhid[c], dhid_other[c], xhat[c], rstd[c], vec, out_weight
        )
        dres1[c], g0[c], _, sums1[c] = got
        if c == ORDER[0]:
            inner.step()
            outer_b.step()
            inner_b.step()
        if c == ORDER[1]:
            outer_a.step(early)
            inner.step()
            outer_b.step()
        if c == ORDER[2]:
            inner_b.step()
            inner.step()
            outer_b.step()
        into = [probs[after] for after in ORDER[ORDER.index(c) + 1 :][:1]]
        got = attend_back(
            order, c, got[2], prob, q_far[c], k_far, v_far, ur_far, r_far, o_far, carry, into
        )
        if into:
            got, (prob,) = got
        dq[c], *carry = got
    dk, dv, dm, dz = carry
    if dp == 16:
        total_outer_b = total_of(order, outer_b, "outer_b_total")
        total_inner = total_of(order, inner, "inner_total")
    outer_a.step()
    inner_b.step()
    operands = (enc_low, dq, dk, dv, g0, mix_low)
    if dp == 16:
        got = attention_grads(order, slab, where, *operands)
        first_pair, second_pair = swap_core(got[0:2], dp), swap_core(got[2:4], dp)
    else:
        first_pair = second_pair = plain_grads(order, *operands)
    rest = 0 if dp == 16 else SPLIT
    part_a = scatter(first_pair, x_first, "part_a", 0, SPLIT)
    part_b = scatter(second_pair, z_first, "part_b", rest, 4 * DL - SPLIT)
    part, bias_sums = project_back(order, dq, dk, dv, query_weight, key_weight, value_weight)
    part_other = swap_tensor(part)
    part_a.step()
    part_b.step()
    tables = table_sums(order, dm, dz)
    taps = tap_sums(order, patch_counts, x, part, dres1)
    late = gather_late(order, taps, *sums1, bias_sums, tables)
    late_other = swap_dp(late, 2, dp)
    outer_a.step()
    if dp == 16:
        total_inner_b = total_of(order, inner_b, "inner_b_total")
    part_b.step()
    part_a.step()
    if dp == 16:
        late = add_here(order, late, late_other, "late_2")
        late_other = swap_dp(late, 4, dp)
    part_a.step()
    part_b.step()
    if dp == 16:
        late = add_here(order, late, late_other, "late_4")
        late_other = swap_dp(late, 8, dp)
    input_grad = decode(order, patch_counts, text_weight, patch_weight, part, part_other, dres1)
    if dp == 16:
        total_outer_a = total_of(order, outer_a, "outer_a_total")
        grad_q, grad_k, grad_v, grad_o, sum_outer, inner_total, small = last_totals(
            order, part_a, part_b, total_outer_a, total_outer_b, total_inner, total_inner_b,
            late, late_other, slab,
        )
    else:
        inner_total = jnp.concatenate([inner.total(), inner_b.total()], axis=1)
        sum_outer = jnp.concatenate([outer_a.total(), outer_b.total()], axis=1)
        both = jnp.concatenate([part_a.total(), part_b.total()], axis=1)
        grad_q, grad_k, grad_v, grad_o = jnp.split(both, 4, axis=1)
        small = jnp.concatenate([late, early], axis=0)
        bit = 2
        while bit < dp:
            small = small + swap_dp(small, bit, dp)
            bit *= 2
    small = finish(
        order, jnp.reshape(place, (1,)).astype(jnp.int32), small, swap_dp(small, 1, dp),
        swap_tensor(small[0:16]), swap_both(small[0:16], dp), D // dp,
    )
    text, patch, out_b, gain1, shift1, outer_b, gain2, shift2 = small[:8]
    query_b, value_b, inner_b, line, width, height = small[8:]
    return (
        layer_out.reshape(1, SEQ, D),
        input_grad.reshape(1, SEQ, D),
        text,
        patch,
        grad_q,
        query_b,
        grad_k,
        grad_v,
        value_b,
        jnp.transpose(grad_o),
        out_b,
        jnp.transpose(line),
        jnp.transpose(width),
        jnp.transpose(height),
        gain1,
        shift1,
        inner_total,
        inner_b,
        jnp.transpose(sum_outer),
        outer_b,
        gain2,
        shift2,
    )


def solution(mesh):
    placed = (
        P("dp", None, None),
        P("dp"),
        P("dp", None, None),
        P(),
        P(),
        P(None, "tensor"),
        P("tensor"),
        P(None, "tensor"),
        P(None, "tensor"),
        P("tensor"),
        P("tensor", None),
        P(),
        P(None, "tensor"),
        P(None, "tensor"),
        P(None, "tensor"),
        P(),
        P(),
        P(None, "tensor"),
        P("tensor"),
        P("tensor", None),
        P(),
        P(),
        P(),
        P("dp", None, None),
    )
    return jax.shard_map(
        functools.partial(per_device, mesh.shape["dp"]),
        mesh=mesh,
        in_specs=placed,
        out_specs=(
            P("dp", None, None),
            P("dp", None, None),
            P(None, None, "dp"),
            P(None, "dp"),
            P("dp", "tensor"),
            P("tensor"),
            P("dp", "tensor"),
            P("dp", "tensor"),
            P("tensor"),
            P("tensor", "dp"),
            P("dp"),
            P(None, "tensor"),
            P(None, "tensor"),
            P(None, "tensor"),
            P("dp"),
            P("dp"),
            P("dp", "tensor"),
            P("tensor"),
            P("tensor", "dp"),
            P("dp"),
            P("dp"),
            P("dp"),
        ),
        check_vma=False,
    )
```

```python
import functools

import jax
import jax.numpy as jnp
from jax import lax
from jax.experimental import pallas as pl
from jax.experimental.pallas import tpu as pltpu
from jax.sharding import PartitionSpec as P

HEADS = 12
TEXT = 512
GRID_SMALL = 7
GRID_LARGE = 14
BINS_1D = 32
BINS_2D = 64
BIN_WIDTH = 8

F32 = jnp.float32
BF16 = jnp.bfloat16
EPS = 1e-05
NEG = -1000000000.0
HIGHEST = lax.Precision.HIGHEST

D = 768
SEQ = 708
ROWS = 720
KEYS = 768
CHUNKS = ((0, 256), (256, 256), (512, 208))
ORDER = (2, 0, 1)
SUB = 128
PAIR = 128
HL = 6
DL = 384
FL = 1536
MARGIN = 16
MIB = 1024 * 1024


def vmem():
    return pl.BlockSpec(memory_space=pltpu.VMEM)


def anywhere():
    return pl.BlockSpec(memory_space=pl.ANY)


def hbm():
    return pl.BlockSpec(memory_space=pltpu.HBM)


def smem():
    return pl.BlockSpec(memory_space=pltpu.SMEM)


def params(mib):
    return pltpu.CompilerParams(vmem_limit_bytes=mib * MIB)


def sds(shape, dtype):
    return jax.ShapeDtypeStruct(shape, dtype)


TOKEN = jax.ShapeDtypeStruct((8, 128), jnp.float32)


class Order:
    def __init__(self):
        self.token = None

    def __call__(
        self, kernel, operands, in_specs, out_shape, out_specs, mib=10, us=1, out=(), into=(),
        scratch_shapes=(), **more,
    ):
        operands, in_specs = list(operands), list(in_specs)
        count, outs, moved = len(operands), len(out_shape), len(out) + len(into)
        operands += [*out, *into]
        in_specs += [vmem()] * len(out) + [hbm()] * len(into)
        has_token = self.token is not None
        grid = "grid" in more
        token_spec = pl.BlockSpec(TOKEN.shape, lambda *i: (0, 0)) if grid else vmem()
        if has_token:
            operands.append(self.token)
            in_specs.append(token_spec)
        shapes = [sds(a.shape, a.dtype) for a in (*out, *into)]
        specs = [hbm()] * len(out) + [vmem()] * len(into)
        scratch_shapes = list(scratch_shapes)
        if moved:
            scratch_shapes.append(pltpu.SemaphoreType.DMA((moved,)))

        def body(*refs):
            rest = list(refs)
            sources = rest[count : count + moved]
            del rest[count : count + moved + has_token]
            at = count + outs
            targets = rest[at : at + moved]
            rest[at + moved][...] = jnp.zeros(TOKEN.shape, F32)
            del rest[at : at + moved + 1]
            copies = start_all(zip(sources, targets), rest.pop()) if moved else []
            kernel(*rest)
            for copy in copies:
                copy.wait()

        got = pl.pallas_call(
            body,
            out_shape=tuple(out_shape) + tuple(shapes) + (TOKEN,),
            in_specs=in_specs,
            out_specs=tuple(out_specs) + tuple(specs) + (token_spec,),
            scratch_shapes=scratch_shapes,
            compiler_params=params(mib),
            cost_estimate=cost(us),
            **more,
        )(*operands)
        self.token = got[-1]
        if moved:
            return got[:outs], got[outs:-1]
        return got[:-1]


def start_all(pairs, sems, first=0):
    copies = [
        pltpu.make_async_copy(src, dst, sems.at[first + i]) for i, (src, dst) in enumerate(pairs)
    ]
    for copy in copies:
        copy.start()
    return copies


def dot(a, b):
    return lax.dot_general(a, b, (((1,), (0,)), ((), ())), preferred_element_type=F32)


def dot_nt(a, b):
    return lax.dot_general(a, b, (((1,), (1,)), ((), ())), preferred_element_type=F32)


def dot_tn(a, b):
    return lax.dot_general(a, b, (((0,), (0,)), ((), ())), preferred_element_type=F32)


def cost(us):
    return pl.CostEstimate(flops=int(us * 1.0e6), bytes_accessed=int(us * 1.0e3), transcendentals=0)


def iota(shape, dim):
    return lax.broadcasted_iota(jnp.int32, shape, dim)


def first_lanes():
    return iota((1, PAIR), 1) < 64


def tables_kernel(
    where_ref, tab_ref, boxes_hbm, wo_hbm,
    z_ref, m_ref, o_ref, u_ref, r_ref, mine_ref, ur_ref,
    box_scr, boxes_ref, wo_ref, sems,
):
    half = DL // 2
    rows = pl.ds(pl.multiple_of(where_ref[1] * half, half), half)
    copies = start_all(
        (
            (boxes_hbm, boxes_ref),
            (wo_hbm.at[rows, :], wo_ref),
        ),
        sems,
    )
    for copy in copies:
        copy.wait()
    mine_ref[...] = wo_ref[...].astype(F32)
    lane = iota((BINS_1D, 768), 1)
    bucket = jnp.where(lane < 640, jnp.clip(lane - 256, -16, 15) + 16, 0)
    line_pick = (bucket == iota((BINS_1D, 768), 0)).astype(BF16)
    line_base = dot(tab_ref[:, 0:BINS_1D], line_pick)
    lane = iota((BINS_2D, PAIR), 1)
    bucket = jnp.clip(lane - 64, -32, 31) + 32
    plane_pick = (bucket == iota((BINS_2D, PAIR), 0)).astype(BF16)
    bases = [
        dot(tab_ref[:, BINS_1D + 64 * plane : BINS_1D + 64 * plane + 64], plane_pick)
        for plane in range(2)
    ]
    first = first_lanes()
    zeros = jnp.zeros((64, PAIR), BF16)
    for h in range(HL):
        spread = jnp.broadcast_to(line_base[h : h + 1, :], (SUB, 768))
        rolled = pltpu.roll(spread, 0, 1, stride=1, stride_axis=0)
        z_ref[h] = rolled[:, :640]
        for plane in range(2):
            spread = jnp.broadcast_to(bases[plane][h : h + 1, :], (64, PAIR))
            for below in range(2):
                one = pltpu.roll(spread, 64 + below, 1, stride=1, stride_axis=0)
                both = jnp.where(first, one, pltpu.roll(one, 64, 1)).astype(BF16)
                start = h * 512 + plane * 256 + below * 128
                m_ref[plane * 64 : plane * 64 + 64, start : start + 128] = both
                m_ref[64 - plane * 64 : 128 - plane * 64, start : start + 128] = zeros
    box_scr[...] = jnp.full((8, KEYS), -1, jnp.int32)
    box_scr[0:2, 0:SEQ] = boxes_ref[...]
    row = iota((512, KEYS), 0)
    value = 8 * (row % 64) + row // 64
    for plane in range(2):
        o_ref[plane * 512 : plane * 512 + 512, :] = (
            value == box_scr[plane : plane + 1, :]
        ).astype(F32).astype(BF16)
    turned = jnp.transpose(box_scr[...].astype(F32))[0:ROWS, :].astype(jnp.int32)
    left = jnp.broadcast_to(turned[:, 0:1], (ROWS, PAIR))
    right = jnp.broadcast_to(turned[:, 1:2], (ROWS, PAIR))
    lane = iota((ROWS, PAIR), 1)
    both = jnp.where(lane < 64, left, right)
    r_ref[0] = left & 7
    r_ref[1] = right & 7
    upper = lax.shift_right_logical(both, 3)
    inner = lane & 63
    u_ref[...] = (upper == inner).astype(F32).astype(BF16)
    ur_ref[...] = (63 - upper == inner).astype(F32).astype(BF16)


def make_tables(order, where, tab, boxes, wo):
    return order(
        tables_kernel,
        (where, tab, boxes, wo),
        [smem(), vmem()] + [hbm()] * 2,
        (
            sds((HL, SUB, 640), F32),
            sds((128, HL * 512), BF16),
            sds((1024, KEYS), BF16),
            sds((ROWS, PAIR), BF16),
            sds((2, ROWS, PAIR), jnp.int32),
            sds((DL // 2, D), F32),
            sds((ROWS, PAIR), BF16),
        ),
        [vmem()] * 7,
        us=20000,
        scratch_shapes=[
            pltpu.VMEM((8, KEYS), jnp.int32),
            pltpu.VMEM(boxes.shape, jnp.int32),
            pltpu.VMEM((DL // 2, D), BF16),
            pltpu.SemaphoreType.DMA((2,)),
        ],
        name="bias_tables",
    )


def copy_kernel(src, dst, scr, sems):
    for pair in ((src, scr), (scr, dst)):
        copy = pltpu.make_async_copy(*pair, sems.at[0])
        copy.start()
        copy.wait()


def pass_on(order, x):
    return order(
        copy_kernel,
        (x,),
        [anywhere()],
        (sds(x.shape, x.dtype),),
        [anywhere()],
        scratch_shapes=[pltpu.VMEM(x.shape, x.dtype), pltpu.SemaphoreType.DMA((1,))],
        name="pass_on",
    )[0]


def text_taps(text_ref, cols):
    taps = {}
    for dilate in range(3):
        for tap in range(3):
            shift = (tap - 1) * (dilate + 1)
            row = text_ref[dilate, tap : tap + 1, cols].astype(F32)
            taps[shift] = row if shift not in taps else taps[shift] + row
    return taps


def text_conv_block(win, taps, sign):
    total = win[8:40] * (taps[0] + 1.0)
    for shift in (-3, -2, -1, 1, 2, 3):
        start = 8 + sign * shift
        total = total + win[start : start + 32] * taps[shift]
    return total


def grid_masks(side):
    place = iota((208, PAIR), 0)
    row = jnp.floor((place.astype(F32) + 0.5) * (1.0 / side)).astype(jnp.int32)
    col = place - row * side
    return (place < side * side, col >= 1, col <= side - 2)


def patch_conv_cols(win, patch_ref, cols, side, sign):
    live, has_left, has_right = grid_masks(side)
    total = None
    for ds in (-1, 0, 1):
        part = None
        for dr in (-1, 0, 1):
            tap = 3 * (dr + 1) + ds + 1
            start = MARGIN + sign * (dr * side + ds)
            term = win[start : start + 208] * patch_ref[tap : tap + 1, cols].astype(F32)
            part = term if part is None else part + term
        if ds * sign == -1:
            part = jnp.where(has_left, part, 0.0)
        if ds * sign == 1:
            part = jnp.where(has_right, part, 0.0)
        total = part if total is None else total + part
    return jnp.where(live, total, 0.0)


def fill_patches(patch_scr, source, count):
    zero = jnp.zeros((MARGIN, D), F32)
    patch_scr[0:MARGIN, :] = zero
    patch_scr[MARGIN + 208 : MARGIN + 208 + MARGIN, :] = zero
    live = iota((208, PAIR), 0) < count
    for c in range(D // PAIR):
        cols = slice(c * PAIR, c * PAIR + PAIR)
        patch_scr[MARGIN : MARGIN + 208, cols] = jnp.where(live, source(cols), 0.0)


def load_page(x_ref, count, text_scr, patch_scr, raw_scr):
    zero8 = jnp.zeros((8, D), F32)
    text_scr[0:8, :] = zero8
    text_scr[520:528, :] = zero8
    for b in range(TEXT // 64):
        text_scr[8 + 64 * b : 72 + 64 * b, :] = x_ref[64 * b : 64 * b + 64, :].astype(F32)
    raw_scr[...] = jnp.zeros((208, D), F32)
    raw_scr[0 : SEQ - TEXT, :] = x_ref[TEXT:SEQ, :].astype(F32)
    fill_patches(patch_scr, lambda cols: raw_scr[:, cols], count)


PAGE_SCRATCH = [
    pltpu.VMEM((528, D), F32),
    pltpu.VMEM((208 + 2 * MARGIN, D), F32),
    pltpu.VMEM((208, D), F32),
]


def by_grid(count, patches):
    large = count == GRID_LARGE * GRID_LARGE

    @pl.when(large)
    def _():
        patches(GRID_LARGE)

    @pl.when(jnp.logical_not(large))
    def _():
        patches(GRID_SMALL)


def encode_kernel(
    count_ref, x_hbm, text_ref, patch_ref, bias_ref, wq_hbm, wk_hbm, wv_hbm,
    q0, q1, q2, k_ref, v_ref, e0, e1, e2, l0, l1, l2,
    text_scr, patch_scr, raw_scr, x_ref, wq_ref, wk_ref, wv_ref, sems,
):
    copies = start_all(
        ((x_hbm, x_ref), (wq_hbm, wq_ref), (wk_hbm, wk_ref), (wv_hbm, wv_ref)), sems
    )
    count = count_ref[0]
    copies[0].wait()
    load_page(x_ref, count, text_scr, patch_scr, raw_scr)

    for c in range(2):
        cols = slice(c * 384, c * 384 + 384)
        taps = text_taps(text_ref, cols)

        def one(b, carry, cols=cols, taps=taps, out=None, first=0):
            base = pl.multiple_of(b * 32, 32)
            win = text_scr[pl.ds(first + base, 48), cols]
            out[pl.ds(base, 32), cols] = text_conv_block(win, taps, 1)
            return carry

        for (first, rows), out in zip(CHUNKS, (e0, e1)):
            lax.fori_loop(0, rows // 32, functools.partial(one, out=out, first=first), 0)

    def patches(side):
        for c in range(D // PAIR):
            cols = slice(c * PAIR, c * PAIR + PAIR)
            e2[:, cols] = raw_scr[:, cols] + patch_conv_cols(
                patch_scr[:, cols], patch_ref, cols, side, 1
            )

    by_grid(count, patches)
    for copy in copies[1:]:
        copy.wait()
    for (start, rows), e, low, q in zip(CHUNKS, (e0, e1, e2), (l0, l1, l2), (q0, q1, q2)):
        enc = e[...].astype(BF16)
        low[...] = enc
        query = (dot(enc, wq_ref[...]) + bias_ref[0:1, :]).astype(BF16)
        q[...] = query * jnp.asarray(0.125, BF16)
        k_ref[start : start + rows, :] = dot(enc, wk_ref[...]).astype(BF16)
        value = dot(enc, wv_ref[...]) + bias_ref[1:2, :]
        v_ref[start : start + rows, :] = value.astype(BF16)
    k_ref[ROWS:KEYS, :] = jnp.zeros((KEYS - ROWS, DL), BF16)
    v_ref[ROWS:KEYS, :] = jnp.zeros((KEYS - ROWS, DL), BF16)


def encode(order, count, x, text, patch, bias, wq, wk, wv, out):
    chunk = lambda width, dtype: tuple(sds((rows, width), dtype) for _, rows in CHUNKS)
    keys = (sds((KEYS, DL), BF16), sds((KEYS, DL), BF16))
    got, far = order(
        encode_kernel,
        (count, x, text, patch, bias, wq, wk, wv),
        [smem(), hbm()] + [vmem()] * 3 + [hbm()] * 3,
        chunk(DL, BF16) + keys + chunk(D, F32) + chunk(D, BF16),
        [vmem()] * 11,
        scratch_shapes=PAGE_SCRATCH
        + [pltpu.VMEM((SEQ, D), BF16)]
        + [pltpu.VMEM((D, DL), BF16)] * 3
        + [pltpu.SemaphoreType.DMA((4,))],
        mib=12,
        us=8000,
        out=out,
        name="encode_project",
    )
    return got[0:5], got[5:8], got[8:11], far


def bias_rows(e, r_col, k, rows):
    step = 2 * k + (iota((rows, PAIR), 1) >= 64).astype(jnp.int32)
    return jnp.where(step >= r_col, e[0], e[1]).astype(BF16)


def line_rows(z_ref, h, sub, rows):
    groups = [min(max(g - sub + 2, 0), 4) for g in range(KEYS // SUB)]
    return jnp.concatenate([z_ref[h, 0:rows, g * 128 : g * 128 + 128] for g in groups], axis=1)


def attend_kernel(
    start, rows, count_ref, q_ref, k_ref, v_ref, u_ref, r_ref, m_ref, o_ref, z_ref,
    p_ref, mix_ref, low_ref,
):
    live = iota((1, KEYS), 1) < TEXT + count_ref[0]
    first = first_lanes()
    r_w = r_ref[0, start : start + rows, :]
    r_h = r_ref[1, start : start + rows, :]
    u = u_ref[start : start + rows, :]
    for pair in range(HL // 2):
        cols = slice(pair * PAIR, pair * PAIR + PAIR)
        q = q_ref[:, cols]
        k = k_ref[:, cols]
        v = v_ref[:, cols]
        mixed = []
        for half in range(2):
            h = 2 * pair + half
            mine = first if half == 0 else jnp.logical_not(first)
            qm = jnp.where(mine, q, jnp.zeros_like(q))
            e = dot(u, m_ref[:, h * 512 : h * 512 + 512])
            parts = [bias_rows((e[:, 0:128], e[:, 128:256]), r_w, kk, rows) for kk in range(4)]
            parts += [bias_rows((e[:, 256:384], e[:, 384:512]), r_h, kk, rows) for kk in range(4)]
            picked = jnp.concatenate(parts, axis=1)
            s = dot(picked, o_ref[...]) + dot_nt(qm, k)
            pieces = []
            for at in range(0, rows, SUB):
                size = min(SUB, rows - at)
                pieces.append(line_rows(z_ref, h, (start + at) // SUB, size))
            s = s + jnp.concatenate(pieces, axis=0)
            s = jnp.where(live, s, NEG)
            top = jnp.max(s, axis=1, keepdims=True)
            ex = jnp.exp(s - top)
            total = jnp.sum(ex, axis=1, keepdims=True)
            prob = (ex * (1.0 / total)).astype(BF16)
            p_ref[h] = prob
            mixed.append(dot(prob, v))
        low = jnp.where(first, mixed[0], mixed[1]).astype(BF16)
        low_ref[:, cols] = low
        mix_ref[:, cols] = low.astype(F32)


def attend(order, c, count, q, k, v, u, r, m, o, z, out):
    start, rows = CHUNKS[c]
    return order(
        functools.partial(attend_kernel, start, rows),
        (count, q, k, v, u, r, m, o, z),
        [smem()] + [vmem()] * 8,
        (sds((HL, rows, KEYS), BF16), sds((rows, DL), F32), sds((rows, DL), BF16)),
        [vmem()] * 3,
        out=out,
        name=f"attend_{c}",
    )


def feed_kernel(
    where_ref, own_ref, other_ref, enc_hbm, vec_ref, wo_ref, wo_a_ref, wo_b_ref, wi_ref, bi_ref,
    w2_ref, xhat_ref, rstd_ref, hlow_ref, act_ref, slope_ref, part_ref, enc_ref, sems,
):
    (copy,) = start_all(((enc_hbm, enc_ref),), sems)
    half = where_ref[0]
    core = where_ref[1]
    own = dot(own_ref[...].astype(BF16), wo_ref[...])
    other = other_ref[...].astype(BF16)
    low = jnp.where(core == 0, wo_a_ref[...], wo_b_ref[...]).astype(BF16)
    high = jnp.where(core == 0, wo_b_ref[...], wo_a_ref[...]).astype(BF16)
    other = dot(other, jnp.concatenate([low, high], axis=0))
    attended = jnp.where(half == 0, own, other) + jnp.where(half == 0, other, own)
    copy.wait()
    v = enc_ref[...] + (attended + vec_ref[0:1, :])
    centre = v - jnp.mean(v, axis=1, keepdims=True)
    rstd = lax.rsqrt(jnp.mean(centre * centre, axis=1, keepdims=True) + EPS)
    xhat = centre * rstd
    xhat_ref[...] = xhat
    rstd_ref[...] = jnp.broadcast_to(rstd, rstd_ref.shape)
    hlow = (xhat * vec_ref[1:2, :] + vec_ref[2:3, :]).astype(BF16)
    hlow_ref[...] = hlow
    total = None
    for n in range(FL // 512):
        cols = slice(n * 512, n * 512 + 512)
        pre = dot(hlow, wi_ref[:, cols]) + bi_ref[0:1, cols]
        gate = 0.5 + 0.5 * lax.erf(pre * 0.7071067811865476)
        slope_ref[:, cols] = gate + pre * (0.3989422804014327 * jnp.exp(-0.5 * pre * pre))
        act = (pre * gate).astype(BF16)
        act_ref[:, cols] = act
        term = dot(act, w2_ref[cols, :])
        total = term if total is None else total + term
    part_ref[...] = total


def feed(order, c, where, own, other, enc, vec, wo, wo_a, wo_b, wi, bi, w2, out):
    _, rows = CHUNKS[c]
    return order(
        feed_kernel,
        (where, own, other, enc, vec, wo, wo_a, wo_b, wi, bi, w2),
        [smem()] + [vmem()] * 2 + [hbm()] + [vmem()] * 7,
        (
            sds((rows, D), F32),
            sds((rows, 128), F32),
            sds((rows, D), BF16),
            sds((rows, FL), BF16),
            sds((rows, FL), F32),
            sds((rows, D), F32),
        ),
        [vmem()] * 6,
        scratch_shapes=[pltpu.VMEM((rows, D), F32), pltpu.SemaphoreType.DMA((1,))],
        out=out,
        name=f"feed_{c}",
    )


def norm_back(dy, xhat, rstd, gain):
    dxh = dy * gain
    return rstd * (
        dxh
        - jnp.mean(dxh, axis=1, keepdims=True)
        - xhat * jnp.mean(dxh * xhat, axis=1, keepdims=True)
    )


def col_sum(x):
    return jnp.sum(x, axis=0, keepdims=True)


def feed_back_kernel(
    start, rows, first, count_ref, own_ref, other_ref, xhat1_ref, cot_ref, vec_ref, w2_ref,
    slope_ref, wi_ref, *rest,
):
    if not first:
        rest = rest[1:]
    out_ref, dres_ref, g2_ref, g1_ref, part_ref, sums_ref = rest
    place = start + iota((rows, 1), 0)
    live = place < TEXT + count_ref[0]
    hidden = xhat1_ref[...] * vec_ref[1:2, :] + vec_ref[2:3, :]
    v = hidden + ((own_ref[...] + other_ref[...]) + vec_ref[3:4, :])
    centre = v - jnp.mean(v, axis=1, keepdims=True)
    rstd = lax.rsqrt(jnp.mean(centre * centre, axis=1, keepdims=True) + EPS)
    xhat = centre * rstd
    y = xhat * vec_ref[4:5, :] + vec_ref[5:6, :]
    out_ref[0:rows, :] = jnp.where(live, y, 0.0).astype(BF16)
    dy = jnp.where(live, cot_ref[0:rows, :].astype(F32), 0.0)
    sums_ref[...] = jnp.zeros(sums_ref.shape, F32)
    sums_ref[2:3, 0:D] = col_sum(dy * xhat)
    sums_ref[3:4, 0:D] = col_sum(dy)
    dres = norm_back(dy, xhat, rstd, vec_ref[4:5, :])
    dres_ref[...] = dres
    sums_ref[1:2, 0:D] = col_sum(dres)
    g2 = dres.astype(BF16)
    g2_ref[...] = g2
    total = None
    for n in range(FL // 512):
        cols = slice(n * 512, n * 512 + 512)
        d_inner = dot_nt(g2, w2_ref[cols, :]) * slope_ref[:, cols]
        sums_ref[0:1, cols] = col_sum(d_inner)
        g1 = d_inner.astype(BF16)
        g1_ref[:, cols] = g1
        term = dot_nt(g1, wi_ref[:, cols])
        total = term if total is None else total + term
    part_ref[...] = total


def feed_back(order, c, count, own, other, xhat1, cot, vec, w2, slope, wi, out_so_far):
    start, rows = CHUNKS[c]
    high = 256 if start == TEXT else rows
    block = pl.BlockSpec((high, D), lambda i: (start // high, 0))
    whole = lambda a: pl.BlockSpec(a.shape, lambda i: (0, 0))
    shapes = (
        sds((SEQ, D), BF16),
        sds((rows, D), F32),
        sds((rows, D), BF16),
        sds((rows, FL), BF16),
        sds((rows, D), F32),
        sds((8, FL), F32),
    )
    operands = [count, own, other, xhat1, cot, vec, w2, slope, wi]
    specs = [smem()] + [vmem()] * 3 + [block] + [vmem()] * 4
    aliases = {}
    if out_so_far is not None:
        operands.append(out_so_far)
        specs.append(anywhere())
        aliases = {9: 0}
    return order(
        functools.partial(feed_back_kernel, start, rows, out_so_far is None),
        operands,
        specs,
        shapes,
        [block] + [vmem()] * 5,
        grid=(1,),
        input_output_aliases=aliases,
        name=f"feed_back_{c}",
    )


def store_slabs(slab, core, grad, keep_ref, send_ref):
    for i in range(D // (2 * slab)):
        even = grad[2 * i * slab : (2 * i + 1) * slab]
        odd = grad[(2 * i + 1) * slab : (2 * i + 2) * slab]
        keep_ref[i * slab : (i + 1) * slab, :] = jnp.where(core == 0, even, odd)
        send_ref[i * slab : (i + 1) * slab, :] = jnp.where(core == 0, odd, even)


def tn_sum(lefts, rights):
    total = None
    for left, right in zip(lefts, rights):
        term = dot_tn(left[...], right[...].astype(BF16))
        total = term if total is None else total + term
    return total


def put_grads(slab, where_ref, grad, outs):
    if slab is None:
        outs[0][...] = grad
    else:
        store_slabs(slab, where_ref[1], grad, *outs)


def chunk_grads_kernel(slab, has_total, where_ref, left_ref, right_ref, *refs):
    grad = dot_tn(left_ref[...], right_ref[...])
    if has_total:
        grad = refs[0][...] + grad
    put_grads(slab, where_ref, grad, refs[has_total:])


def chunk_grads(order, slab, where, left, right, total, last, name):
    width = right.shape[1]
    block = 512
    piece = lambda rows: pl.BlockSpec((rows, block), lambda i: (0, i))
    whole = pl.BlockSpec(left.shape, lambda i: (0, 0))
    apart = last and slab is not None
    rows, count = (D // 2, 2) if apart else (D, 1)
    operands, specs, aliases = [where, left, right], [smem(), whole, piece(right.shape[0])], {}
    if total is not None:
        operands.append(total)
        specs.append(piece(D))
        if not apart:
            aliases = {3: 0}
    return order(
        functools.partial(chunk_grads_kernel, slab if apart else None, total is not None),
        operands,
        specs,
        (sds((rows, width), F32),) * count,
        [piece(rows)] * count,
        grid=(width // block,),
        input_output_aliases=aliases,
        mib=16,
        name=name,
    )


SPLIT = 768


def attention_grads_kernel(slab, where_ref, *refs):
    low, dq, (dk_ref, dv_ref), g0, mix = refs[0:3], refs[3:6], refs[6:8], refs[8:11], refs[11:14]
    chunks = lambda ref: [ref.at[start : start + rows] for start, rows in CHUNKS]
    todo = ((low, dq), (low, chunks(dk_ref)), (low, chunks(dv_ref)), (g0, mix))
    for i, (lefts, rights) in enumerate(todo):
        grad = tn_sum(lefts, rights)
        first, last = i * DL, i * DL + DL
        for part, (low_end, high_end) in enumerate(((0, SPLIT), (SPLIT, 4 * DL))):
            begin, end = max(first, low_end), min(last, high_end)
            if begin < end:
                cols = slice(begin - low_end, end - low_end)
                outs = [ref.at[:, cols] for ref in refs[14 + 2 * part : 16 + 2 * part]]
                store_slabs(slab, where_ref[1], grad[:, begin - first : end - first], *outs)


def attention_grads(order, slab, where, enc_low, dq, dk, dv, g0, mix):
    operands = [*enc_low, *dq, dk, dv, *g0, *mix]
    widths = (SPLIT, SPLIT, 4 * DL - SPLIT, 4 * DL - SPLIT)
    return order(
        functools.partial(attention_grads_kernel, slab),
        (where, *operands),
        [smem()] + [vmem()] * len(operands),
        [sds((D // 2, width), F32) for width in widths],
        [vmem()] * 4,
        name="attention_grads",
    )


def plain_grads_kernel(*refs):
    low, dq, (dk_ref, dv_ref), g0, mix = refs[0:3], refs[3:6], refs[6:8], refs[8:11], refs[11:14]
    chunks = lambda ref: [ref.at[start : start + rows] for start, rows in CHUNKS]
    todo = ((low, dq), (low, chunks(dk_ref)), (low, chunks(dv_ref)), (g0, mix))
    for i, (lefts, rights) in enumerate(todo):
        refs[14][:, i * DL : i * DL + DL] = tn_sum(lefts, rights)


def plain_grads(order, enc_low, dq, dk, dv, g0, mix):
    operands = [*enc_low, *dq, dk, dv, *g0, *mix]
    return order(
        plain_grads_kernel, operands, [vmem()] * len(operands), (sds((D, 4 * DL), F32),), [vmem()],
        name="plain_grads",
    )


def halve_kernel(slabs, high, where_bit, count, extra, where_ref, *refs):
    *smalls, a_ref, b_ref, own_ref, out_ref = refs
    mine = where_ref[where_bit]
    total = a_ref.shape[0] - (extra if count == 0 else 0)
    run = high * (total // slabs)
    for i in range(slabs // (2 * high)):
        for ref, which in ((own_ref, mine), (out_ref, 1 - mine)):
            rows = pl.ds(pl.multiple_of((2 * i + which) * run, 8), run)
            ref[i * run : (i + 1) * run, :] = a_ref[rows, :] + b_ref[rows, :]
    if extra == 0:
        return
    width = D
    small = a_ref[total:, 0:width] + b_ref[total:, 0:width] if count == 0 else smalls[0][...]
    for ref in smalls[1:]:
        small = small + ref[...]
    for ref in (own_ref, out_ref):
        ref[total // 2 :, 0:width] = small
        if ref.shape[1] > width:
            rest = (extra, ref.shape[1] - width)
            ref[total // 2 :, width:] = jnp.zeros(rest, F32)


def halve(order, where, pair, slabs, high, where_bit, first, width, name, smalls=(), extra=0):
    rows = pair[0].shape[0]
    total = rows - (0 if smalls else extra)
    if extra == 0:
        block = 512 if width % 512 == 0 and first % 512 == 0 else 384
    else:
        block = width
    at = first // block
    out_rows = total // 2 + extra
    half = pl.BlockSpec((out_rows, block), lambda i: (0, i))
    return order(
        functools.partial(halve_kernel, slabs, high, where_bit, len(smalls), extra),
        [where, *smalls, *pair],
        [smem()]
        + [pl.BlockSpec(a.shape, lambda i: (0, 0)) for a in smalls]
        + [pl.BlockSpec((rows, block), lambda i: (0, at + i))] * 2,
        (sds((out_rows, width), F32),) * 2,
        [half, half],
        grid=(width // block,),
        mib=12,
        name=name,
    )


def norm_back_kernel(
    dres2_ref, own_ref, other_ref, xhat_ref, rstd_ref, vec_ref, wo_ref,
    dres1_far, g0_ref, dmix_ref, sums_ref, dres1_ref, sems,
):
    dhid = dres2_ref[...] + (own_ref[...] + other_ref[...])
    xhat = xhat_ref[...]
    sums_ref[...] = jnp.zeros(sums_ref.shape, F32)
    sums_ref[1:2, :] = col_sum(dhid * xhat)
    sums_ref[2:3, :] = col_sum(dhid)
    dres1 = norm_back(dhid, xhat, rstd_ref[:, 0:1], vec_ref[1:2, :])
    dres1_ref[...] = dres1
    (copy,) = start_all(((dres1_ref, dres1_far),), sems)
    sums_ref[0:1, :] = col_sum(dres1)
    g0 = dres1.astype(BF16)
    g0_ref[...] = g0
    dmix_ref[...] = dot_nt(g0, wo_ref[...]).astype(BF16)
    copy.wait()


def norm_one_back(order, c, dres2, own, other, xhat, rstd, vec, wo):
    _, rows = CHUNKS[c]
    return order(
        norm_back_kernel,
        (dres2, own, other, xhat, rstd, vec, wo),
        [vmem()] * 7,
        (sds((rows, D), F32), sds((rows, D), BF16), sds((rows, DL), BF16), sds((8, D), F32)),
        [hbm()] + [vmem()] * 3,
        scratch_shapes=[pltpu.VMEM((rows, D), F32), pltpu.SemaphoreType.DMA((1,))],
        us=20000 if c == ORDER[0] else 1,
        name=f"norm_back_{c}",
    )


def attend_back_kernel(
    start, rows, first, dmix_ref, p_ref, q_ref, k_ref, v_ref, ur_ref, r_ref, o_ref, *rest,
):
    if not first:
        dk_in, dv_in, dm_in, dz_in = rest[:4]
        rest = rest[4:]
    dq_ref, dk_ref, dv_ref, dm_ref, dz_ref = rest
    if first:
        dz_ref[...] = jnp.zeros(dz_ref.shape, F32)
    else:
        dz_ref[...] = dz_in[...]

    lanes = first_lanes()
    r_w = r_ref[0, start : start + rows, :]
    r_h = r_ref[1, start : start + rows, :]
    upper = (iota((rows, PAIR), 1) >= 64).astype(jnp.int32)
    ur = ur_ref[start : start + rows, :]
    pick = lambda h, a: jnp.where(
        lanes if h % 2 == 0 else jnp.logical_not(lanes), a, jnp.zeros_like(a)
    )
    pair_cols = lambda h: slice(h // 2 * PAIR, h // 2 * PAIR + PAIR)

    def dprob_of(h):
        return dot_nt(pick(h, dmix_ref[:, pair_cols(h)]), v_ref[:, pair_cols(h)])

    def back_of(h, dprob):
        cols = pair_cols(h)
        prob = p_ref[h]
        prob_f = prob.astype(F32)
        both = prob_f * dprob
        ds = both - prob_f * jnp.sum(both, axis=1, keepdims=True)
        low = ds.astype(BF16)
        dq = dot(low, pick(h, k_ref[:, cols]))
        dk = dot_tn(low, pick(h, q_ref[:, cols]))
        dv = dot_tn(prob, pick(h, dmix_ref[:, cols]))
        dbias = dot_nt(low, o_ref[...])
        for at in range(0, rows, SUB):
            size = min(SUB, rows - at)
            sub = (start + at) // SUB
            sums = {}
            for g in range(KEYS // SUB):
                group = min(max(g - sub + 2, 0), 4)
                piece = ds[at : at + size, g * 128 : g * 128 + 128]
                sums[group] = piece if group not in sums else sums[group] + piece
            for group, piece in sums.items():
                dz_ref[h, 0:size, group * 128 : group * 128 + 128] += piece
        return dq, dk, dv, dbias

    def table_of(h, dbias):
        parts = []
        for plane, r_col in ((0, r_w), (1, r_h)):
            same = None
            under = None
            for kk in range(4):
                base = plane * 512 + kk * 128
                piece = dbias[:, base : base + 128]
                ok = (2 * kk + upper) >= r_col
                yes = jnp.where(ok, piece, 0.0)
                no = jnp.where(ok, 0.0, piece)
                same = yes if same is None else same + yes
                under = no if under is None else under + no
            parts += [same, under]
        dm = dot_tn(ur, jnp.concatenate(parts, axis=1).astype(BF16))
        at = slice(h * 512, h * 512 + 512)
        dm_ref[:, at] = dm if first else dm_in[:, at] + dm

    dprob = dprob_of(0)
    totals = None
    for h in range(HL):
        following = dprob_of(h + 1) if h + 1 < HL else None
        dq, dk, dv, dbias = back_of(h, dprob)
        dprob = following
        cols = pair_cols(h)
        if h % 2 == 0:
            totals = (dq, dk, dv)
        else:
            dq_ref[:, cols] = (totals[0] + dq) * 0.125
            dk = totals[1] + dk
            dv = totals[2] + dv
            dk_ref[:, cols] = dk if first else dk_in[:, cols] + dk
            dv_ref[:, cols] = dv if first else dv_in[:, cols] + dv
        table_of(h, dbias)


def attend_back(order, c, dmix, p, q, k, v, ur, r, o, carry, into):
    start, rows = CHUNKS[c]
    operands = [dmix, p, q, k, v, ur, r, o]
    aliases = {}
    if carry is not None:
        operands += list(carry)
        aliases = {8 + i: 1 + i for i in range(4)}
    return order(
        functools.partial(attend_back_kernel, start, rows, carry is None),
        operands,
        [vmem()] * len(operands),
        (
            sds((rows, DL), F32),
            sds((KEYS, DL), F32),
            sds((KEYS, DL), F32),
            sds((128, HL * 512), F32),
            sds((HL, SUB, 640), F32),
        ),
        [vmem()] * 5,
        input_output_aliases=aliases,
        into=into,
        name=f"attend_back_{c}",
    )


def table_sums_kernel(dm_ref, dz_ref, out_ref):
    lane = iota((PAIR, BINS_2D), 0)
    plane_bin = jnp.clip(lane - 64, -32, 31) + 32
    plane_pick = (plane_bin == iota((PAIR, BINS_2D), 1)).astype(F32)
    lane = iota((512, BINS_1D), 0)
    line_bin = jnp.clip(lane - 256, -16, 15) + 16
    line_pick = (line_bin == iota((512, BINS_1D), 1)).astype(F32)
    first = first_lanes()
    flip = (iota((SUB, SUB), 0) + iota((SUB, SUB), 1) == SUB - 1).astype(F32)
    bin_id = iota((1, BINS_1D), 1)
    exact = functools.partial(
        lax.dot_general,
        dimension_numbers=(((1,), (0,)), ((), ())),
        precision=HIGHEST,
        preferred_element_type=F32,
    )
    out_ref[...] = jnp.zeros(out_ref.shape, F32)
    for h in range(HL):
        z = dz_ref[h]
        left = jnp.sum(z[:, 0:128])
        right = jnp.sum(z[:, 512:640])
        band = jnp.concatenate([z[:, 128:512], jnp.zeros((SUB, 128), F32)], axis=1)
        band = pltpu.roll(exact(flip, band), 512 - 127 + 128, 1, stride=1, stride_axis=0)
        line = exact(col_sum(band), line_pick)
        line = line + jnp.where(bin_id == 0, left, 0.0) + jnp.where(bin_id == 31, right, 0.0)
        out_ref[h : h + 1, 0:BINS_1D] = line
        for plane in range(2):
            total = None
            for below in range(2):
                at = h * 512 + plane * 256 + below * 128
                g = dm_ref[plane * 64 : plane * 64 + 64, at : at + 128]
                g = jnp.where(first, g + pltpu.roll(g, 64, 1), 0.0)
                g = pltpu.roll(g, 1 - below, 1, stride=1, stride_axis=0)
                total = g if total is None else total + g
            summed = exact(col_sum(total), plane_pick)
            at = BINS_1D + plane * 64
            out_ref[h : h + 1, at : at + 64] = summed


def table_sums(order, dm, dz):
    return order(
        table_sums_kernel,
        (dm, dz),
        [vmem()] * 2,
        (sds((8, 256), F32),),
        [vmem()],
        name="table_sums",
    )[0]


def project_back_kernel(
    q0, q1, q2, dk_ref, dv_ref, wq_ref, wk_ref, wv_ref, part_ref, bias_ref,
):
    sum_q = None
    sum_v = None
    for (start, rows), dq in zip(CHUNKS, (q0, q1, q2)):
        query = dq[...]
        value = dv_ref[start : start + rows, :]
        sum_q = col_sum(query) if sum_q is None else sum_q + col_sum(query)
        sum_v = col_sum(value) if sum_v is None else sum_v + col_sum(value)
        query = query.astype(BF16)
        key = dk_ref[start : start + rows, :].astype(BF16)
        value = value.astype(BF16)
        part_ref[start : start + rows, :] = (
            dot_nt(query, wq_ref[...]) + dot_nt(key, wk_ref[...]) + dot_nt(value, wv_ref[...])
        )
    bias_ref[...] = jnp.zeros(bias_ref.shape, F32)
    bias_ref[0:1, 0:DL] = sum_q
    bias_ref[0:1, DL:D] = sum_v


def project_back(order, dq, dk, dv, wq, wk, wv):
    return order(
        project_back_kernel,
        (*dq, dk, dv, wq, wk, wv),
        [vmem()] * 8,
        (sds((ROWS, D), F32), sds((8, D), F32)),
        [vmem()] * 2,
        us=15000,
        name="project_back",
    )


def taps_kernel(
    count_ref, x_hbm, pt, r0_far, r1_far, r2_far, out_ref,
    text_scr, patch_scr, raw_scr, x_ref, r0, r1, r2, sems,
):
    count = count_ref[0]
    copies = start_all(((x_hbm, x_ref), (r0_far, r0), (r1_far, r1), (r2_far, r2)), sems)
    copies[0].wait()
    load_page(x_ref, count, text_scr, patch_scr, raw_scr)
    for copy in copies[1:]:
        copy.wait()
    out_ref[...] = jnp.zeros(out_ref.shape, F32)
    shifts = tuple(range(-3, 4))
    for c in range(2):
        cols = slice(c * 384, c * 384 + 384)

        def one(b, sums, cols=cols, res=None, first=0):
            base = pl.multiple_of(b * 32, 32)
            win = text_scr[pl.ds(first + base, 48), cols]
            grad = pt[pl.ds(first + base, 32), cols] + 0.5 * res[pl.ds(base, 32), cols]
            out = []
            for shift, total in zip(shifts, sums):
                prod = grad * win[8 + shift : 40 + shift]
                out.append(total + jnp.sum(prod.reshape(4, 8, 384), axis=0))
            return tuple(out)

        sums = tuple(jnp.zeros((8, 384), F32) for _ in shifts)
        for (first, rows), res in zip(CHUNKS, (r0, r1)):
            sums = lax.fori_loop(
                0, rows // 32, functools.partial(one, res=res, first=first), sums
            )
        for row, total in enumerate(sums):
            out_ref[row : row + 1, cols] = col_sum(total)

    def patches(side):
        live, has_left, has_right = grid_masks(side)
        for c in range(D // PAIR):
            cols = slice(c * PAIR, c * PAIR + PAIR)
            win = patch_scr[:, cols]
            grad = jnp.where(live, pt[TEXT:ROWS, cols] + 0.5 * r2[:, cols], 0.0)
            for ds in (-1, 0, 1):
                masked = grad
                if ds == -1:
                    masked = jnp.where(has_left, grad, 0.0)
                if ds == 1:
                    masked = jnp.where(has_right, grad, 0.0)
                for dr in (-1, 0, 1):
                    row = 7 + 3 * (dr + 1) + ds + 1
                    at = MARGIN + dr * side + ds
                    out_ref[row : row + 1, cols] = col_sum(masked * win[at : at + 208])

    by_grid(count, patches)


def tap_sums(order, count, x, part, res):
    return order(
        taps_kernel,
        (count, x, part, *res),
        [smem(), hbm(), vmem()] + [hbm()] * 3,
        (sds((16, D), F32),),
        [vmem()],
        scratch_shapes=PAGE_SCRATCH
        + [pltpu.VMEM((SEQ, D), BF16)]
        + [pltpu.VMEM((rows, D), F32) for _, rows in CHUNKS]
        + [pltpu.SemaphoreType.DMA((4,))],
        mib=14,
        name="tap_sums",
    )[0]


def decode_text_kernel(text_ref, p, s, r0, r1, out_ref, text_scr):
    zero8 = jnp.zeros((8, D), F32)
    text_scr[0:8, :] = zero8
    text_scr[520:528, :] = zero8
    for r, (at, rows) in zip((r0, r1), CHUNKS):
        for b in range(rows // 64):
            res = r[64 * b : 64 * b + 64, :]
            here = slice(at + 64 * b, at + 64 * b + 64)
            text_scr[8 + at + 64 * b : 72 + at + 64 * b, :] = res + (p[here, :] + s[here, :])
    for c in range(2):
        cols = slice(c * 384, c * 384 + 384)
        taps = text_taps(text_ref, cols)

        def one(b, carry, cols=cols, taps=taps):
            base = pl.multiple_of(b * 32, 32)
            win = text_scr[pl.ds(base, 48), cols]
            out_ref[pl.ds(base, 32), cols] = text_conv_block(win, taps, -1).astype(BF16)
            return carry

        lax.fori_loop(0, TEXT // 32, one, 0)


def decode_kernel(
    count_ref, text_ref, patch_ref, p_far, s_far, r0_far, r1_far, r2_far, out_ref,
    text_scr, patch_scr, raw_scr, p, s, r0, r1, r2, sems,
):
    pairs = ((p_far, p), (s_far, s), (r0_far, r0), (r1_far, r1), (r2_far, r2))
    for copy in start_all(pairs, sems):
        copy.wait()
    decode_text_kernel(text_ref, p, s, r0, r1, out_ref, text_scr)
    count = count_ref[0]
    raw_scr[...] = r2[...] + (p[TEXT:ROWS, :] + s[TEXT:ROWS, :])
    fill_patches(patch_scr, lambda cols: raw_scr[:, cols], count)

    def patches(side):
        for c in range(D // PAIR):
            cols = slice(c * PAIR, c * PAIR + PAIR)
            total = raw_scr[:, cols] + patch_conv_cols(patch_scr[:, cols], patch_ref, cols, side, -1)
            out_ref[TEXT:SEQ, cols] = total[0 : SEQ - TEXT].astype(BF16)

    by_grid(count, patches)


def decode(order, count, text_w, patch_w, part, other, res):
    return order(
        decode_kernel,
        (count, text_w, patch_w, part, other, *res),
        [smem()] + [vmem()] * 2 + [hbm()] * 5,
        (sds((SEQ, D), BF16),),
        whole_blocks((sds((SEQ, D), BF16),)),
        grid=(1,),
        scratch_shapes=PAGE_SCRATCH
        + [pltpu.VMEM((ROWS, D), F32)] * 2
        + [pltpu.VMEM((rows, D), F32) for _, rows in CHUNKS]
        + [pltpu.SemaphoreType.DMA((5,))],
        mib=18,
        name="decode",
    )[0]


def swap_tensor(x):
    return lax.ppermute(x, "tensor", [(0, 1), (1, 0)])


def swap_dp(x, bit, dp):
    return lax.ppermute(x, "dp", [(i, i ^ bit) for i in range(dp)])


def swap_core(parts, dp):
    return (parts[0], swap_dp(parts[1], 1, dp)) if len(parts) == 2 else parts


class Scatter:
    def __init__(self, order, dp, where, pair, bits, name, first, width):
        self.order, self.dp, self.where, self.bits, self.name = order, dp, where, bits, name
        self.window = (first, width)
        self.pair = pair
        self.left = list(range(1, dp.bit_length() - 1))
        self.extra = 0

    def step(self, *smalls):
        if len(self.pair) == 1:
            return
        bit = self.bits[0]
        self.bits = self.bits[1:]
        at = self.left.index(bit)
        if smalls:
            self.extra = smalls[0].shape[0]
        own, out = halve(
            self.order, self.where, self.pair, 2 ** len(self.left), 2**at, 1 + bit, *self.window,
            f"{self.name}_{bit}", smalls, self.extra,
        )
        self.window = (0, self.window[1])
        self.left.remove(bit)
        self.pair = (own, swap_dp(out, 2**bit, self.dp))

    def total(self):
        first, width = self.window
        whole = self.pair[0][:, first : first + width]
        return lax.psum_scatter(whole, "dp", scatter_dimension=0, tiled=True)


def whole_blocks(shapes):
    return [pl.BlockSpec(a.shape, lambda i, n=len(a.shape): (0,) * n) for a in shapes]


EARLY = 8
LATE = 24


def total_of(order, part, name):
    return add_blocks(order, *part.pair, name)


def add_blocks(order, *pair_name):
    *pair, name = pair_name
    shapes = (sds(pair[0].shape, F32),)
    return order(
        add_kernel, pair, whole_blocks(pair), shapes, whole_blocks(shapes), grid=(1,), name=name
    )[0]


def add_kernel(a, b, out):
    out[...] = a[...] + b[...]


def add_here(order, a, b, name):
    return order(
        add_kernel, (a, b), [vmem()] * 2, (sds(a.shape, F32),), [vmem()], name=name
    )[0]


def joint_kernel(where_ref, sum_ref, a_ref, b_ref, own_ref, out_ref):
    mine = where_ref[4]
    slab = a_ref.shape[0] // 2
    width = a_ref.shape[1]
    for ref, which in ((own_ref, mine), (out_ref, 1 - mine)):
        rows = pl.ds(pl.multiple_of(which * slab, 8), slab)
        ref[0:slab, 0:D] = sum_ref[rows, :]
        ref[0:slab, D : D + width] = a_ref[rows, :] + b_ref[rows, :]
        ref[slab:, 0:D] = sum_ref[2 * slab :, :]
        ref[slab:, D : D + width] = jnp.zeros((EARLY, width), F32)


def joint_step(order, dp, where, summed, part):
    rows, width = part.pair[0].shape
    shapes = (sds((rows // 2 + EARLY, D + width), F32),) * 2
    operands = (summed, *part.pair)
    own, out = order(
        joint_kernel, (where, *operands), [smem()] + whole_blocks(operands), shapes,
        whole_blocks(shapes), grid=(1,), name="joint_3",
    )
    return own, swap_dp(out, 8, dp)


def last_totals_kernel(
    both, b0, b1, joint, ob, ia, q_ref, k_ref, v_ref, o_ref, outer_ref, inner_ref, small_ref,
):
    slab = q_ref.shape[0]
    q_ref[...] = both[0:slab, 0:DL]
    k_ref[...] = both[0:slab, DL:D]
    both = b0[...] + b1[...]
    v_ref[...] = both[0:slab, 0:DL]
    o_ref[...] = both[0:slab, DL:D]
    small_ref[0:LATE, :] = both[slab:, 0:D]
    split = joint.shape[1] - D
    outer_ref[:, 0:split] = joint[0:slab, D : D + split]
    outer_ref[:, split:FL] = ob[...]
    inner_ref[:, 0:D] = ia[...]
    inner_ref[:, D:FL] = joint[0:slab, 0:D]
    small_ref[LATE : LATE + EARLY, :] = joint[slab:, 0:D]


def last_totals(order, total_a, part_b, *rest):
    *rest, slab = rest
    operands = [total_a, *part_b.pair, *rest]
    plain = sds((slab, DL), F32)
    wide = sds((slab, FL), F32)
    shapes = (plain,) * 4 + (wide, wide, sds((LATE + EARLY, D), F32))
    return order(
        last_totals_kernel, operands, whole_blocks(operands), shapes, whole_blocks(shapes),
        grid=(1,), name="last_totals",
    )


def gather_early_kernel(f0, f1, f2, out):
    sums = f0[...] + f1[...] + f2[...]
    out[...] = jnp.zeros(out.shape, F32)
    out[0:1, :] = sums[0:1, 0:D]
    out[1:2, :] = sums[0:1, D:FL]
    out[2:5, :] = sums[1:4, 0:D]


def gather_early(order, sums, into):
    (early,), moved = order(
        gather_early_kernel, sums, [vmem()] * 3, (sds((EARLY, D), F32),), [vmem()], into=into,
        name="gather_early",
    )
    return early, moved


def gather_late_kernel(taps, a0, a1, a2, bias, tab, out):
    out[...] = jnp.zeros(out.shape, F32)
    out[0:16, :] = taps[0:16, :]
    out[16:19, :] = (a0[...] + a1[...] + a2[...])[0:3]
    out[19:20, :] = bias[0:1, :]
    for h in range(HL):
        at = 256 * (h % 3)
        out[20 + h // 3 : 21 + h // 3, at : at + 256] = tab[h : h + 1, :]


def gather_late(order, *rest):
    return order(
        gather_late_kernel, rest, [vmem()] * 6, (sds((LATE, D), F32),), [vmem()],
        name="gather_late",
    )[0]


def finish_kernel(
    place_ref, own, core, other, both,
    text, patch, out_b, gain1, shift1, outer_b, gain2, shift2,
    query_b, value_b, inner_b, line, width, height,
):
    small = own[...] + core[...]
    slab = patch.shape[1]
    turn = lambda a: pltpu.roll(a, lax.rem(D - place_ref[0] * slab, D), 1)[:, 0:slab]
    shard = turn(small)
    taps = shard[0:16] + turn(other[...] + both[...])
    for dilate in range(3):
        for tap in range(3):
            text[dilate, tap] = taps[3 + (tap - 1) * (dilate + 1)]
    patch[...] = taps[7:16]
    rows = (16, 17, 18, LATE + 2, LATE + 3, LATE + 4)
    for i, ref in zip(rows, (out_b, gain1, shift1, outer_b, gain2, shift2)):
        ref[...] = shard[i]
    query_b[...] = small[19, 0:DL]
    value_b[...] = small[19, DL:D]
    inner_b[0:D] = small[LATE]
    inner_b[D:FL] = small[LATE + 1]
    for h in range(HL):
        row, at = 20 + h // 3, 256 * (h % 3)
        line[h : h + 1, :] = small[row : row + 1, at : at + 32]
        width[h : h + 1, :] = small[row : row + 1, at + 32 : at + 96]
        height[h : h + 1, :] = small[row : row + 1, at + 96 : at + 160]


def finish(order, place, own, core, other, both, slab):
    f = lambda *shape: sds(shape, F32)
    shapes = (f(3, 3, slab), f(9, slab)) + (f(slab),) * 6
    shapes += (f(DL), f(DL), f(FL), f(HL, 32), f(HL, 64), f(HL, 64))
    return order(
        finish_kernel, (place, own, core, other, both),
        [smem()] + whole_blocks((own, core, other, both)), shapes, whole_blocks(shapes), grid=(1,),
        name="finish",
    )


def swap_both(x, dp):
    pairs = [(2 * i + t, 2 * (i ^ 1) + (t ^ 1)) for i in range(dp) for t in range(2)]
    return lax.ppermute(x, ("dp", "tensor"), pairs)


def per_device(
    dp,
    page_tokens,
    patch_counts,
    token_boxes,
    text_weight,
    patch_weight,
    query_weight,
    query_bias,
    key_weight,
    value_weight,
    value_bias,
    out_weight,
    out_bias,
    line_table,
    width_table,
    height_table,
    norm1_gain,
    norm1_shift,
    inner_weight,
    inner_bias,
    outer_weight,
    outer_bias,
    norm2_gain,
    norm2_shift,
    cotangent,
):
    place = lax.axis_index("dp")
    half = lax.axis_index("tensor")
    core = place % 2
    bits = [(place // 2**i) % 2 for i in range(4)]
    where = jnp.stack([half] + bits).astype(jnp.int32)
    x = page_tokens.reshape(SEQ, D)
    cot = cotangent.reshape(SEQ, D)
    slab = D // dp if dp == 16 else None
    order = Order()

    z, m, o, u, r, wo_mine, ur = make_tables(
        order,
        where,
        jnp.concatenate([jnp.transpose(a) for a in (line_table, width_table, height_table)], axis=1),
        token_boxes.reshape(2, SEQ),
        out_weight,
    )
    wo_a = swap_tensor(wo_mine)
    row = lax.broadcasted_iota(jnp.int32, (8, 1), 0)
    bias = jnp.where(row == 0, query_bias[None, :], value_bias[None, :]).astype(F32)
    (q0, q1, q2, k, v), enc, enc_low, (o_far, ur_far, r_far) = encode(
        order, patch_counts, x, text_weight, patch_weight, bias,
        query_weight, key_weight, value_weight, (o, ur, r),
    )
    q = (q0, q1, q2)

    vec = jnp.zeros((8, 1), F32)
    for i, a in enumerate(
        (out_bias, norm1_gain, norm1_shift, outer_bias, norm2_gain, norm2_shift)
    ):
        vec = jnp.where(row == i, a[None, :].astype(F32), vec)
    bi = jnp.broadcast_to(inner_bias[None, :].astype(F32), (8, FL))
    probs, mix, mix_low, mix_other = ([None] * 3 for _ in range(4))
    xhat, rstd, hlow, act, slope, outer, outer_other = ([None] * 3 for _ in range(7))

    def attention_of(c, out):
        (p, a, low), far = attend(order, c, patch_counts, q[c], k, v, u, r, m, o, z, out)
        mix[c], mix_other[c] = a, swap_tensor(a)
        return (p, low), far

    def feed_of(c, out=()):
        got = feed(
            order, c, where, mix[c], mix_other[c], enc[c], vec, out_weight, wo_a, wo_b,
            inner_weight, bi, outer_weight, out,
        )
        far = None
        if out:
            got, far = got
        for keep, a in zip((xhat, rstd, hlow, act, slope, outer), got):
            keep[c] = a
        outer_other[c] = swap_tensor(got[5])
        return far

    near, enc = attention_of(ORDER[0], enc)
    wo_a = pass_on(order, wo_a)
    wo_b = swap_dp(wo_a, 1, dp)
    near, far = attention_of(ORDER[1], (*near, *enc_low, q0, q1, q2, k, v))
    probs[ORDER[0]], mix_low[ORDER[0]], *far = far
    enc_low, q_far, k_far, v_far = far[0:3], far[3:6], far[6], far[7]
    near, (probs[ORDER[1]], mix_low[ORDER[1]]) = attention_of(ORDER[2], near)
    probs[ORDER[2]], mix_low[ORDER[2]] = feed_of(ORDER[0], near)
    feed_of(ORDER[1])
    feed_of(ORDER[2])
    layer_out, inner_grad, outer_grad = None, None, None
    dres2, g2, g1, dhid, dhid_other, sums2 = ([None] * 3 for _ in range(6))
    for c in ORDER:
        got = feed_back(
            order, c, patch_counts, outer[c], outer_other[c], xhat[c], cot, vec, outer_weight,
            slope[c], inner_weight, layer_out,
        )
        layer_out = got[0]
        for keep, a in zip((dres2, g2, g1, dhid, sums2), got[1:]):
            keep[c] = a
        dhid_other[c] = swap_tensor(got[4])
        last = c == ORDER[2]
        inner_grad = chunk_grads(
            order, slab, where, hlow[c], g1[c], inner_grad, last, f"inner_grads_{c}"
        )
        outer_grad = chunk_grads(
            order, slab, where, g2[c], act[c], outer_grad, last, f"outer_grads_{c}"
        )
        if not last:
            inner_grad, outer_grad = inner_grad[0], outer_grad[0]
    scatter = functools.partial(Scatter, order, dp, where)
    x_first, z_first = (1, 2, 3), (2, 3, 1)
    inner_pair, outer_pair = swap_core(inner_grad, dp), swap_core(outer_grad, dp)
    inner = scatter(inner_pair, x_first, "inner", 0, D)
    inner_b = scatter(inner_pair, x_first, "inner_b", D, D)
    outer_a = scatter(outer_pair, x_first, "outer_a", 0, D)
    outer_b = scatter(outer_pair, z_first, "outer_b", D, D)
    early, (prob,) = gather_early(order, sums2, (probs[ORDER[0]],))
    carry = None
    dres1, g0, dq, sums1 = ([None] * 3 for _ in range(4))
    for c in ORDER:
        got = norm_one_back(
            order, c, dres2[c], dhid[c], dhid_other[c], xhat[c], rstd[c], vec, out_weight
        )
        dres1[c], g0[c], _, sums1[c] = got
        if c == ORDER[0]:
            inner.step()
            outer_b.step()
            inner_b.step(early)
        if c == ORDER[1]:
            outer_a.step()
            inner.step()
            outer_b.step()
        if c == ORDER[2]:
            inner_b.step()
            inner.step()
            outer_b.step()
        into = [probs[after] for after in ORDER[ORDER.index(c) + 1 :][:1]]
        if not into:
            into = [query_weight, key_weight, value_weight]
        got = attend_back(
            order, c, got[2], prob, q_far[c], k_far, v_far, ur_far, r_far, o_far, carry, into
        )
        got, into = got
        prob = into[0]
        dq[c], *carry = got
    weights = into
    dk, dv, dm, dz = carry
    if dp == 16:
        total_outer_b = total_of(order, outer_b, "outer_b_total")
        total_inner = total_of(order, inner, "inner_total")
    outer_a.step()
    if dp == 16:
        inner_b = total_of(order, inner_b, "inner_b_sum")
    operands = (enc_low, dq, dk, dv, g0, mix_low)
    if dp == 16:
        got = attention_grads(order, slab, where, *operands)
        first_pair, second_pair = swap_core(got[0:2], dp), swap_core(got[2:4], dp)
    else:
        first_pair = second_pair = plain_grads(order, *operands)
    rest = 0 if dp == 16 else SPLIT
    part_a = scatter(first_pair, x_first, "part_a", 0, SPLIT)
    part_b = scatter(second_pair, x_first, "part_b", rest, 4 * DL - SPLIT)
    part, bias_sums = project_back(order, dq, dk, dv, *weights)
    part_other = swap_tensor(part)
    part_a.step()
    tables = table_sums(order, dm, dz)
    taps = tap_sums(order, patch_counts, x, part, dres1)
    late = gather_late(order, taps, *sums1, bias_sums, tables)
    if dp == 16:
        joint = joint_step(order, dp, where, inner_b, outer_a)
    part_b.step(late)
    part_a.step()
    if dp == 16:
        joint = add_blocks(order, *joint, "joint_total")
    part_a.step()
    part_b.step()
    if dp == 16:
        total_a = total_of(order, part_a, "part_a_total")
    part_b.step()
    input_grad = decode(order, patch_counts, text_weight, patch_weight, part, part_other, dres1)
    if dp == 16:
        grad_q, grad_k, grad_v, grad_o, sum_outer, inner_total, small = last_totals(
            order, total_a, part_b, joint, total_outer_b, total_inner, slab
        )
    else:
        inner_total = jnp.concatenate([inner.total(), inner_b.total()], axis=1)
        sum_outer = jnp.concatenate([outer_a.total(), outer_b.total()], axis=1)
        both = jnp.concatenate([part_a.total(), part_b.total()], axis=1)
        grad_q, grad_k, grad_v, grad_o = jnp.split(both, 4, axis=1)
        small = jnp.concatenate([late, early], axis=0)
        bit = 2
        while bit < dp:
            small = small + swap_dp(small, bit, dp)
            bit *= 2
    small_others = (
        swap_dp(small, 1, dp), swap_tensor(small[0:16]), swap_both(small[0:16], dp)
    )
    small = finish(
        order, jnp.reshape(place, (1,)).astype(jnp.int32), small, *small_others, D // dp
    )
    text, patch, out_b, gain1, shift1, outer_b, gain2, shift2 = small[:8]
    query_b, value_b, inner_b, line, width, height = small[8:]
    return (
        layer_out.reshape(1, SEQ, D),
        input_grad.reshape(1, SEQ, D),
        text,
        patch,
        grad_q,
        query_b,
        grad_k,
        grad_v,
        value_b,
        jnp.transpose(grad_o),
        out_b,
        jnp.transpose(line),
        jnp.transpose(width),
        jnp.transpose(height),
        gain1,
        shift1,
        inner_total,
        inner_b,
        jnp.transpose(sum_outer),
        outer_b,
        gain2,
        shift2,
    )


def solution(mesh):
    placed = (
        P("dp", None, None),
        P("dp"),
        P("dp", None, None),
        P(),
        P(),
        P(None, "tensor"),
        P("tensor"),
        P(None, "tensor"),
        P(None, "tensor"),
        P("tensor"),
        P("tensor", None),
        P(),
        P(None, "tensor"),
        P(None, "tensor"),
        P(None, "tensor"),
        P(),
        P(),
        P(None, "tensor"),
        P("tensor"),
        P("tensor", None),
        P(),
        P(),
        P(),
        P("dp", None, None),
    )
    return jax.shard_map(
        functools.partial(per_device, mesh.shape["dp"]),
        mesh=mesh,
        in_specs=placed,
        out_specs=(
            P("dp", None, None),
            P("dp", None, None),
            P(None, None, "dp"),
            P(None, "dp"),
            P("dp", "tensor"),
            P("tensor"),
            P("dp", "tensor"),
            P("dp", "tensor"),
            P("tensor"),
            P("tensor", "dp"),
            P("dp"),
            P(None, "tensor"),
            P(None, "tensor"),
            P(None, "tensor"),
            P("dp"),
            P("dp"),
            P("dp", "tensor"),
            P("tensor"),
            P("tensor", "dp"),
            P("dp"),
            P("dp"),
            P("dp"),
        ),
        check_vma=False,
    )
```

```python
import functools

import jax
import jax.numpy as jnp
from jax import lax
from jax.experimental import pallas as pl
from jax.experimental.pallas import tpu as pltpu
from jax.sharding import PartitionSpec as P

HEADS = 12
TEXT = 512
GRID_SMALL = 7
GRID_LARGE = 14
BINS_1D = 32
BINS_2D = 64
BIN_WIDTH = 8

F32 = jnp.float32
BF16 = jnp.bfloat16
EPS = 1e-05
NEG = -1000000000.0
HIGHEST = lax.Precision.HIGHEST

D = 768
SEQ = 708
ROWS = 720
KEYS = 768
CHUNKS = ((0, 256), (256, 256), (512, 208))
ORDER = (2, 0, 1)
SUB = 128
PAIR = 128
HL = 6
DL = 384
FL = 1536
MARGIN = 16
MIB = 1024 * 1024


def vmem():
    return pl.BlockSpec(memory_space=pltpu.VMEM)


def anywhere():
    return pl.BlockSpec(memory_space=pl.ANY)


def hbm():
    return pl.BlockSpec(memory_space=pltpu.HBM)


def smem():
    return pl.BlockSpec(memory_space=pltpu.SMEM)


def params(mib):
    return pltpu.CompilerParams(vmem_limit_bytes=mib * MIB)


def sds(shape, dtype):
    return jax.ShapeDtypeStruct(shape, dtype)


TOKEN = jax.ShapeDtypeStruct((8, 128), jnp.float32)


class Order:
    def __init__(self):
        self.token = None

    def __call__(
        self, kernel, operands, in_specs, out_shape, out_specs, mib=10, us=1, out=(), into=(),
        scratch_shapes=(), **more,
    ):
        operands, in_specs = list(operands), list(in_specs)
        count, outs, moved = len(operands), len(out_shape), len(out) + len(into)
        operands += [*out, *into]
        in_specs += [vmem()] * len(out) + [hbm()] * len(into)
        has_token = self.token is not None
        grid = "grid" in more
        token_spec = pl.BlockSpec(TOKEN.shape, lambda *i: (0, 0)) if grid else vmem()
        if has_token:
            operands.append(self.token)
            in_specs.append(token_spec)
        shapes = [sds(a.shape, a.dtype) for a in (*out, *into)]
        specs = [hbm()] * len(out) + [vmem()] * len(into)
        scratch_shapes = list(scratch_shapes)
        if moved:
            scratch_shapes.append(pltpu.SemaphoreType.DMA((moved,)))

        def body(*refs):
            rest = list(refs)
            sources = rest[count : count + moved]
            del rest[count : count + moved + has_token]
            at = count + outs
            targets = rest[at : at + moved]
            rest[at + moved][...] = jnp.zeros(TOKEN.shape, F32)
            del rest[at : at + moved + 1]
            copies = start_all(zip(sources, targets), rest.pop()) if moved else []
            kernel(*rest)
            for copy in copies:
                copy.wait()

        got = pl.pallas_call(
            body,
            out_shape=tuple(out_shape) + tuple(shapes) + (TOKEN,),
            in_specs=in_specs,
            out_specs=tuple(out_specs) + tuple(specs) + (token_spec,),
            scratch_shapes=scratch_shapes,
            compiler_params=params(mib),
            cost_estimate=cost(us),
            **more,
        )(*operands)
        self.token = got[-1]
        if moved:
            return got[:outs], got[outs:-1]
        return got[:-1]


def start_all(pairs, sems, first=0):
    copies = [
        pltpu.make_async_copy(src, dst, sems.at[first + i]) for i, (src, dst) in enumerate(pairs)
    ]
    for copy in copies:
        copy.start()
    return copies


def dot(a, b):
    return lax.dot_general(a, b, (((1,), (0,)), ((), ())), preferred_element_type=F32)


def dot_nt(a, b):
    return lax.dot_general(a, b, (((1,), (1,)), ((), ())), preferred_element_type=F32)


def dot_tn(a, b):
    return lax.dot_general(a, b, (((0,), (0,)), ((), ())), preferred_element_type=F32)


def cost(us):
    return pl.CostEstimate(flops=int(us * 1.0e6), bytes_accessed=int(us * 1.0e3), transcendentals=0)


def iota(shape, dim):
    return lax.broadcasted_iota(jnp.int32, shape, dim)


def first_lanes():
    return iota((1, PAIR), 1) < 64


def tables_kernel(
    where_ref, tab_ref, boxes_hbm, wo_hbm,
    z_ref, m_ref, o_ref, u_ref, r_ref, mine_ref, ur_ref,
    box_scr, boxes_ref, wo_ref, sems,
):
    half = DL // 2
    rows = pl.ds(pl.multiple_of(where_ref[1] * half, half), half)
    copies = start_all(
        (
            (boxes_hbm, boxes_ref),
            (wo_hbm.at[rows, :], wo_ref),
        ),
        sems,
    )
    for copy in copies:
        copy.wait()
    mine_ref[...] = wo_ref[...].astype(F32)
    lane = iota((BINS_1D, 768), 1)
    bucket = jnp.where(lane < 640, jnp.clip(lane - 256, -16, 15) + 16, 0)
    line_pick = (bucket == iota((BINS_1D, 768), 0)).astype(BF16)
    line_base = dot(tab_ref[:, 0:BINS_1D], line_pick)
    lane = iota((BINS_2D, PAIR), 1)
    bucket = jnp.clip(lane - 64, -32, 31) + 32
    plane_pick = (bucket == iota((BINS_2D, PAIR), 0)).astype(BF16)
    bases = [
        dot(tab_ref[:, BINS_1D + 64 * plane : BINS_1D + 64 * plane + 64], plane_pick)
        for plane in range(2)
    ]
    first = first_lanes()
    zeros = jnp.zeros((64, PAIR), BF16)
    for h in range(HL):
        spread = jnp.broadcast_to(line_base[h : h + 1, :], (SUB, 768))
        rolled = pltpu.roll(spread, 0, 1, stride=1, stride_axis=0)
        z_ref[h] = rolled[:, :640]
        for plane in range(2):
            spread = jnp.broadcast_to(bases[plane][h : h + 1, :], (64, PAIR))
            for below in range(2):
                one = pltpu.roll(spread, 64 + below, 1, stride=1, stride_axis=0)
                both = jnp.where(first, one, pltpu.roll(one, 64, 1)).astype(BF16)
                start = h * 512 + plane * 256 + below * 128
                m_ref[plane * 64 : plane * 64 + 64, start : start + 128] = both
                m_ref[64 - plane * 64 : 128 - plane * 64, start : start + 128] = zeros
    box_scr[...] = jnp.full((8, KEYS), -1, jnp.int32)
    box_scr[0:2, 0:SEQ] = boxes_ref[...]
    row = iota((512, KEYS), 0)
    value = 8 * (row % 64) + row // 64
    for plane in range(2):
        o_ref[plane * 512 : plane * 512 + 512, :] = (
            value == box_scr[plane : plane + 1, :]
        ).astype(F32).astype(BF16)
    turned = jnp.transpose(box_scr[...].astype(F32))[0:ROWS, :].astype(jnp.int32)
    left = jnp.broadcast_to(turned[:, 0:1], (ROWS, PAIR))
    right = jnp.broadcast_to(turned[:, 1:2], (ROWS, PAIR))
    lane = iota((ROWS, PAIR), 1)
    both = jnp.where(lane < 64, left, right)
    r_ref[0] = left & 7
    r_ref[1] = right & 7
    upper = lax.shift_right_logical(both, 3)
    inner = lane & 63
    u_ref[...] = (upper == inner).astype(F32).astype(BF16)
    ur_ref[...] = (63 - upper == inner).astype(F32).astype(BF16)


def make_tables(order, where, tab, boxes, wo):
    return order(
        tables_kernel,
        (where, tab, boxes, wo),
        [smem(), vmem()] + [hbm()] * 2,
        (
            sds((HL, SUB, 640), F32),
            sds((128, HL * 512), BF16),
            sds((1024, KEYS), BF16),
            sds((ROWS, PAIR), BF16),
            sds((2, ROWS, PAIR), jnp.int32),
            sds((DL // 2, D), F32),
            sds((ROWS, PAIR), BF16),
        ),
        [vmem()] * 7,
        us=20000,
        scratch_shapes=[
            pltpu.VMEM((8, KEYS), jnp.int32),
            pltpu.VMEM(boxes.shape, jnp.int32),
            pltpu.VMEM((DL // 2, D), BF16),
            pltpu.SemaphoreType.DMA((2,)),
        ],
        name="bias_tables",
    )


def copy_kernel(src, dst, scr, sems):
    for pair in ((src, scr), (scr, dst)):
        copy = pltpu.make_async_copy(*pair, sems.at[0])
        copy.start()
        copy.wait()


def pass_on(order, x):
    return order(
        copy_kernel,
        (x,),
        [anywhere()],
        (sds(x.shape, x.dtype),),
        [anywhere()],
        scratch_shapes=[pltpu.VMEM(x.shape, x.dtype), pltpu.SemaphoreType.DMA((1,))],
        name="pass_on",
    )[0]


def text_taps(text_ref, cols):
    taps = {}
    for dilate in range(3):
        for tap in range(3):
            shift = (tap - 1) * (dilate + 1)
            row = text_ref[dilate, tap : tap + 1, cols].astype(F32)
            taps[shift] = row if shift not in taps else taps[shift] + row
    return taps


def text_conv_block(win, taps, sign):
    total = win[8:40] * (taps[0] + 1.0)
    for shift in (-3, -2, -1, 1, 2, 3):
        start = 8 + sign * shift
        total = total + win[start : start + 32] * taps[shift]
    return total


def grid_masks(side):
    place = iota((208, PAIR), 0)
    row = jnp.floor((place.astype(F32) + 0.5) * (1.0 / side)).astype(jnp.int32)
    col = place - row * side
    return (place < side * side, col >= 1, col <= side - 2)


def patch_conv_cols(win, patch_ref, cols, side, sign):
    live, has_left, has_right = grid_masks(side)
    total = None
    for ds in (-1, 0, 1):
        part = None
        for dr in (-1, 0, 1):
            tap = 3 * (dr + 1) + ds + 1
            start = MARGIN + sign * (dr * side + ds)
            term = win[start : start + 208] * patch_ref[tap : tap + 1, cols].astype(F32)
            part = term if part is None else part + term
        if ds * sign == -1:
            part = jnp.where(has_left, part, 0.0)
        if ds * sign == 1:
            part = jnp.where(has_right, part, 0.0)
        total = part if total is None else total + part
    return jnp.where(live, total, 0.0)


def fill_patches(patch_scr, source, count):
    zero = jnp.zeros((MARGIN, D), F32)
    patch_scr[0:MARGIN, :] = zero
    patch_scr[MARGIN + 208 : MARGIN + 208 + MARGIN, :] = zero
    live = iota((208, PAIR), 0) < count
    for c in range(D // PAIR):
        cols = slice(c * PAIR, c * PAIR + PAIR)
        patch_scr[MARGIN : MARGIN + 208, cols] = jnp.where(live, source(cols), 0.0)


def load_page(x_ref, count, text_scr, patch_scr, raw_scr):
    zero8 = jnp.zeros((8, D), F32)
    text_scr[0:8, :] = zero8
    text_scr[520:528, :] = zero8
    for b in range(TEXT // 64):
        text_scr[8 + 64 * b : 72 + 64 * b, :] = x_ref[64 * b : 64 * b + 64, :].astype(F32)
    raw_scr[...] = jnp.zeros((208, D), F32)
    raw_scr[0 : SEQ - TEXT, :] = x_ref[TEXT:SEQ, :].astype(F32)
    fill_patches(patch_scr, lambda cols: raw_scr[:, cols], count)


PAGE_SCRATCH = [
    pltpu.VMEM((528, D), F32),
    pltpu.VMEM((208 + 2 * MARGIN, D), F32),
    pltpu.VMEM((208, D), F32),
]


def by_grid(count, patches):
    large = count == GRID_LARGE * GRID_LARGE

    @pl.when(large)
    def _():
        patches(GRID_LARGE)

    @pl.when(jnp.logical_not(large))
    def _():
        patches(GRID_SMALL)


def encode_kernel(
    count_ref, x_hbm, text_ref, patch_ref, bias_ref, wq_hbm, wk_hbm, wv_hbm,
    q0, q1, q2, k_ref, v_ref, e0, e1, e2, l0, l1, l2,
    text_scr, patch_scr, raw_scr, x_ref, wq_ref, wk_ref, wv_ref, sems,
):
    copies = start_all(
        ((x_hbm, x_ref), (wq_hbm, wq_ref), (wk_hbm, wk_ref), (wv_hbm, wv_ref)), sems
    )
    count = count_ref[0]
    copies[0].wait()
    load_page(x_ref, count, text_scr, patch_scr, raw_scr)

    for c in range(2):
        cols = slice(c * 384, c * 384 + 384)
        taps = text_taps(text_ref, cols)

        def one(b, carry, cols=cols, taps=taps, out=None, first=0):
            base = pl.multiple_of(b * 32, 32)
            win = text_scr[pl.ds(first + base, 48), cols]
            out[pl.ds(base, 32), cols] = text_conv_block(win, taps, 1)
            return carry

        for (first, rows), out in zip(CHUNKS, (e0, e1)):
            lax.fori_loop(0, rows // 32, functools.partial(one, out=out, first=first), 0)

    def patches(side):
        for c in range(D // PAIR):
            cols = slice(c * PAIR, c * PAIR + PAIR)
            e2[:, cols] = raw_scr[:, cols] + patch_conv_cols(
                patch_scr[:, cols], patch_ref, cols, side, 1
            )

    by_grid(count, patches)
    for copy in copies[1:]:
        copy.wait()
    for (start, rows), e, low, q in zip(CHUNKS, (e0, e1, e2), (l0, l1, l2), (q0, q1, q2)):
        enc = e[...].astype(BF16)
        low[...] = enc
        query = (dot(enc, wq_ref[...]) + bias_ref[0:1, :]).astype(BF16)
        q[...] = query * jnp.asarray(0.125, BF16)
        k_ref[start : start + rows, :] = dot(enc, wk_ref[...]).astype(BF16)
        value = dot(enc, wv_ref[...]) + bias_ref[1:2, :]
        v_ref[start : start + rows, :] = value.astype(BF16)
    k_ref[ROWS:KEYS, :] = jnp.zeros((KEYS - ROWS, DL), BF16)
    v_ref[ROWS:KEYS, :] = jnp.zeros((KEYS - ROWS, DL), BF16)


def encode(order, count, x, text, patch, bias, wq, wk, wv, out):
    chunk = lambda width, dtype: tuple(sds((rows, width), dtype) for _, rows in CHUNKS)
    keys = (sds((KEYS, DL), BF16), sds((KEYS, DL), BF16))
    got, far = order(
        encode_kernel,
        (count, x, text, patch, bias, wq, wk, wv),
        [smem(), hbm()] + [vmem()] * 3 + [hbm()] * 3,
        chunk(DL, BF16) + keys + chunk(D, F32) + chunk(D, BF16),
        [vmem()] * 11,
        scratch_shapes=PAGE_SCRATCH
        + [pltpu.VMEM((SEQ, D), BF16)]
        + [pltpu.VMEM((D, DL), BF16)] * 3
        + [pltpu.SemaphoreType.DMA((4,))],
        mib=12,
        us=8000,
        out=out,
        name="encode_project",
    )
    return got[0:5], got[5:8], got[8:11], far


def bias_rows(e, r_col, k, rows):
    step = 2 * k + (iota((rows, PAIR), 1) >= 64).astype(jnp.int32)
    return jnp.where(step >= r_col, e[0], e[1]).astype(BF16)


def line_rows(z_ref, h, sub, rows):
    groups = [min(max(g - sub + 2, 0), 4) for g in range(KEYS // SUB)]
    return jnp.concatenate([z_ref[h, 0:rows, g * 128 : g * 128 + 128] for g in groups], axis=1)


def attend_kernel(
    start, rows, count_ref, q_ref, k_ref, v_ref, u_ref, r_ref, m_ref, o_ref, z_ref,
    p_ref, mix_ref, low_ref,
):
    live = iota((1, KEYS), 1) < TEXT + count_ref[0]
    first = first_lanes()
    r_w = r_ref[0, start : start + rows, :]
    r_h = r_ref[1, start : start + rows, :]
    u = u_ref[start : start + rows, :]
    for pair in range(HL // 2):
        cols = slice(pair * PAIR, pair * PAIR + PAIR)
        q = q_ref[:, cols]
        k = k_ref[:, cols]
        v = v_ref[:, cols]
        mixed = []
        for half in range(2):
            h = 2 * pair + half
            mine = first if half == 0 else jnp.logical_not(first)
            qm = jnp.where(mine, q, jnp.zeros_like(q))
            e = dot(u, m_ref[:, h * 512 : h * 512 + 512])
            parts = [bias_rows((e[:, 0:128], e[:, 128:256]), r_w, kk, rows) for kk in range(4)]
            parts += [bias_rows((e[:, 256:384], e[:, 384:512]), r_h, kk, rows) for kk in range(4)]
            picked = jnp.concatenate(parts, axis=1)
            s = dot(picked, o_ref[...]) + dot_nt(qm, k)
            pieces = []
            for at in range(0, rows, SUB):
                size = min(SUB, rows - at)
                pieces.append(line_rows(z_ref, h, (start + at) // SUB, size))
            s = s + jnp.concatenate(pieces, axis=0)
            s = jnp.where(live, s, NEG)
            top = jnp.max(s, axis=1, keepdims=True)
            ex = jnp.exp(s - top)
            total = jnp.sum(ex, axis=1, keepdims=True)
            prob = (ex * (1.0 / total)).astype(BF16)
            p_ref[h] = prob
            mixed.append(dot(prob, v))
        low = jnp.where(first, mixed[0], mixed[1]).astype(BF16)
        low_ref[:, cols] = low
        mix_ref[:, cols] = low.astype(F32)


def attend(order, c, count, q, k, v, u, r, m, o, z, out):
    start, rows = CHUNKS[c]
    return order(
        functools.partial(attend_kernel, start, rows),
        (count, q, k, v, u, r, m, o, z),
        [smem()] + [vmem()] * 8,
        (sds((HL, rows, KEYS), BF16), sds((rows, DL), F32), sds((rows, DL), BF16)),
        [vmem()] * 3,
        out=out,
        name=f"attend_{c}",
    )


def feed_kernel(
    where_ref, own_ref, other_ref, enc_hbm, vec_ref, wo_ref, wo_a_ref, wo_b_ref, wi_ref, bi_ref,
    w2_ref, xhat_ref, rstd_ref, hlow_ref, act_ref, slope_ref, part_ref, enc_ref, sems,
):
    (copy,) = start_all(((enc_hbm, enc_ref),), sems)
    half = where_ref[0]
    core = where_ref[1]
    own = dot(own_ref[...].astype(BF16), wo_ref[...])
    other = other_ref[...].astype(BF16)
    low = jnp.where(core == 0, wo_a_ref[...], wo_b_ref[...]).astype(BF16)
    high = jnp.where(core == 0, wo_b_ref[...], wo_a_ref[...]).astype(BF16)
    other = dot(other, jnp.concatenate([low, high], axis=0))
    attended = jnp.where(half == 0, own, other) + jnp.where(half == 0, other, own)
    copy.wait()
    v = enc_ref[...] + (attended + vec_ref[0:1, :])
    centre = v - jnp.mean(v, axis=1, keepdims=True)
    rstd = lax.rsqrt(jnp.mean(centre * centre, axis=1, keepdims=True) + EPS)
    xhat = centre * rstd
    xhat_ref[...] = xhat
    rstd_ref[...] = jnp.broadcast_to(rstd, rstd_ref.shape)
    hlow = (xhat * vec_ref[1:2, :] + vec_ref[2:3, :]).astype(BF16)
    hlow_ref[...] = hlow
    total = None
    for n in range(FL // 512):
        cols = slice(n * 512, n * 512 + 512)
        pre = dot(hlow, wi_ref[:, cols]) + bi_ref[0:1, cols]
        gate = 0.5 + 0.5 * lax.erf(pre * 0.7071067811865476)
        slope_ref[:, cols] = gate + pre * (0.3989422804014327 * jnp.exp(-0.5 * pre * pre))
        act = (pre * gate).astype(BF16)
        act_ref[:, cols] = act
        term = dot(act, w2_ref[cols, :])
        total = term if total is None else total + term
    part_ref[...] = total


def feed(order, c, where, own, other, enc, vec, wo, wo_a, wo_b, wi, bi, w2, out):
    _, rows = CHUNKS[c]
    return order(
        feed_kernel,
        (where, own, other, enc, vec, wo, wo_a, wo_b, wi, bi, w2),
        [smem()] + [vmem()] * 2 + [hbm()] + [vmem()] * 7,
        (
            sds((rows, D), F32),
            sds((rows, 128), F32),
            sds((rows, D), BF16),
            sds((rows, FL), BF16),
            sds((rows, FL), F32),
            sds((rows, D), F32),
        ),
        [vmem()] * 6,
        scratch_shapes=[pltpu.VMEM((rows, D), F32), pltpu.SemaphoreType.DMA((1,))],
        out=out,
        name=f"feed_{c}",
    )


def norm_back(dy, xhat, rstd, gain):
    dxh = dy * gain
    return rstd * (
        dxh
        - jnp.mean(dxh, axis=1, keepdims=True)
        - xhat * jnp.mean(dxh * xhat, axis=1, keepdims=True)
    )


def col_sum(x):
    return jnp.sum(x, axis=0, keepdims=True)


def feed_back_kernel(
    start, rows, first, count_ref, own_ref, other_ref, xhat1_ref, cot_ref, vec_ref, w2_ref,
    slope_ref, wi_ref, *rest,
):
    if not first:
        rest = rest[1:]
    out_ref, dres_ref, g2_ref, g1_ref, part_ref, sums_ref = rest
    place = start + iota((rows, 1), 0)
    live = place < TEXT + count_ref[0]
    hidden = xhat1_ref[...] * vec_ref[1:2, :] + vec_ref[2:3, :]
    v = hidden + ((own_ref[...] + other_ref[...]) + vec_ref[3:4, :])
    centre = v - jnp.mean(v, axis=1, keepdims=True)
    rstd = lax.rsqrt(jnp.mean(centre * centre, axis=1, keepdims=True) + EPS)
    xhat = centre * rstd
    y = xhat * vec_ref[4:5, :] + vec_ref[5:6, :]
    out_ref[0:rows, :] = jnp.where(live, y, 0.0).astype(BF16)
    dy = jnp.where(live, cot_ref[0:rows, :].astype(F32), 0.0)
    sums_ref[...] = jnp.zeros(sums_ref.shape, F32)
    sums_ref[2:3, 0:D] = col_sum(dy * xhat)
    sums_ref[3:4, 0:D] = col_sum(dy)
    dres = norm_back(dy, xhat, rstd, vec_ref[4:5, :])
    dres_ref[...] = dres
    sums_ref[1:2, 0:D] = col_sum(dres)
    g2 = dres.astype(BF16)
    g2_ref[...] = g2
    total = None
    for n in range(FL // 512):
        cols = slice(n * 512, n * 512 + 512)
        d_inner = dot_nt(g2, w2_ref[cols, :]) * slope_ref[:, cols]
        sums_ref[0:1, cols] = col_sum(d_inner)
        g1 = d_inner.astype(BF16)
        g1_ref[:, cols] = g1
        term = dot_nt(g1, wi_ref[:, cols])
        total = term if total is None else total + term
    part_ref[...] = total


def feed_back(order, c, count, own, other, xhat1, cot, vec, w2, slope, wi, out_so_far):
    start, rows = CHUNKS[c]
    high = 256 if start == TEXT else rows
    block = pl.BlockSpec((high, D), lambda i: (start // high, 0))
    whole = lambda a: pl.BlockSpec(a.shape, lambda i: (0, 0))
    shapes = (
        sds((SEQ, D), BF16),
        sds((rows, D), F32),
        sds((rows, D), BF16),
        sds((rows, FL), BF16),
        sds((rows, D), F32),
        sds((8, FL), F32),
    )
    operands = [count, own, other, xhat1, cot, vec, w2, slope, wi]
    specs = [smem()] + [vmem()] * 3 + [block] + [vmem()] * 4
    aliases = {}
    if out_so_far is not None:
        operands.append(out_so_far)
        specs.append(anywhere())
        aliases = {9: 0}
    return order(
        functools.partial(feed_back_kernel, start, rows, out_so_far is None),
        operands,
        specs,
        shapes,
        [block] + [vmem()] * 5,
        grid=(1,),
        input_output_aliases=aliases,
        name=f"feed_back_{c}",
    )


def store_slabs(slab, core, grad, keep_ref, send_ref):
    for i in range(D // (2 * slab)):
        even = grad[2 * i * slab : (2 * i + 1) * slab]
        odd = grad[(2 * i + 1) * slab : (2 * i + 2) * slab]
        keep_ref[i * slab : (i + 1) * slab, :] = jnp.where(core == 0, even, odd)
        send_ref[i * slab : (i + 1) * slab, :] = jnp.where(core == 0, odd, even)


def tn_sum(lefts, rights):
    total = None
    for left, right in zip(lefts, rights):
        term = dot_tn(left[...], right[...].astype(BF16))
        total = term if total is None else total + term
    return total


def put_grads(slab, where_ref, grad, outs):
    if slab is None:
        outs[0][...] = grad
    else:
        store_slabs(slab, where_ref[1], grad, *outs)


def chunk_grads_kernel(slab, has_total, where_ref, left_ref, right_ref, *refs):
    grad = dot_tn(left_ref[...], right_ref[...])
    if has_total:
        grad = refs[0][...] + grad
    put_grads(slab, where_ref, grad, refs[has_total:])


def chunk_grads(order, slab, where, left, right, total, last, name):
    width = right.shape[1]
    block = 512
    piece = lambda rows: pl.BlockSpec((rows, block), lambda i: (0, i))
    whole = pl.BlockSpec(left.shape, lambda i: (0, 0))
    apart = last and slab is not None
    rows, count = (D // 2, 2) if apart else (D, 1)
    operands, specs, aliases = [where, left, right], [smem(), whole, piece(right.shape[0])], {}
    if total is not None:
        operands.append(total)
        specs.append(piece(D))
        if not apart:
            aliases = {3: 0}
    return order(
        functools.partial(chunk_grads_kernel, slab if apart else None, total is not None),
        operands,
        specs,
        (sds((rows, width), F32),) * count,
        [piece(rows)] * count,
        grid=(width // block,),
        input_output_aliases=aliases,
        mib=16,
        name=name,
    )


SPLIT = 768


def attention_grads_kernel(slab, where_ref, *refs):
    low, dq, (dk_ref, dv_ref), g0, mix = refs[0:3], refs[3:6], refs[6:8], refs[8:11], refs[11:14]
    chunks = lambda ref: [ref.at[start : start + rows] for start, rows in CHUNKS]
    todo = ((low, dq), (low, chunks(dk_ref)), (low, chunks(dv_ref)), (g0, mix))
    one = lambda refs: jnp.concatenate([ref[...].astype(BF16) for ref in refs], axis=0)
    wide = jnp.concatenate([one(rights) for _, rights in todo[0:3]], axis=1)
    wide = dot_tn(one(low), wide)
    grads = [wide[:, i * DL : i * DL + DL] for i in range(3)] + [dot_tn(one(g0), one(mix))]
    for i, grad in enumerate(grads):
        first, last = i * DL, i * DL + DL
        for part, (low_end, high_end) in enumerate(((0, SPLIT), (SPLIT, 4 * DL))):
            begin, end = max(first, low_end), min(last, high_end)
            if begin < end:
                cols = slice(begin - low_end, end - low_end)
                outs = [ref.at[:, cols] for ref in refs[14 + 2 * part : 16 + 2 * part]]
                store_slabs(slab, where_ref[1], grad[:, begin - first : end - first], *outs)


def attention_grads(order, slab, where, enc_low, dq, dk, dv, g0, mix):
    operands = [*enc_low, *dq, dk, dv, *g0, *mix]
    widths = (SPLIT, SPLIT, 4 * DL - SPLIT, 4 * DL - SPLIT)
    return order(
        functools.partial(attention_grads_kernel, slab),
        (where, *operands),
        [smem()] + [vmem()] * len(operands),
        [sds((D // 2, width), F32) for width in widths],
        [vmem()] * 4,
        name="attention_grads",
    )


def plain_grads_kernel(*refs):
    low, dq, (dk_ref, dv_ref), g0, mix = refs[0:3], refs[3:6], refs[6:8], refs[8:11], refs[11:14]
    chunks = lambda ref: [ref.at[start : start + rows] for start, rows in CHUNKS]
    todo = ((low, dq), (low, chunks(dk_ref)), (low, chunks(dv_ref)), (g0, mix))
    for i, (lefts, rights) in enumerate(todo):
        refs[14][:, i * DL : i * DL + DL] = tn_sum(lefts, rights)


def plain_grads(order, enc_low, dq, dk, dv, g0, mix):
    operands = [*enc_low, *dq, dk, dv, *g0, *mix]
    return order(
        plain_grads_kernel, operands, [vmem()] * len(operands), (sds((D, 4 * DL), F32),), [vmem()],
        name="plain_grads",
    )


def halve_kernel(slabs, high, where_bit, count, extra, where_ref, *refs):
    *smalls, a_ref, b_ref, own_ref, out_ref = refs
    mine = where_ref[where_bit]
    total = a_ref.shape[0] - (extra if count == 0 else 0)
    run = high * (total // slabs)
    for i in range(slabs // (2 * high)):
        for ref, which in ((own_ref, mine), (out_ref, 1 - mine)):
            rows = pl.ds(pl.multiple_of((2 * i + which) * run, 8), run)
            ref[i * run : (i + 1) * run, :] = a_ref[rows, :] + b_ref[rows, :]
    if extra == 0:
        return
    width = D
    small = a_ref[total:, 0:width] + b_ref[total:, 0:width] if count == 0 else smalls[0][...]
    for ref in smalls[1:]:
        small = small + ref[...]
    for ref in (own_ref, out_ref):
        ref[total // 2 :, 0:width] = small
        if ref.shape[1] > width:
            rest = (extra, ref.shape[1] - width)
            ref[total // 2 :, width:] = jnp.zeros(rest, F32)


def halve(order, where, pair, slabs, high, where_bit, first, width, name, smalls=(), extra=0):
    rows = pair[0].shape[0]
    total = rows - (0 if smalls else extra)
    if extra == 0:
        block = 512 if width % 512 == 0 and first % 512 == 0 else 384
    else:
        block = width
    at = first // block
    out_rows = total // 2 + extra
    half = pl.BlockSpec((out_rows, block), lambda i: (0, i))
    return order(
        functools.partial(halve_kernel, slabs, high, where_bit, len(smalls), extra),
        [where, *smalls, *pair],
        [smem()]
        + [pl.BlockSpec(a.shape, lambda i: (0, 0)) for a in smalls]
        + [pl.BlockSpec((rows, block), lambda i: (0, at + i))] * 2,
        (sds((out_rows, width), F32),) * 2,
        [half, half],
        grid=(width // block,),
        mib=12,
        name=name,
    )


def norm_back_kernel(
    dres2_ref, own_ref, other_ref, xhat_ref, rstd_ref, vec_ref, wo_ref,
    dres1_far, g0_ref, dmix_ref, sums_ref, dres1_ref, sems,
):
    dhid = dres2_ref[...] + (own_ref[...] + other_ref[...])
    xhat = xhat_ref[...]
    sums_ref[...] = jnp.zeros(sums_ref.shape, F32)
    sums_ref[1:2, :] = col_sum(dhid * xhat)
    sums_ref[2:3, :] = col_sum(dhid)
    dres1 = norm_back(dhid, xhat, rstd_ref[:, 0:1], vec_ref[1:2, :])
    dres1_ref[...] = dres1
    (copy,) = start_all(((dres1_ref, dres1_far),), sems)
    sums_ref[0:1, :] = col_sum(dres1)
    g0 = dres1.astype(BF16)
    g0_ref[...] = g0
    dmix_ref[...] = dot_nt(g0, wo_ref[...]).astype(BF16)
    copy.wait()


def norm_one_back(order, c, dres2, own, other, xhat, rstd, vec, wo):
    _, rows = CHUNKS[c]
    return order(
        norm_back_kernel,
        (dres2, own, other, xhat, rstd, vec, wo),
        [vmem()] * 7,
        (sds((rows, D), F32), sds((rows, D), BF16), sds((rows, DL), BF16), sds((8, D), F32)),
        [hbm()] + [vmem()] * 3,
        scratch_shapes=[pltpu.VMEM((rows, D), F32), pltpu.SemaphoreType.DMA((1,))],
        us=20000 if c == ORDER[0] else 1,
        name=f"norm_back_{c}",
    )


def attend_back_kernel(
    start, rows, first, dmix_ref, p_ref, q_ref, k_ref, v_ref, ur_ref, r_ref, o_ref, *rest,
):
    if not first:
        dk_in, dv_in, dm_in, dz_in = rest[:4]
        rest = rest[4:]
    dq_ref, dk_ref, dv_ref, dm_ref, dz_ref = rest
    if first:
        dz_ref[...] = jnp.zeros(dz_ref.shape, F32)
    else:
        dz_ref[...] = dz_in[...]

    lanes = first_lanes()
    r_w = r_ref[0, start : start + rows, :]
    r_h = r_ref[1, start : start + rows, :]
    upper = (iota((rows, PAIR), 1) >= 64).astype(jnp.int32)
    ur = ur_ref[start : start + rows, :]
    pick = lambda h, a: jnp.where(
        lanes if h % 2 == 0 else jnp.logical_not(lanes), a, jnp.zeros_like(a)
    )
    pair_cols = lambda h: slice(h // 2 * PAIR, h // 2 * PAIR + PAIR)

    def dprob_of(h):
        return dot_nt(pick(h, dmix_ref[:, pair_cols(h)]), v_ref[:, pair_cols(h)])

    def back_of(h, dprob):
        cols = pair_cols(h)
        prob = p_ref[h]
        prob_f = prob.astype(F32)
        both = prob_f * dprob
        ds = both - prob_f * jnp.sum(both, axis=1, keepdims=True)
        low = ds.astype(BF16)
        dq = dot(low, pick(h, k_ref[:, cols]))
        dk = dot_tn(low, pick(h, q_ref[:, cols]))
        dv = dot_tn(prob, pick(h, dmix_ref[:, cols]))
        dbias = dot_nt(low, o_ref[...])
        for at in range(0, rows, SUB):
            size = min(SUB, rows - at)
            sub = (start + at) // SUB
            sums = {}
            for g in range(KEYS // SUB):
                group = min(max(g - sub + 2, 0), 4)
                piece = ds[at : at + size, g * 128 : g * 128 + 128]
                sums[group] = piece if group not in sums else sums[group] + piece
            for group, piece in sums.items():
                dz_ref[h, 0:size, group * 128 : group * 128 + 128] += piece
        return dq, dk, dv, dbias

    def table_of(h, dbias):
        parts = []
        for plane, r_col in ((0, r_w), (1, r_h)):
            same = None
            total = None
            for kk in range(4):
                base = plane * 512 + kk * 128
                piece = dbias[:, base : base + 128]
                yes = jnp.where((2 * kk + upper) >= r_col, piece, 0.0)
                same = yes if same is None else same + yes
                total = piece if total is None else total + piece
            parts += [same, total - same]
        dm = dot_tn(ur, jnp.concatenate(parts, axis=1).astype(BF16))
        at = slice(h * 512, h * 512 + 512)
        dm_ref[:, at] = dm if first else dm_in[:, at] + dm

    dprob = dprob_of(0)
    totals = None
    for h in range(HL):
        following = dprob_of(h + 1) if h + 1 < HL else None
        dq, dk, dv, dbias = back_of(h, dprob)
        dprob = following
        cols = pair_cols(h)
        if h % 2 == 0:
            totals = (dq, dk, dv)
        else:
            dq_ref[:, cols] = (totals[0] + dq) * 0.125
            dk = totals[1] + dk
            dv = totals[2] + dv
            dk_ref[:, cols] = dk if first else dk_in[:, cols] + dk
            dv_ref[:, cols] = dv if first else dv_in[:, cols] + dv
        table_of(h, dbias)


def attend_back(order, c, dmix, p, q, k, v, ur, r, o, carry, into):
    start, rows = CHUNKS[c]
    operands = [dmix, p, q, k, v, ur, r, o]
    aliases = {}
    if carry is not None:
        operands += list(carry)
        aliases = {8 + i: 1 + i for i in range(4)}
    return order(
        functools.partial(attend_back_kernel, start, rows, carry is None),
        operands,
        [vmem()] * len(operands),
        (
            sds((rows, DL), F32),
            sds((KEYS, DL), F32),
            sds((KEYS, DL), F32),
            sds((128, HL * 512), F32),
            sds((HL, SUB, 640), F32),
        ),
        [vmem()] * 5,
        input_output_aliases=aliases,
        into=into,
        name=f"attend_back_{c}",
    )


def table_sums_kernel(dm_ref, dz_ref, out_ref):
    lane = iota((PAIR, BINS_2D), 0)
    plane_bin = jnp.clip(lane - 64, -32, 31) + 32
    plane_pick = (plane_bin == iota((PAIR, BINS_2D), 1)).astype(F32)
    lane = iota((512, BINS_1D), 0)
    line_bin = jnp.clip(lane - 256, -16, 15) + 16
    line_pick = (line_bin == iota((512, BINS_1D), 1)).astype(F32)
    first = first_lanes()
    flip = (iota((SUB, SUB), 0) + iota((SUB, SUB), 1) == SUB - 1).astype(F32)
    bin_id = iota((1, BINS_1D), 1)
    exact = functools.partial(
        lax.dot_general,
        dimension_numbers=(((1,), (0,)), ((), ())),
        precision=HIGHEST,
        preferred_element_type=F32,
    )
    out_ref[...] = jnp.zeros(out_ref.shape, F32)
    for h in range(HL):
        z = dz_ref[h]
        left = jnp.sum(z[:, 0:128])
        right = jnp.sum(z[:, 512:640])
        band = jnp.concatenate([z[:, 128:512], jnp.zeros((SUB, 128), F32)], axis=1)
        band = pltpu.roll(exact(flip, band), 512 - 127 + 128, 1, stride=1, stride_axis=0)
        line = exact(col_sum(band), line_pick)
        line = line + jnp.where(bin_id == 0, left, 0.0) + jnp.where(bin_id == 31, right, 0.0)
        out_ref[h : h + 1, 0:BINS_1D] = line
        for plane in range(2):
            total = None
            for below in range(2):
                at = h * 512 + plane * 256 + below * 128
                g = dm_ref[plane * 64 : plane * 64 + 64, at : at + 128]
                g = jnp.where(first, g + pltpu.roll(g, 64, 1), 0.0)
                g = pltpu.roll(g, 1 - below, 1, stride=1, stride_axis=0)
                total = g if total is None else total + g
            summed = exact(col_sum(total), plane_pick)
            at = BINS_1D + plane * 64
            out_ref[h : h + 1, at : at + 64] = summed


def table_sums(order, dm, dz):
    return order(
        table_sums_kernel,
        (dm, dz),
        [vmem()] * 2,
        (sds((8, 256), F32),),
        [vmem()],
        name="table_sums",
    )[0]


def project_back_kernel(
    q0, q1, q2, dk_ref, dv_ref, wq_ref, wk_ref, wv_ref, part_ref, bias_ref,
):
    sum_q = None
    sum_v = None
    for (start, rows), dq in zip(CHUNKS, (q0, q1, q2)):
        query = dq[...]
        value = dv_ref[start : start + rows, :]
        sum_q = col_sum(query) if sum_q is None else sum_q + col_sum(query)
        sum_v = col_sum(value) if sum_v is None else sum_v + col_sum(value)
        query = query.astype(BF16)
        key = dk_ref[start : start + rows, :].astype(BF16)
        value = value.astype(BF16)
        part_ref[start : start + rows, :] = (
            dot_nt(query, wq_ref[...]) + dot_nt(key, wk_ref[...]) + dot_nt(value, wv_ref[...])
        )
    bias_ref[...] = jnp.zeros(bias_ref.shape, F32)
    bias_ref[0:1, 0:DL] = sum_q
    bias_ref[0:1, DL:D] = sum_v


def project_back(order, dq, dk, dv, wq, wk, wv):
    return order(
        project_back_kernel,
        (*dq, dk, dv, wq, wk, wv),
        [vmem()] * 8,
        (sds((ROWS, D), F32), sds((8, D), F32)),
        [vmem()] * 2,
        us=15000,
        name="project_back",
    )


def taps_kernel(
    count_ref, x_hbm, pt, r0_far, r1_far, r2_far, out_ref,
    text_scr, patch_scr, raw_scr, x_ref, r0, r1, r2, sems,
):
    count = count_ref[0]
    copies = start_all(((x_hbm, x_ref), (r0_far, r0), (r1_far, r1), (r2_far, r2)), sems)
    copies[0].wait()
    load_page(x_ref, count, text_scr, patch_scr, raw_scr)
    for copy in copies[1:]:
        copy.wait()
    out_ref[...] = jnp.zeros(out_ref.shape, F32)
    shifts = tuple(range(-3, 4))
    for c in range(2):
        cols = slice(c * 384, c * 384 + 384)

        def one(b, sums, cols=cols, res=None, first=0):
            base = pl.multiple_of(b * 32, 32)
            win = text_scr[pl.ds(first + base, 48), cols]
            grad = pt[pl.ds(first + base, 32), cols] + 0.5 * res[pl.ds(base, 32), cols]
            out = []
            for shift, total in zip(shifts, sums):
                prod = grad * win[8 + shift : 40 + shift]
                out.append(total + jnp.sum(prod.reshape(4, 8, 384), axis=0))
            return tuple(out)

        sums = tuple(jnp.zeros((8, 384), F32) for _ in shifts)
        for (first, rows), res in zip(CHUNKS, (r0, r1)):
            sums = lax.fori_loop(
                0, rows // 32, functools.partial(one, res=res, first=first), sums
            )
        for row, total in enumerate(sums):
            out_ref[row : row + 1, cols] = col_sum(total)

    def patches(side):
        live, has_left, has_right = grid_masks(side)
        for c in range(D // PAIR):
            cols = slice(c * PAIR, c * PAIR + PAIR)
            win = patch_scr[:, cols]
            grad = jnp.where(live, pt[TEXT:ROWS, cols] + 0.5 * r2[:, cols], 0.0)
            for ds in (-1, 0, 1):
                masked = grad
                if ds == -1:
                    masked = jnp.where(has_left, grad, 0.0)
                if ds == 1:
                    masked = jnp.where(has_right, grad, 0.0)
                for dr in (-1, 0, 1):
                    row = 7 + 3 * (dr + 1) + ds + 1
                    at = MARGIN + dr * side + ds
                    out_ref[row : row + 1, cols] = col_sum(masked * win[at : at + 208])

    by_grid(count, patches)


def tap_sums(order, count, x, part, res):
    return order(
        taps_kernel,
        (count, x, part, *res),
        [smem(), hbm(), vmem()] + [hbm()] * 3,
        (sds((16, D), F32),),
        [vmem()],
        scratch_shapes=PAGE_SCRATCH
        + [pltpu.VMEM((SEQ, D), BF16)]
        + [pltpu.VMEM((rows, D), F32) for _, rows in CHUNKS]
        + [pltpu.SemaphoreType.DMA((4,))],
        mib=14,
        name="tap_sums",
    )[0]


def decode_text_kernel(text_ref, p, s, r0, r1, out_ref, text_scr):
    zero8 = jnp.zeros((8, D), F32)
    text_scr[0:8, :] = zero8
    text_scr[520:528, :] = zero8
    for r, (at, rows) in zip((r0, r1), CHUNKS):
        for b in range(rows // 64):
            res = r[64 * b : 64 * b + 64, :]
            here = slice(at + 64 * b, at + 64 * b + 64)
            text_scr[8 + at + 64 * b : 72 + at + 64 * b, :] = res + (p[here, :] + s[here, :])
    for c in range(2):
        cols = slice(c * 384, c * 384 + 384)
        taps = text_taps(text_ref, cols)

        def one(b, carry, cols=cols, taps=taps):
            base = pl.multiple_of(b * 32, 32)
            win = text_scr[pl.ds(base, 48), cols]
            out_ref[pl.ds(base, 32), cols] = text_conv_block(win, taps, -1).astype(BF16)
            return carry

        lax.fori_loop(0, TEXT // 32, one, 0)


def decode_kernel(
    count_ref, text_ref, patch_ref, p_far, s_far, r0_far, r1_far, r2_far, out_ref,
    text_scr, patch_scr, raw_scr, p, s, r0, r1, r2, sems,
):
    pairs = ((p_far, p), (s_far, s), (r0_far, r0), (r1_far, r1), (r2_far, r2))
    for copy in start_all(pairs, sems):
        copy.wait()
    decode_text_kernel(text_ref, p, s, r0, r1, out_ref, text_scr)
    count = count_ref[0]
    raw_scr[...] = r2[...] + (p[TEXT:ROWS, :] + s[TEXT:ROWS, :])
    fill_patches(patch_scr, lambda cols: raw_scr[:, cols], count)

    def patches(side):
        for c in range(D // PAIR):
            cols = slice(c * PAIR, c * PAIR + PAIR)
            total = raw_scr[:, cols] + patch_conv_cols(patch_scr[:, cols], patch_ref, cols, side, -1)
            out_ref[TEXT:SEQ, cols] = total[0 : SEQ - TEXT].astype(BF16)

    by_grid(count, patches)


def decode(order, count, text_w, patch_w, part, other, res):
    return order(
        decode_kernel,
        (count, text_w, patch_w, part, other, *res),
        [smem()] + [vmem()] * 2 + [hbm()] * 5,
        (sds((SEQ, D), BF16),),
        whole_blocks((sds((SEQ, D), BF16),)),
        grid=(1,),
        scratch_shapes=PAGE_SCRATCH
        + [pltpu.VMEM((ROWS, D), F32)] * 2
        + [pltpu.VMEM((rows, D), F32) for _, rows in CHUNKS]
        + [pltpu.SemaphoreType.DMA((5,))],
        mib=18,
        name="decode",
    )[0]


def swap_tensor(x):
    return lax.ppermute(x, "tensor", [(0, 1), (1, 0)])


def swap_dp(x, bit, dp):
    return lax.ppermute(x, "dp", [(i, i ^ bit) for i in range(dp)])


def swap_core(parts, dp):
    return (parts[0], swap_dp(parts[1], 1, dp)) if len(parts) == 2 else parts


class Scatter:
    def __init__(self, order, dp, where, pair, bits, name, first, width):
        self.order, self.dp, self.where, self.bits, self.name = order, dp, where, bits, name
        self.window = (first, width)
        self.pair = pair
        self.left = list(range(1, dp.bit_length() - 1))
        self.extra = 0

    def step(self, *smalls):
        if len(self.pair) == 1:
            return
        bit = self.bits[0]
        self.bits = self.bits[1:]
        at = self.left.index(bit)
        if smalls:
            self.extra = smalls[0].shape[0]
        own, out = halve(
            self.order, self.where, self.pair, 2 ** len(self.left), 2**at, 1 + bit, *self.window,
            f"{self.name}_{bit}", smalls, self.extra,
        )
        self.window = (0, self.window[1])
        self.left.remove(bit)
        self.pair = (own, swap_dp(out, 2**bit, self.dp))

    def total(self):
        first, width = self.window
        whole = self.pair[0][:, first : first + width]
        return lax.psum_scatter(whole, "dp", scatter_dimension=0, tiled=True)


def whole_blocks(shapes):
    return [pl.BlockSpec(a.shape, lambda i, n=len(a.shape): (0,) * n) for a in shapes]


EARLY = 8
LATE = 24


def total_of(order, part, name):
    return add_blocks(order, *part.pair, name)


def add_blocks(order, *pair_name):
    *pair, name = pair_name
    shapes = (sds(pair[0].shape, F32),)
    return order(
        add_kernel, pair, whole_blocks(pair), shapes, whole_blocks(shapes), grid=(1,), name=name
    )[0]


def add_kernel(a, b, out):
    out[...] = a[...] + b[...]


def add_here(order, a, b, name):
    return order(
        add_kernel, (a, b), [vmem()] * 2, (sds(a.shape, F32),), [vmem()], name=name
    )[0]


def joint_kernel(where_ref, sum_ref, a_ref, b_ref, own_ref, out_ref):
    mine = where_ref[4]
    slab = a_ref.shape[0] // 2
    width = a_ref.shape[1]
    for ref, which in ((own_ref, mine), (out_ref, 1 - mine)):
        rows = pl.ds(pl.multiple_of(which * slab, 8), slab)
        ref[0:slab, 0:D] = sum_ref[rows, :]
        ref[0:slab, D : D + width] = a_ref[rows, :] + b_ref[rows, :]
        ref[slab:, 0:D] = sum_ref[2 * slab :, :]
        ref[slab:, D : D + width] = jnp.zeros((EARLY, width), F32)


def joint_step(order, dp, where, summed, part):
    rows, width = part.pair[0].shape
    shapes = (sds((rows // 2 + EARLY, D + width), F32),) * 2
    operands = (summed, *part.pair)
    own, out = order(
        joint_kernel, (where, *operands), [smem()] + whole_blocks(operands), shapes,
        whole_blocks(shapes), grid=(1,), name="joint_3",
    )
    return own, swap_dp(out, 8, dp)


def last_totals_kernel(
    both, b0, b1, joint, ob, ia, q_ref, k_ref, v_ref, o_ref, outer_ref, inner_ref, small_ref,
):
    slab = q_ref.shape[0]
    q_ref[...] = both[0:slab, 0:DL]
    k_ref[...] = both[0:slab, DL:D]
    both = b0[...] + b1[...]
    v_ref[...] = both[0:slab, 0:DL]
    o_ref[...] = both[0:slab, DL:D]
    small_ref[0:LATE, :] = both[slab:, 0:D]
    split = joint.shape[1] - D
    outer_ref[:, 0:split] = joint[0:slab, D : D + split]
    outer_ref[:, split:FL] = ob[...]
    inner_ref[:, 0:D] = ia[...]
    inner_ref[:, D:FL] = joint[0:slab, 0:D]
    small_ref[LATE : LATE + EARLY, :] = joint[slab:, 0:D]


def last_totals(order, total_a, part_b, *rest):
    *rest, slab = rest
    operands = [total_a, *part_b.pair, *rest]
    plain = sds((slab, DL), F32)
    wide = sds((slab, FL), F32)
    shapes = (plain,) * 4 + (wide, wide, sds((LATE + EARLY, D), F32))
    return order(
        last_totals_kernel, operands, whole_blocks(operands), shapes, whole_blocks(shapes),
        grid=(1,), name="last_totals",
    )


def gather_early_kernel(f0, f1, f2, out):
    sums = f0[...] + f1[...] + f2[...]
    out[...] = jnp.zeros(out.shape, F32)
    out[0:1, :] = sums[0:1, 0:D]
    out[1:2, :] = sums[0:1, D:FL]
    out[2:5, :] = sums[1:4, 0:D]


def gather_early(order, sums, into):
    (early,), moved = order(
        gather_early_kernel, sums, [vmem()] * 3, (sds((EARLY, D), F32),), [vmem()], into=into,
        name="gather_early",
    )
    return early, moved


def gather_late_kernel(taps, a0, a1, a2, bias, tab, out):
    out[...] = jnp.zeros(out.shape, F32)
    out[0:16, :] = taps[0:16, :]
    out[16:19, :] = (a0[...] + a1[...] + a2[...])[0:3]
    out[19:20, :] = bias[0:1, :]
    for h in range(HL):
        at = 256 * (h % 3)
        out[20 + h // 3 : 21 + h // 3, at : at + 256] = tab[h : h + 1, :]


def gather_late(order, *rest):
    return order(
        gather_late_kernel, rest, [vmem()] * 6, (sds((LATE, D), F32),), [vmem()],
        name="gather_late",
    )[0]


def finish_kernel(
    place_ref, own, core, other, both,
    text, patch, out_b, gain1, shift1, outer_b, gain2, shift2,
    query_b, value_b, inner_b, line, width, height,
):
    small = own[...] + core[...]
    slab = patch.shape[1]
    turn = lambda a: pltpu.roll(a, lax.rem(D - place_ref[0] * slab, D), 1)[:, 0:slab]
    shard = turn(small)
    taps = shard[0:16] + turn(other[...] + both[...])
    for dilate in range(3):
        for tap in range(3):
            text[dilate, tap] = taps[3 + (tap - 1) * (dilate + 1)]
    patch[...] = taps[7:16]
    rows = (16, 17, 18, LATE + 2, LATE + 3, LATE + 4)
    for i, ref in zip(rows, (out_b, gain1, shift1, outer_b, gain2, shift2)):
        ref[...] = shard[i]
    query_b[...] = small[19, 0:DL]
    value_b[...] = small[19, DL:D]
    inner_b[0:D] = small[LATE]
    inner_b[D:FL] = small[LATE + 1]
    for h in range(HL):
        row, at = 20 + h // 3, 256 * (h % 3)
        line[h : h + 1, :] = small[row : row + 1, at : at + 32]
        width[h : h + 1, :] = small[row : row + 1, at + 32 : at + 96]
        height[h : h + 1, :] = small[row : row + 1, at + 96 : at + 160]


def finish(order, place, own, core, other, both, slab):
    f = lambda *shape: sds(shape, F32)
    shapes = (f(3, 3, slab), f(9, slab)) + (f(slab),) * 6
    shapes += (f(DL), f(DL), f(FL), f(HL, 32), f(HL, 64), f(HL, 64))
    return order(
        finish_kernel, (place, own, core, other, both),
        [smem()] + whole_blocks((own, core, other, both)), shapes, whole_blocks(shapes), grid=(1,),
        name="finish",
    )


def swap_both(x, dp):
    pairs = [(2 * i + t, 2 * (i ^ 1) + (t ^ 1)) for i in range(dp) for t in range(2)]
    return lax.ppermute(x, ("dp", "tensor"), pairs)


def per_device(
    dp,
    page_tokens,
    patch_counts,
    token_boxes,
    text_weight,
    patch_weight,
    query_weight,
    query_bias,
    key_weight,
    value_weight,
    value_bias,
    out_weight,
    out_bias,
    line_table,
    width_table,
    height_table,
    norm1_gain,
    norm1_shift,
    inner_weight,
    inner_bias,
    outer_weight,
    outer_bias,
    norm2_gain,
    norm2_shift,
    cotangent,
):
    place = lax.axis_index("dp")
    half = lax.axis_index("tensor")
    core = place % 2
    bits = [(place // 2**i) % 2 for i in range(4)]
    where = jnp.stack([half] + bits).astype(jnp.int32)
    x = page_tokens.reshape(SEQ, D)
    cot = cotangent.reshape(SEQ, D)
    slab = D // dp if dp == 16 else None
    order = Order()

    z, m, o, u, r, wo_mine, ur = make_tables(
        order,
        where,
        jnp.concatenate([jnp.transpose(a) for a in (line_table, width_table, height_table)], axis=1),
        token_boxes.reshape(2, SEQ),
        out_weight,
    )
    wo_a = swap_tensor(wo_mine)
    row = lax.broadcasted_iota(jnp.int32, (8, 1), 0)
    bias = jnp.where(row == 0, query_bias[None, :], value_bias[None, :]).astype(F32)
    (q0, q1, q2, k, v), enc, enc_low, (o_far, ur_far, r_far) = encode(
        order, patch_counts, x, text_weight, patch_weight, bias,
        query_weight, key_weight, value_weight, (o, ur, r),
    )
    q = (q0, q1, q2)

    vec = jnp.zeros((8, 1), F32)
    for i, a in enumerate(
        (out_bias, norm1_gain, norm1_shift, outer_bias, norm2_gain, norm2_shift)
    ):
        vec = jnp.where(row == i, a[None, :].astype(F32), vec)
    bi = jnp.broadcast_to(inner_bias[None, :].astype(F32), (8, FL))
    probs, mix, mix_low, mix_other = ([None] * 3 for _ in range(4))
    xhat, rstd, hlow, act, slope, outer, outer_other = ([None] * 3 for _ in range(7))

    def attention_of(c, out):
        (p, a, low), far = attend(order, c, patch_counts, q[c], k, v, u, r, m, o, z, out)
        mix[c], mix_other[c] = a, swap_tensor(a)
        return (p, low), far

    def feed_of(c, out=()):
        got = feed(
            order, c, where, mix[c], mix_other[c], enc[c], vec, out_weight, wo_a, wo_b,
            inner_weight, bi, outer_weight, out,
        )
        far = None
        if out:
            got, far = got
        for keep, a in zip((xhat, rstd, hlow, act, slope, outer), got):
            keep[c] = a
        outer_other[c] = swap_tensor(got[5])
        return far

    near, enc = attention_of(ORDER[0], enc)
    wo_a = pass_on(order, wo_a)
    wo_b = swap_dp(wo_a, 1, dp)
    near, (probs[ORDER[0]], mix_low[ORDER[0]]) = attention_of(ORDER[1], near)
    near, (probs[ORDER[1]], mix_low[ORDER[1]]) = attention_of(ORDER[2], near)
    probs[ORDER[2]], mix_low[ORDER[2]] = feed_of(ORDER[0], near)
    enc_low = feed_of(ORDER[1], enc_low)
    *q_far, k_far, v_far = feed_of(ORDER[2], (q0, q1, q2, k, v))
    layer_out, inner_grad, outer_grad = None, None, None
    dres2, g2, g1, dhid, dhid_other, sums2 = ([None] * 3 for _ in range(6))
    for c in ORDER:
        got = feed_back(
            order, c, patch_counts, outer[c], outer_other[c], xhat[c], cot, vec, outer_weight,
            slope[c], inner_weight, layer_out,
        )
        layer_out = got[0]
        for keep, a in zip((dres2, g2, g1, dhid, sums2), got[1:]):
            keep[c] = a
        dhid_other[c] = swap_tensor(got[4])
        last = c == ORDER[2]
        inner_grad = chunk_grads(
            order, slab, where, hlow[c], g1[c], inner_grad, last, f"inner_grads_{c}"
        )
        outer_grad = chunk_grads(
            order, slab, where, g2[c], act[c], outer_grad, last, f"outer_grads_{c}"
        )
        if not last:
            inner_grad, outer_grad = inner_grad[0], outer_grad[0]
    scatter = functools.partial(Scatter, order, dp, where)
    x_first, z_first = (1, 2, 3), (2, 3, 1)
    inner_pair, outer_pair = swap_core(inner_grad, dp), swap_core(outer_grad, dp)
    inner = scatter(inner_pair, x_first, "inner", 0, D)
    inner_b = scatter(inner_pair, x_first, "inner_b", D, D)
    outer_a = scatter(outer_pair, x_first, "outer_a", 0, D)
    outer_b = scatter(outer_pair, z_first, "outer_b", D, D)
    early, (prob,) = gather_early(order, sums2, (probs[ORDER[0]],))
    carry = None
    dres1, g0, dq, sums1 = ([None] * 3 for _ in range(4))
    for c in ORDER:
        got = norm_one_back(
            order, c, dres2[c], dhid[c], dhid_other[c], xhat[c], rstd[c], vec, out_weight
        )
        dres1[c], g0[c], _, sums1[c] = got
        if c == ORDER[0]:
            inner.step()
            outer_b.step()
            inner_b.step(early)
        if c == ORDER[1]:
            outer_a.step()
            inner.step()
            outer_b.step()
        if c == ORDER[2]:
            inner_b.step()
            inner.step()
            outer_b.step()
        into = [probs[after] for after in ORDER[ORDER.index(c) + 1 :][:1]]
        if not into:
            into = [query_weight, key_weight, value_weight]
        got = attend_back(
            order, c, got[2], prob, q_far[c], k_far, v_far, ur_far, r_far, o_far, carry, into
        )
        got, into = got
        prob = into[0]
        dq[c], *carry = got
    weights = into
    dk, dv, dm, dz = carry
    if dp == 16:
        total_outer_b = total_of(order, outer_b, "outer_b_total")
        total_inner = total_of(order, inner, "inner_total")
    outer_a.step()
    if dp == 16:
        inner_b = total_of(order, inner_b, "inner_b_sum")
    operands = (enc_low, dq, dk, dv, g0, mix_low)
    if dp == 16:
        got = attention_grads(order, slab, where, *operands)
        first_pair, second_pair = swap_core(got[0:2], dp), swap_core(got[2:4], dp)
    else:
        first_pair = second_pair = plain_grads(order, *operands)
    rest = 0 if dp == 16 else SPLIT
    part_a = scatter(first_pair, x_first, "part_a", 0, SPLIT)
    part_b = scatter(second_pair, x_first, "part_b", rest, 4 * DL - SPLIT)
    part, bias_sums = project_back(order, dq, dk, dv, *weights)
    part_other = swap_tensor(part)
    part_a.step()
    tables = table_sums(order, dm, dz)
    taps = tap_sums(order, patch_counts, x, part, dres1)
    late = gather_late(order, taps, *sums1, bias_sums, tables)
    if dp == 16:
        joint = joint_step(order, dp, where, inner_b, outer_a)
    part_b.step(late)
    part_a.step()
    if dp == 16:
        joint = add_blocks(order, *joint, "joint_total")
    part_a.step()
    part_b.step()
    if dp == 16:
        total_a = total_of(order, part_a, "part_a_total")
    part_b.step()
    input_grad = decode(order, patch_counts, text_weight, patch_weight, part, part_other, dres1)
    if dp == 16:
        grad_q, grad_k, grad_v, grad_o, sum_outer, inner_total, small = last_totals(
            order, total_a, part_b, joint, total_outer_b, total_inner, slab
        )
    else:
        inner_total = jnp.concatenate([inner.total(), inner_b.total()], axis=1)
        sum_outer = jnp.concatenate([outer_a.total(), outer_b.total()], axis=1)
        both = jnp.concatenate([part_a.total(), part_b.total()], axis=1)
        grad_q, grad_k, grad_v, grad_o = jnp.split(both, 4, axis=1)
        small = jnp.concatenate([late, early], axis=0)
        bit = 2
        while bit < dp:
            small = small + swap_dp(small, bit, dp)
            bit *= 2
    small_others = (
        swap_dp(small, 1, dp), swap_tensor(small[0:16]), swap_both(small[0:16], dp)
    )
    small = finish(
        order, jnp.reshape(place, (1,)).astype(jnp.int32), small, *small_others, D // dp
    )
    text, patch, out_b, gain1, shift1, outer_b, gain2, shift2 = small[:8]
    query_b, value_b, inner_b, line, width, height = small[8:]
    return (
        layer_out.reshape(1, SEQ, D),
        input_grad.reshape(1, SEQ, D),
        text,
        patch,
        grad_q,
        query_b,
        grad_k,
        grad_v,
        value_b,
        jnp.transpose(grad_o),
        out_b,
        jnp.transpose(line),
        jnp.transpose(width),
        jnp.transpose(height),
        gain1,
        shift1,
        inner_total,
        inner_b,
        jnp.transpose(sum_outer),
        outer_b,
        gain2,
        shift2,
    )


def solution(mesh):
    placed = (
        P("dp", None, None),
        P("dp"),
        P("dp", None, None),
        P(),
        P(),
        P(None, "tensor"),
        P("tensor"),
        P(None, "tensor"),
        P(None, "tensor"),
        P("tensor"),
        P("tensor", None),
        P(),
        P(None, "tensor"),
        P(None, "tensor"),
        P(None, "tensor"),
        P(),
        P(),
        P(None, "tensor"),
        P("tensor"),
        P("tensor", None),
        P(),
        P(),
        P(),
        P("dp", None, None),
    )
    return jax.shard_map(
        functools.partial(per_device, mesh.shape["dp"]),
        mesh=mesh,
        in_specs=placed,
        out_specs=(
            P("dp", None, None),
            P("dp", None, None),
            P(None, None, "dp"),
            P(None, "dp"),
            P("dp", "tensor"),
            P("tensor"),
            P("dp", "tensor"),
            P("dp", "tensor"),
            P("tensor"),
            P("tensor", "dp"),
            P("dp"),
            P(None, "tensor"),
            P(None, "tensor"),
            P(None, "tensor"),
            P("dp"),
            P("dp"),
            P("dp", "tensor"),
            P("tensor"),
            P("tensor", "dp"),
            P("dp"),
            P("dp"),
            P("dp"),
        ),
        check_vma=False,
    )
```

```python
import functools

import jax
import jax.numpy as jnp
from jax import lax
from jax.experimental import pallas as pl
from jax.experimental.pallas import tpu as pltpu
from jax.sharding import PartitionSpec as P

HEADS = 12
TEXT = 512
GRID_SMALL = 7
GRID_LARGE = 14
BINS_1D = 32
BINS_2D = 64
BIN_WIDTH = 8

F32 = jnp.float32
BF16 = jnp.bfloat16
EPS = 1e-05
NEG = -1000000000.0
HIGHEST = lax.Precision.HIGHEST

D = 768
SEQ = 708
ROWS = 720
KEYS = 768
CHUNKS = ((0, 256), (256, 256), (512, 208))
ORDER = (2, 0, 1)
SUB = 128
PAIR = 128
HL = 6
DL = 384
FL = 1536
MARGIN = 16
MIB = 1024 * 1024


def vmem():
    return pl.BlockSpec(memory_space=pltpu.VMEM)


def anywhere():
    return pl.BlockSpec(memory_space=pl.ANY)


def hbm():
    return pl.BlockSpec(memory_space=pltpu.HBM)


def smem():
    return pl.BlockSpec(memory_space=pltpu.SMEM)


def params(mib):
    return pltpu.CompilerParams(vmem_limit_bytes=mib * MIB)


def sds(shape, dtype):
    return jax.ShapeDtypeStruct(shape, dtype)


TOKEN = jax.ShapeDtypeStruct((8, 128), jnp.float32)


class Order:
    def __init__(self):
        self.token = None

    def __call__(
        self, kernel, operands, in_specs, out_shape, out_specs, mib=10, us=1, out=(), into=(),
        scratch_shapes=(), **more,
    ):
        operands, in_specs = list(operands), list(in_specs)
        count, outs, moved = len(operands), len(out_shape), len(out) + len(into)
        operands += [*out, *into]
        in_specs += [vmem()] * len(out) + [hbm()] * len(into)
        has_token = self.token is not None
        grid = "grid" in more
        token_spec = pl.BlockSpec(TOKEN.shape, lambda *i: (0, 0)) if grid else vmem()
        if has_token:
            operands.append(self.token)
            in_specs.append(token_spec)
        shapes = [sds(a.shape, a.dtype) for a in (*out, *into)]
        specs = [hbm()] * len(out) + [vmem()] * len(into)
        scratch_shapes = list(scratch_shapes)
        if moved:
            scratch_shapes.append(pltpu.SemaphoreType.DMA((moved,)))

        def body(*refs):
            rest = list(refs)
            sources = rest[count : count + moved]
            del rest[count : count + moved + has_token]
            at = count + outs
            targets = rest[at : at + moved]
            rest[at + moved][...] = jnp.zeros(TOKEN.shape, F32)
            del rest[at : at + moved + 1]
            copies = start_all(zip(sources, targets), rest.pop()) if moved else []
            kernel(*rest)
            for copy in copies:
                copy.wait()

        got = pl.pallas_call(
            body,
            out_shape=tuple(out_shape) + tuple(shapes) + (TOKEN,),
            in_specs=in_specs,
            out_specs=tuple(out_specs) + tuple(specs) + (token_spec,),
            scratch_shapes=scratch_shapes,
            compiler_params=params(mib),
            cost_estimate=cost(us),
            **more,
        )(*operands)
        self.token = got[-1]
        if moved:
            return got[:outs], got[outs:-1]
        return got[:-1]


def start_all(pairs, sems, first=0):
    copies = [
        pltpu.make_async_copy(src, dst, sems.at[first + i]) for i, (src, dst) in enumerate(pairs)
    ]
    for copy in copies:
        copy.start()
    return copies


def dot(a, b):
    return lax.dot_general(a, b, (((1,), (0,)), ((), ())), preferred_element_type=F32)


def dot_nt(a, b):
    return lax.dot_general(a, b, (((1,), (1,)), ((), ())), preferred_element_type=F32)


def dot_tn(a, b):
    return lax.dot_general(a, b, (((0,), (0,)), ((), ())), preferred_element_type=F32)


def cost(us):
    return pl.CostEstimate(flops=int(us * 1.0e6), bytes_accessed=int(us * 1.0e3), transcendentals=0)


def filled(x, rows):
    return jnp.concatenate([x, jnp.zeros((rows - x.shape[0], x.shape[1]), x.dtype)], axis=0)


def iota(shape, dim):
    return lax.broadcasted_iota(jnp.int32, shape, dim)


def first_lanes():
    return iota((1, PAIR), 1) < 64


def tables_kernel(
    where_ref, tab_ref, boxes_hbm, wo_hbm,
    z_ref, m_ref, o_ref, u_ref, r_ref, mine_ref, ur_ref,
    box_scr, boxes_ref, wo_ref, sems,
):
    half = DL // 2
    rows = pl.ds(pl.multiple_of(where_ref[1] * half, half), half)
    copies = start_all(
        (
            (boxes_hbm, boxes_ref),
            (wo_hbm.at[rows, :], wo_ref),
        ),
        sems,
    )
    for copy in copies:
        copy.wait()
    mine_ref[...] = wo_ref[...].astype(F32)
    lane = iota((BINS_1D, 768), 1)
    bucket = jnp.where(lane < 640, jnp.clip(lane - 256, -16, 15) + 16, 0)
    line_pick = (bucket == iota((BINS_1D, 768), 0)).astype(BF16)
    line_base = dot(tab_ref[:, 0:BINS_1D], line_pick)
    lane = iota((BINS_2D, PAIR), 1)
    bucket = jnp.clip(lane - 64, -32, 31) + 32
    plane_pick = (bucket == iota((BINS_2D, PAIR), 0)).astype(BF16)
    bases = [
        dot(tab_ref[:, BINS_1D + 64 * plane : BINS_1D + 64 * plane + 64], plane_pick)
        for plane in range(2)
    ]
    first = first_lanes()
    zeros = jnp.zeros((64, PAIR), BF16)
    for h in range(HL):
        spread = jnp.broadcast_to(line_base[h : h + 1, :], (SUB, 768))
        rolled = pltpu.roll(spread, 0, 1, stride=1, stride_axis=0)
        z_ref[h] = rolled[:, :640]
        for plane in range(2):
            spread = jnp.broadcast_to(bases[plane][h : h + 1, :], (64, PAIR))
            for below in range(2):
                one = pltpu.roll(spread, 64 + below, 1, stride=1, stride_axis=0)
                both = jnp.where(first, one, pltpu.roll(one, 64, 1)).astype(BF16)
                start = h * 512 + plane * 256 + below * 128
                m_ref[plane * 64 : plane * 64 + 64, start : start + 128] = both
                m_ref[64 - plane * 64 : 128 - plane * 64, start : start + 128] = zeros
    box_scr[...] = jnp.full((8, KEYS), -1, jnp.int32)
    box_scr[0:2, 0:SEQ] = boxes_ref[...]
    row = iota((512, KEYS), 0)
    value = 8 * (row % 64) + row // 64
    for plane in range(2):
        o_ref[plane * 512 : plane * 512 + 512, :] = (
            value == box_scr[plane : plane + 1, :]
        ).astype(F32).astype(BF16)
    turned = jnp.transpose(box_scr[...].astype(F32))[0:ROWS, :].astype(jnp.int32)
    left = jnp.broadcast_to(turned[:, 0:1], (ROWS, PAIR))
    right = jnp.broadcast_to(turned[:, 1:2], (ROWS, PAIR))
    lane = iota((ROWS, PAIR), 1)
    both = jnp.where(lane < 64, left, right)
    r_ref[0] = left & 7
    r_ref[1] = right & 7
    upper = lax.shift_right_logical(both, 3)
    inner = lane & 63
    u_ref[...] = (upper == inner).astype(F32).astype(BF16)
    ur_ref[...] = (63 - upper == inner).astype(F32).astype(BF16)


def make_tables(order, where, tab, boxes, wo):
    return order(
        tables_kernel,
        (where, tab, boxes, wo),
        [smem(), vmem()] + [hbm()] * 2,
        (
            sds((HL, SUB, 640), F32),
            sds((128, HL * 512), BF16),
            sds((1024, KEYS), BF16),
            sds((ROWS, PAIR), BF16),
            sds((2, ROWS, PAIR), jnp.int32),
            sds((DL // 2, D), F32),
            sds((ROWS, PAIR), BF16),
        ),
        [vmem()] * 7,
        us=20000,
        scratch_shapes=[
            pltpu.VMEM((8, KEYS), jnp.int32),
            pltpu.VMEM(boxes.shape, jnp.int32),
            pltpu.VMEM((DL // 2, D), BF16),
            pltpu.SemaphoreType.DMA((2,)),
        ],
        name="bias_tables",
    )


def copy_kernel(src, dst, scr, sems):
    for pair in ((src, scr), (scr, dst)):
        copy = pltpu.make_async_copy(*pair, sems.at[0])
        copy.start()
        copy.wait()


def pass_on(order, x):
    return order(
        copy_kernel,
        (x,),
        [anywhere()],
        (sds(x.shape, x.dtype),),
        [anywhere()],
        scratch_shapes=[pltpu.VMEM(x.shape, x.dtype), pltpu.SemaphoreType.DMA((1,))],
        name="pass_on",
    )[0]


def text_taps(text_ref, cols):
    taps = {}
    for dilate in range(3):
        for tap in range(3):
            shift = (tap - 1) * (dilate + 1)
            row = text_ref[dilate, tap : tap + 1, cols].astype(F32)
            taps[shift] = row if shift not in taps else taps[shift] + row
    return taps


def text_conv_block(win, taps, sign):
    total = win[8:40] * (taps[0] + 1.0)
    for shift in (-3, -2, -1, 1, 2, 3):
        start = 8 + sign * shift
        total = total + win[start : start + 32] * taps[shift]
    return total


def grid_masks(side):
    place = iota((208, PAIR), 0)
    row = jnp.floor((place.astype(F32) + 0.5) * (1.0 / side)).astype(jnp.int32)
    col = place - row * side
    return (place < side * side, col >= 1, col <= side - 2)


def patch_conv_cols(win, patch_ref, cols, side, sign):
    live, has_left, has_right = grid_masks(side)
    total = None
    for ds in (-1, 0, 1):
        part = None
        for dr in (-1, 0, 1):
            tap = 3 * (dr + 1) + ds + 1
            start = MARGIN + sign * (dr * side + ds)
            term = win[start : start + 208] * patch_ref[tap : tap + 1, cols].astype(F32)
            part = term if part is None else part + term
        if ds * sign == -1:
            part = jnp.where(has_left, part, 0.0)
        if ds * sign == 1:
            part = jnp.where(has_right, part, 0.0)
        total = part if total is None else total + part
    return jnp.where(live, total, 0.0)


def fill_patches(patch_scr, source, count):
    zero = jnp.zeros((MARGIN, D), F32)
    patch_scr[0:MARGIN, :] = zero
    patch_scr[MARGIN + 208 : MARGIN + 208 + MARGIN, :] = zero
    live = iota((208, PAIR), 0) < count
    for c in range(D // PAIR):
        cols = slice(c * PAIR, c * PAIR + PAIR)
        patch_scr[MARGIN : MARGIN + 208, cols] = jnp.where(live, source(cols), 0.0)


def load_page(x_ref, count, text_scr, patch_scr, raw_scr):
    zero8 = jnp.zeros((8, D), F32)
    text_scr[0:8, :] = zero8
    text_scr[520:528, :] = zero8
    for b in range(TEXT // 64):
        text_scr[8 + 64 * b : 72 + 64 * b, :] = x_ref[64 * b : 64 * b + 64, :].astype(F32)
    raw_scr[...] = jnp.zeros((208, D), F32)
    raw_scr[0 : SEQ - TEXT, :] = x_ref[TEXT:SEQ, :].astype(F32)
    fill_patches(patch_scr, lambda cols: raw_scr[:, cols], count)


PAGE_SCRATCH = [
    pltpu.VMEM((528, D), F32),
    pltpu.VMEM((208 + 2 * MARGIN, D), F32),
    pltpu.VMEM((208, D), F32),
]


def by_grid(count, patches):
    large = count == GRID_LARGE * GRID_LARGE

    @pl.when(large)
    def _():
        patches(GRID_LARGE)

    @pl.when(jnp.logical_not(large))
    def _():
        patches(GRID_SMALL)


def encode_kernel(
    count_ref, x_hbm, text_ref, patch_ref, bias_ref, wq_hbm, wk_hbm, wv_hbm,
    q0, q1, q2, k_ref, v_ref, e0, e1, e2, l0, l1, l2,
    text_scr, patch_scr, raw_scr, x_ref, wq_ref, wk_ref, wv_ref, sems,
):
    copies = start_all(
        ((x_hbm, x_ref), (wq_hbm, wq_ref), (wk_hbm, wk_ref), (wv_hbm, wv_ref)), sems
    )
    count = count_ref[0]
    copies[0].wait()
    load_page(x_ref, count, text_scr, patch_scr, raw_scr)

    for c in range(2):
        cols = slice(c * 384, c * 384 + 384)
        taps = text_taps(text_ref, cols)

        def one(b, carry, cols=cols, taps=taps, out=None, first=0):
            base = pl.multiple_of(b * 32, 32)
            win = text_scr[pl.ds(first + base, 48), cols]
            out[pl.ds(base, 32), cols] = text_conv_block(win, taps, 1)
            return carry

        for (first, rows), out in zip(CHUNKS, (e0, e1)):
            lax.fori_loop(0, rows // 32, functools.partial(one, out=out, first=first), 0)

    def patches(side):
        for c in range(D // PAIR):
            cols = slice(c * PAIR, c * PAIR + PAIR)
            e2[:, cols] = raw_scr[:, cols] + patch_conv_cols(
                patch_scr[:, cols], patch_ref, cols, side, 1
            )

    by_grid(count, patches)
    for copy in copies[1:]:
        copy.wait()
    for (start, rows), e, low, q in zip(CHUNKS, (e0, e1, e2), (l0, l1, l2), (q0, q1, q2)):
        enc = e[...].astype(BF16)
        low[...] = enc
        query = (dot(enc, wq_ref[...]) + bias_ref[0:1, :]).astype(BF16)
        q[...] = query * jnp.asarray(0.125, BF16)
        k_ref[start : start + rows, :] = dot(enc, wk_ref[...]).astype(BF16)
        value = dot(enc, wv_ref[...]) + bias_ref[1:2, :]
        v_ref[start : start + rows, :] = value.astype(BF16)
    k_ref[ROWS:KEYS, :] = jnp.zeros((KEYS - ROWS, DL), BF16)
    v_ref[ROWS:KEYS, :] = jnp.zeros((KEYS - ROWS, DL), BF16)


def encode(order, count, x, text, patch, bias, wq, wk, wv, out):
    chunk = lambda width, dtype: tuple(sds((rows, width), dtype) for _, rows in CHUNKS)
    keys = (sds((KEYS, DL), BF16), sds((KEYS, DL), BF16))
    got, far = order(
        encode_kernel,
        (count, x, text, patch, bias, wq, wk, wv),
        [smem(), hbm()] + [vmem()] * 3 + [hbm()] * 3,
        chunk(DL, BF16) + keys + chunk(D, F32) + chunk(D, BF16),
        [vmem()] * 11,
        scratch_shapes=PAGE_SCRATCH
        + [pltpu.VMEM((SEQ, D), BF16)]
        + [pltpu.VMEM((D, DL), BF16)] * 3
        + [pltpu.SemaphoreType.DMA((4,))],
        mib=12,
        us=8000,
        out=out,
        name="encode_project",
    )
    return got[0:5], got[5:8], got[8:11], far


def bias_rows(e, r_col, k, rows):
    step = 2 * k + (iota((rows, PAIR), 1) >= 64).astype(jnp.int32)
    return jnp.where(step >= r_col, e[0], e[1]).astype(BF16)


def line_rows(z_ref, h, sub, rows):
    groups = [min(max(g - sub + 2, 0), 4) for g in range(KEYS // SUB)]
    return jnp.concatenate([z_ref[h, 0:rows, g * 128 : g * 128 + 128] for g in groups], axis=1)


def attend_kernel(
    start, rows, count_ref, q_ref, k_ref, v_ref, u_ref, r_ref, m_ref, o_ref, z_ref,
    p_ref, mix_ref, low_ref,
):
    live = iota((1, KEYS), 1) < TEXT + count_ref[0]
    first = first_lanes()
    r_w = r_ref[0, start : start + rows, :]
    r_h = r_ref[1, start : start + rows, :]
    u = u_ref[start : start + rows, :]
    for pair in range(HL // 2):
        cols = slice(pair * PAIR, pair * PAIR + PAIR)
        q = q_ref[:, cols]
        k = k_ref[:, cols]
        v = v_ref[:, cols]
        mixed = []
        for half in range(2):
            h = 2 * pair + half
            mine = first if half == 0 else jnp.logical_not(first)
            qm = jnp.where(mine, q, jnp.zeros_like(q))
            e = dot(u, m_ref[:, h * 512 : h * 512 + 512])
            parts = [bias_rows((e[:, 0:128], e[:, 128:256]), r_w, kk, rows) for kk in range(4)]
            parts += [bias_rows((e[:, 256:384], e[:, 384:512]), r_h, kk, rows) for kk in range(4)]
            picked = jnp.concatenate(parts, axis=1)
            s = dot(picked, o_ref[...]) + dot_nt(qm, k)
            pieces = []
            for at in range(0, rows, SUB):
                size = min(SUB, rows - at)
                pieces.append(line_rows(z_ref, h, (start + at) // SUB, size))
            s = s + jnp.concatenate(pieces, axis=0)
            s = jnp.where(live, s, NEG)
            top = jnp.max(s, axis=1, keepdims=True)
            ex = jnp.exp(s - top)
            total = jnp.sum(ex, axis=1, keepdims=True)
            prob = (ex * (1.0 / total)).astype(BF16)
            p_ref[h] = prob
            mixed.append(dot(prob, v))
        low = jnp.where(first, mixed[0], mixed[1]).astype(BF16)
        low_ref[:, cols] = low
        mix_ref[:, cols] = low.astype(F32)


def attend(order, c, count, q, k, v, u, r, m, o, z, out):
    start, rows = CHUNKS[c]
    return order(
        functools.partial(attend_kernel, start, rows),
        (count, q, k, v, u, r, m, o, z),
        [smem()] + [vmem()] * 8,
        (sds((HL, rows, KEYS), BF16), sds((rows, DL), F32), sds((rows, DL), BF16)),
        [vmem()] * 3,
        out=out,
        name=f"attend_{c}",
    )


def feed_kernel(
    where_ref, own_ref, other_ref, enc_hbm, vec_ref, wo_ref, wo_a_ref, wo_b_ref, wi_ref, bi_ref,
    w2_ref, xhat_ref, rstd_ref, hlow_ref, act_ref, slope_ref, part_ref, enc_ref, sems,
):
    (copy,) = start_all(((enc_hbm, enc_ref),), sems)
    half = where_ref[0]
    core = where_ref[1]
    own = dot(own_ref[...].astype(BF16), wo_ref[...])
    other = other_ref[...].astype(BF16)
    low = jnp.where(core == 0, wo_a_ref[...], wo_b_ref[...]).astype(BF16)
    high = jnp.where(core == 0, wo_b_ref[...], wo_a_ref[...]).astype(BF16)
    other = dot(other, jnp.concatenate([low, high], axis=0))
    attended = jnp.where(half == 0, own, other) + jnp.where(half == 0, other, own)
    copy.wait()
    v = enc_ref[...] + (attended + vec_ref[0:1, :])
    centre = v - jnp.mean(v, axis=1, keepdims=True)
    rstd = lax.rsqrt(jnp.mean(centre * centre, axis=1, keepdims=True) + EPS)
    xhat = centre * rstd
    xhat_ref[...] = xhat
    rstd_ref[...] = jnp.broadcast_to(rstd, rstd_ref.shape)
    hlow = (xhat * vec_ref[1:2, :] + vec_ref[2:3, :]).astype(BF16)
    hlow_ref[...] = hlow
    total = None
    for n in range(FL // 512):
        cols = slice(n * 512, n * 512 + 512)
        pre = dot(hlow, wi_ref[:, cols]) + bi_ref[0:1, cols]
        gate = 0.5 + 0.5 * lax.erf(pre * 0.7071067811865476)
        slope_ref[:, cols] = gate + pre * (0.3989422804014327 * jnp.exp(-0.5 * pre * pre))
        act = (pre * gate).astype(BF16)
        act_ref[:, cols] = act
        term = dot(act, w2_ref[cols, :])
        total = term if total is None else total + term
    part_ref[...] = total


def feed(order, c, where, own, other, enc, vec, wo, wo_a, wo_b, wi, bi, w2, out):
    _, rows = CHUNKS[c]
    return order(
        feed_kernel,
        (where, own, other, enc, vec, wo, wo_a, wo_b, wi, bi, w2),
        [smem()] + [vmem()] * 2 + [hbm()] + [vmem()] * 7,
        (
            sds((rows, D), F32),
            sds((rows, 128), F32),
            sds((rows, D), BF16),
            sds((rows, FL), BF16),
            sds((rows, FL), F32),
            sds((rows, D), F32),
        ),
        [vmem()] * 6,
        scratch_shapes=[pltpu.VMEM((rows, D), F32), pltpu.SemaphoreType.DMA((1,))],
        out=out,
        name=f"feed_{c}",
    )


def norm_back(dy, xhat, rstd, gain):
    dxh = dy * gain
    return rstd * (
        dxh
        - jnp.mean(dxh, axis=1, keepdims=True)
        - xhat * jnp.mean(dxh * xhat, axis=1, keepdims=True)
    )


def col_sum(x):
    return jnp.sum(x, axis=0, keepdims=True)


def feed_back_kernel(
    start, rows, first, count_ref, own_ref, other_ref, xhat1_ref, cot_ref, vec_ref, w2_ref,
    slope_ref, wi_ref, *rest,
):
    if not first:
        rest = rest[1:]
    out_ref, dres_ref, g2_ref, g1_ref, part_ref, sums_ref = rest
    place = start + iota((rows, 1), 0)
    live = place < TEXT + count_ref[0]
    hidden = xhat1_ref[...] * vec_ref[1:2, :] + vec_ref[2:3, :]
    v = hidden + ((own_ref[...] + other_ref[...]) + vec_ref[3:4, :])
    centre = v - jnp.mean(v, axis=1, keepdims=True)
    rstd = lax.rsqrt(jnp.mean(centre * centre, axis=1, keepdims=True) + EPS)
    xhat = centre * rstd
    y = xhat * vec_ref[4:5, :] + vec_ref[5:6, :]
    out_ref[0:rows, :] = jnp.where(live, y, 0.0).astype(BF16)
    dy = jnp.where(live, cot_ref[0:rows, :].astype(F32), 0.0)
    sums_ref[...] = jnp.zeros(sums_ref.shape, F32)
    sums_ref[2:3, 0:D] = col_sum(dy * xhat)
    sums_ref[3:4, 0:D] = col_sum(dy)
    dres = norm_back(dy, xhat, rstd, vec_ref[4:5, :])
    dres_ref[...] = dres
    sums_ref[1:2, 0:D] = col_sum(dres)
    g2 = dres.astype(BF16)
    g2_ref[...] = g2
    total = None
    for n in range(FL // 512):
        cols = slice(n * 512, n * 512 + 512)
        d_inner = dot_nt(g2, w2_ref[cols, :]) * slope_ref[:, cols]
        sums_ref[0:1, cols] = col_sum(d_inner)
        g1 = d_inner.astype(BF16)
        g1_ref[:, cols] = g1
        term = dot_nt(g1, wi_ref[:, cols])
        total = term if total is None else total + term
    part_ref[...] = total


def feed_back(order, c, count, own, other, xhat1, cot, vec, w2, slope, wi, out_so_far):
    start, rows = CHUNKS[c]
    high = 256 if start == TEXT else rows
    block = pl.BlockSpec((high, D), lambda i: (start // high, 0))
    whole = lambda a: pl.BlockSpec(a.shape, lambda i: (0, 0))
    shapes = (
        sds((SEQ, D), BF16),
        sds((rows, D), F32),
        sds((rows, D), BF16),
        sds((rows, FL), BF16),
        sds((rows, D), F32),
        sds((8, FL), F32),
    )
    operands = [count, own, other, xhat1, cot, vec, w2, slope, wi]
    specs = [smem()] + [vmem()] * 3 + [block] + [vmem()] * 4
    aliases = {}
    if out_so_far is not None:
        operands.append(out_so_far)
        specs.append(anywhere())
        aliases = {9: 0}
    return order(
        functools.partial(feed_back_kernel, start, rows, out_so_far is None),
        operands,
        specs,
        shapes,
        [block] + [vmem()] * 5,
        grid=(1,),
        input_output_aliases=aliases,
        name=f"feed_back_{c}",
    )


def store_slabs(slab, core, grad, keep_ref, send_ref):
    for i in range(D // (2 * slab)):
        even = grad[2 * i * slab : (2 * i + 1) * slab]
        odd = grad[(2 * i + 1) * slab : (2 * i + 2) * slab]
        keep_ref[i * slab : (i + 1) * slab, :] = jnp.where(core == 0, even, odd)
        send_ref[i * slab : (i + 1) * slab, :] = jnp.where(core == 0, odd, even)


def tn_sum(lefts, rights):
    total = None
    for left, right in zip(lefts, rights):
        term = dot_tn(left[...], right[...].astype(BF16))
        total = term if total is None else total + term
    return total


def put_grads(slab, where_ref, grad, outs):
    if slab is None:
        outs[0][...] = grad
    else:
        store_slabs(slab, where_ref[1], grad, *outs)


def chunk_grads_kernel(slab, has_total, where_ref, left_ref, right_ref, *refs):
    grad = dot_tn(left_ref[...], right_ref[...])
    if has_total:
        grad = refs[0][...] + grad
    put_grads(slab, where_ref, grad, refs[has_total:])


def chunk_grads(order, slab, where, left, right, total, last, name):
    width = right.shape[1]
    block = 512
    piece = lambda rows: pl.BlockSpec((rows, block), lambda i: (0, i))
    whole = pl.BlockSpec(left.shape, lambda i: (0, 0))
    apart = last and slab is not None
    rows, count = (D // 2, 2) if apart else (D, 1)
    operands, specs, aliases = [where, left, right], [smem(), whole, piece(right.shape[0])], {}
    if total is not None:
        operands.append(total)
        specs.append(piece(D))
        if not apart:
            aliases = {3: 0}
    return order(
        functools.partial(chunk_grads_kernel, slab if apart else None, total is not None),
        operands,
        specs,
        (sds((rows, width), F32),) * count,
        [piece(rows)] * count,
        grid=(width // block,),
        input_output_aliases=aliases,
        mib=16,
        name=name,
    )


SPLIT = 768


def attention_grads_kernel(slab, where_ref, *refs):
    low, dq, (dk_ref, dv_ref), g0, mix = refs[0:3], refs[3:6], refs[6:8], refs[8:11], refs[11:14]
    chunks = lambda ref: [ref.at[start : start + rows] for start, rows in CHUNKS]
    todo = ((low, dq), (low, chunks(dk_ref)), (low, chunks(dv_ref)), (g0, mix))
    one = lambda refs: jnp.concatenate([ref[...].astype(BF16) for ref in refs], axis=0)
    wide = jnp.concatenate([one(rights) for _, rights in todo[0:3]], axis=1)
    wide = dot_tn(one(low), wide)
    grads = [wide[:, i * DL : i * DL + DL] for i in range(3)] + [dot_tn(one(g0), one(mix))]
    for i, grad in enumerate(grads):
        first, last = i * DL, i * DL + DL
        for part, (low_end, high_end) in enumerate(((0, SPLIT), (SPLIT, 4 * DL))):
            begin, end = max(first, low_end), min(last, high_end)
            if begin < end:
                cols = slice(begin - low_end, end - low_end)
                outs = [ref.at[:, cols] for ref in refs[14 + 2 * part : 16 + 2 * part]]
                store_slabs(slab, where_ref[1], grad[:, begin - first : end - first], *outs)


def attention_grads(order, slab, where, enc_low, dq, dk, dv, g0, mix):
    operands = [*enc_low, *dq, dk, dv, *g0, *mix]
    widths = (SPLIT, SPLIT, 4 * DL - SPLIT, 4 * DL - SPLIT)
    return order(
        functools.partial(attention_grads_kernel, slab),
        (where, *operands),
        [smem()] + [vmem()] * len(operands),
        [sds((D // 2, width), F32) for width in widths],
        [vmem()] * 4,
        name="attention_grads",
    )


def plain_grads_kernel(*refs):
    low, dq, (dk_ref, dv_ref), g0, mix = refs[0:3], refs[3:6], refs[6:8], refs[8:11], refs[11:14]
    chunks = lambda ref: [ref.at[start : start + rows] for start, rows in CHUNKS]
    todo = ((low, dq), (low, chunks(dk_ref)), (low, chunks(dv_ref)), (g0, mix))
    for i, (lefts, rights) in enumerate(todo):
        refs[14][:, i * DL : i * DL + DL] = tn_sum(lefts, rights)


def plain_grads(order, enc_low, dq, dk, dv, g0, mix):
    operands = [*enc_low, *dq, dk, dv, *g0, *mix]
    return order(
        plain_grads_kernel, operands, [vmem()] * len(operands), (sds((D, 4 * DL), F32),), [vmem()],
        name="plain_grads",
    )


def halve_kernel(slabs, high, where_bit, count, extra, where_ref, *refs):
    *smalls, a_ref, b_ref, own_ref, out_ref = refs
    mine = where_ref[where_bit]
    total = a_ref.shape[0] - (extra if count == 0 else 0)
    run = high * (total // slabs)
    for i in range(slabs // (2 * high)):
        for ref, which in ((own_ref, mine), (out_ref, 1 - mine)):
            rows = pl.ds(pl.multiple_of((2 * i + which) * run, 8), run)
            ref[i * run : (i + 1) * run, :] = a_ref[rows, :] + b_ref[rows, :]
    if extra == 0:
        return
    width = D
    small = a_ref[total:, 0:width] + b_ref[total:, 0:width] if count == 0 else smalls[0][...]
    for ref in smalls[1:]:
        small = small + ref[...]
    for ref in (own_ref, out_ref):
        ref[total // 2 :, 0:width] = small
        if ref.shape[1] > width:
            rest = (extra, ref.shape[1] - width)
            ref[total // 2 :, width:] = jnp.zeros(rest, F32)


def halve(order, where, pair, slabs, high, where_bit, first, width, name, smalls=(), extra=0):
    rows = pair[0].shape[0]
    total = rows - (0 if smalls else extra)
    if extra == 0:
        block = 512 if width % 512 == 0 and first % 512 == 0 else 384
    else:
        block = width
    at = first // block
    out_rows = total // 2 + extra
    half = pl.BlockSpec((out_rows, block), lambda i: (0, i))
    return order(
        functools.partial(halve_kernel, slabs, high, where_bit, len(smalls), extra),
        [where, *smalls, *pair],
        [smem()]
        + [pl.BlockSpec(a.shape, lambda i: (0, 0)) for a in smalls]
        + [pl.BlockSpec((rows, block), lambda i: (0, at + i))] * 2,
        (sds((out_rows, width), F32),) * 2,
        [half, half],
        grid=(width // block,),
        mib=12,
        name=name,
    )


def norm_back_kernel(
    dres2_ref, own_ref, other_ref, xhat_ref, rstd_ref, vec_ref, wo_ref,
    dres1_far, g0_ref, dmix_ref, sums_ref, dres1_ref, sems,
):
    dhid = dres2_ref[...] + (own_ref[...] + other_ref[...])
    xhat = xhat_ref[...]
    sums_ref[...] = jnp.zeros(sums_ref.shape, F32)
    sums_ref[1:2, :] = col_sum(dhid * xhat)
    sums_ref[2:3, :] = col_sum(dhid)
    dres1 = norm_back(dhid, xhat, rstd_ref[:, 0:1], vec_ref[1:2, :])
    dres1_ref[...] = dres1
    (copy,) = start_all(((dres1_ref, dres1_far),), sems)
    sums_ref[0:1, :] = col_sum(dres1)
    g0 = dres1.astype(BF16)
    g0_ref[...] = g0
    dmix_ref[...] = dot_nt(g0, wo_ref[...]).astype(BF16)
    copy.wait()


def norm_one_back(order, c, dres2, own, other, xhat, rstd, vec, wo):
    _, rows = CHUNKS[c]
    return order(
        norm_back_kernel,
        (dres2, own, other, xhat, rstd, vec, wo),
        [vmem()] * 7,
        (sds((rows, D), F32), sds((rows, D), BF16), sds((rows, DL), BF16), sds((8, D), F32)),
        [hbm()] + [vmem()] * 3,
        scratch_shapes=[pltpu.VMEM((rows, D), F32), pltpu.SemaphoreType.DMA((1,))],
        us=20000 if c == ORDER[0] else 1,
        name=f"norm_back_{c}",
    )


def attend_back_kernel(
    start, rows, first, dmix_ref, p_ref, q_ref, k_ref, v_ref, ur_ref, r_ref, o_ref, *rest,
):
    if not first:
        dk_in, dv_in, dm_in, dz_in = rest[:4]
        rest = rest[4:]
    dq_ref, dk_ref, dv_ref, dm_ref, dz_ref = rest
    if first:
        dz_ref[...] = jnp.zeros(dz_ref.shape, F32)
    else:
        dz_ref[...] = dz_in[...]

    lanes = first_lanes()
    r_w = r_ref[0, start : start + rows, :]
    r_h = r_ref[1, start : start + rows, :]
    upper = (iota((rows, PAIR), 1) >= 64).astype(jnp.int32)
    ur = ur_ref[start : start + rows, :]
    pick = lambda h, a: jnp.where(
        lanes if h % 2 == 0 else jnp.logical_not(lanes), a, jnp.zeros_like(a)
    )
    pair_cols = lambda h: slice(h // 2 * PAIR, h // 2 * PAIR + PAIR)

    def dprob_of(h):
        return dot_nt(pick(h, dmix_ref[:, pair_cols(h)]), v_ref[:, pair_cols(h)])

    def back_of(h, dprob):
        cols = pair_cols(h)
        prob = p_ref[h]
        prob_f = prob.astype(F32)
        both = prob_f * dprob
        ds = both - prob_f * jnp.sum(both, axis=1, keepdims=True)
        low = ds.astype(BF16)
        dq = dot(low, pick(h, k_ref[:, cols]))
        dk = dot_tn(low, pick(h, q_ref[:, cols]))
        dv = dot_tn(prob, pick(h, dmix_ref[:, cols]))
        dbias = dot_nt(low, o_ref[...])
        for at in range(0, rows, SUB):
            size = min(SUB, rows - at)
            sub = (start + at) // SUB
            sums = {}
            for g in range(KEYS // SUB):
                group = min(max(g - sub + 2, 0), 4)
                piece = ds[at : at + size, g * 128 : g * 128 + 128]
                sums[group] = piece if group not in sums else sums[group] + piece
            for group, piece in sums.items():
                dz_ref[h, 0:size, group * 128 : group * 128 + 128] += piece
        return dq, dk, dv, dbias

    def table_of(h, dbias):
        parts = []
        for plane, r_col in ((0, r_w), (1, r_h)):
            same = None
            total = None
            for kk in range(4):
                base = plane * 512 + kk * 128
                piece = dbias[:, base : base + 128]
                yes = jnp.where((2 * kk + upper) >= r_col, piece, 0.0)
                same = yes if same is None else same + yes
                total = piece if total is None else total + piece
            parts += [same, total - same]
        dm = dot_tn(ur, jnp.concatenate(parts, axis=1).astype(BF16))
        at = slice(h * 512, h * 512 + 512)
        dm_ref[:, at] = dm if first else dm_in[:, at] + dm

    dprob = dprob_of(0)
    totals = None
    for h in range(HL):
        following = dprob_of(h + 1) if h + 1 < HL else None
        dq, dk, dv, dbias = back_of(h, dprob)
        dprob = following
        cols = pair_cols(h)
        if h % 2 == 0:
            totals = (dq, dk, dv)
        else:
            dq_ref[:, cols] = (totals[0] + dq) * 0.125
            dk = totals[1] + dk
            dv = totals[2] + dv
            dk_ref[:, cols] = dk if first else dk_in[:, cols] + dk
            dv_ref[:, cols] = dv if first else dv_in[:, cols] + dv
        table_of(h, dbias)


def attend_back(order, c, dmix, p, q, k, v, ur, r, o, carry, into):
    start, rows = CHUNKS[c]
    operands = [dmix, p, q, k, v, ur, r, o]
    aliases = {}
    if carry is not None:
        operands += list(carry)
        aliases = {8 + i: 1 + i for i in range(4)}
    return order(
        functools.partial(attend_back_kernel, start, rows, carry is None),
        operands,
        [vmem()] * len(operands),
        (
            sds((rows, DL), F32),
            sds((KEYS, DL), F32),
            sds((KEYS, DL), F32),
            sds((128, HL * 512), F32),
            sds((HL, SUB, 640), F32),
        ),
        [vmem()] * 5,
        input_output_aliases=aliases,
        into=into,
        name=f"attend_back_{c}",
    )


def table_sums_kernel(dm_ref, dz_ref, out_ref):
    lane = iota((PAIR, BINS_2D), 0)
    plane_bin = jnp.clip(lane - 64, -32, 31) + 32
    plane_pick = (plane_bin == iota((PAIR, BINS_2D), 1)).astype(F32)
    lane = iota((512, BINS_1D), 0)
    line_bin = jnp.clip(lane - 256, -16, 15) + 16
    line_pick = (line_bin == iota((512, BINS_1D), 1)).astype(F32)
    first = first_lanes()
    flip = (iota((SUB, SUB), 0) + iota((SUB, SUB), 1) == SUB - 1).astype(F32)
    bin_id = iota((1, BINS_1D), 1)
    exact = functools.partial(
        lax.dot_general,
        dimension_numbers=(((1,), (0,)), ((), ())),
        precision=HIGHEST,
        preferred_element_type=F32,
    )
    out_ref[...] = jnp.zeros(out_ref.shape, F32)
    for h in range(HL):
        z = dz_ref[h]
        left = jnp.sum(z[:, 0:128])
        right = jnp.sum(z[:, 512:640])
        band = jnp.concatenate([z[:, 128:512], jnp.zeros((SUB, 128), F32)], axis=1)
        band = pltpu.roll(exact(flip, band), 512 - 127 + 128, 1, stride=1, stride_axis=0)
        line = exact(col_sum(band), line_pick)
        line = line + jnp.where(bin_id == 0, left, 0.0) + jnp.where(bin_id == 31, right, 0.0)
        out_ref[h : h + 1, 0:BINS_1D] = line
        for plane in range(2):
            total = None
            for below in range(2):
                at = h * 512 + plane * 256 + below * 128
                g = dm_ref[plane * 64 : plane * 64 + 64, at : at + 128]
                g = jnp.where(first, g + pltpu.roll(g, 64, 1), 0.0)
                g = pltpu.roll(g, 1 - below, 1, stride=1, stride_axis=0)
                total = g if total is None else total + g
            summed = exact(col_sum(total), plane_pick)
            at = BINS_1D + plane * 64
            out_ref[h : h + 1, at : at + 64] = summed


def table_sums(order, dm, dz):
    return order(
        table_sums_kernel,
        (dm, dz),
        [vmem()] * 2,
        (sds((8, 256), F32),),
        [vmem()],
        name="table_sums",
    )[0]


def project_back_kernel(
    q0, q1, q2, dk_ref, dv_ref, wq_ref, wk_ref, wv_ref, part_ref, bias_ref,
):
    sum_q = None
    sum_v = None
    for (start, rows), dq in zip(CHUNKS, (q0, q1, q2)):
        query = dq[...]
        value = dv_ref[start : start + rows, :]
        sum_q = col_sum(query) if sum_q is None else sum_q + col_sum(query)
        sum_v = col_sum(value) if sum_v is None else sum_v + col_sum(value)
        query = query.astype(BF16)
        key = dk_ref[start : start + rows, :].astype(BF16)
        value = value.astype(BF16)
        part = dot_nt(query, wq_ref[...]) + dot_nt(key, wk_ref[...]) + dot_nt(value, wv_ref[...])
        rows = min(rows, part_ref.shape[0] - start)
        part_ref[start : start + rows, :] = part[0:rows]
    bias_ref[...] = jnp.zeros(bias_ref.shape, F32)
    bias_ref[0:1, 0:DL] = sum_q
    bias_ref[0:1, DL:D] = sum_v


def project_back(order, dq, dk, dv, wq, wk, wv):
    return order(
        project_back_kernel,
        (*dq, dk, dv, wq, wk, wv),
        [vmem()] * 8,
        (sds((ROWS - 8, D), F32), sds((8, D), F32)),
        [vmem()] * 2,
        us=15000,
        name="project_back",
    )


def taps_kernel(
    count_ref, x_hbm, pt, r0_far, r1_far, r2_far, out_ref,
    text_scr, patch_scr, raw_scr, x_ref, r0, r1, r2, sems,
):
    count = count_ref[0]
    copies = start_all(((x_hbm, x_ref), (r0_far, r0), (r1_far, r1), (r2_far, r2)), sems)
    copies[0].wait()
    load_page(x_ref, count, text_scr, patch_scr, raw_scr)
    for copy in copies[1:]:
        copy.wait()
    out_ref[...] = jnp.zeros(out_ref.shape, F32)
    shifts = tuple(range(-3, 4))
    for c in range(2):
        cols = slice(c * 384, c * 384 + 384)

        def one(b, sums, cols=cols, res=None, first=0):
            base = pl.multiple_of(b * 32, 32)
            win = text_scr[pl.ds(first + base, 48), cols]
            grad = pt[pl.ds(first + base, 32), cols] + 0.5 * res[pl.ds(base, 32), cols]
            out = []
            for shift, total in zip(shifts, sums):
                prod = grad * win[8 + shift : 40 + shift]
                out.append(total + jnp.sum(prod.reshape(4, 8, 384), axis=0))
            return tuple(out)

        sums = tuple(jnp.zeros((8, 384), F32) for _ in shifts)
        for (first, rows), res in zip(CHUNKS, (r0, r1)):
            sums = lax.fori_loop(
                0, rows // 32, functools.partial(one, res=res, first=first), sums
            )
        for row, total in enumerate(sums):
            out_ref[row : row + 1, cols] = col_sum(total)

    def patches(side):
        live, has_left, has_right = grid_masks(side)
        for c in range(D // PAIR):
            cols = slice(c * PAIR, c * PAIR + PAIR)
            win = patch_scr[:, cols]
            grad = jnp.where(live, filled(pt[TEXT:, cols], 208) + 0.5 * r2[:, cols], 0.0)
            for ds in (-1, 0, 1):
                masked = grad
                if ds == -1:
                    masked = jnp.where(has_left, grad, 0.0)
                if ds == 1:
                    masked = jnp.where(has_right, grad, 0.0)
                for dr in (-1, 0, 1):
                    row = 7 + 3 * (dr + 1) + ds + 1
                    at = MARGIN + dr * side + ds
                    out_ref[row : row + 1, cols] = col_sum(masked * win[at : at + 208])

    by_grid(count, patches)


def tap_sums(order, count, x, part, res):
    return order(
        taps_kernel,
        (count, x, part, *res),
        [smem(), hbm(), vmem()] + [hbm()] * 3,
        (sds((16, D), F32),),
        [vmem()],
        scratch_shapes=PAGE_SCRATCH
        + [pltpu.VMEM((SEQ, D), BF16)]
        + [pltpu.VMEM((rows, D), F32) for _, rows in CHUNKS]
        + [pltpu.SemaphoreType.DMA((4,))],
        mib=14,
        name="tap_sums",
    )[0]


def decode_text_kernel(text_ref, p, s, r0, r1, out_ref, text_scr):
    zero8 = jnp.zeros((8, D), F32)
    text_scr[0:8, :] = zero8
    text_scr[520:528, :] = zero8
    for r, (at, rows) in zip((r0, r1), CHUNKS):
        for b in range(rows // 64):
            res = r[64 * b : 64 * b + 64, :]
            here = slice(at + 64 * b, at + 64 * b + 64)
            text_scr[8 + at + 64 * b : 72 + at + 64 * b, :] = res + (p[here, :] + s[here, :])
    for c in range(2):
        cols = slice(c * 384, c * 384 + 384)
        taps = text_taps(text_ref, cols)

        def one(b, carry, cols=cols, taps=taps):
            base = pl.multiple_of(b * 32, 32)
            win = text_scr[pl.ds(base, 48), cols]
            out_ref[pl.ds(base, 32), cols] = text_conv_block(win, taps, -1).astype(BF16)
            return carry

        lax.fori_loop(0, TEXT // 32, one, 0)


def decode_kernel(
    count_ref, text_ref, patch_ref, p_far, s_far, r0_far, r1_far, r2_far, out_ref,
    text_scr, patch_scr, raw_scr, p, s, r0, r1, r2, sems,
):
    pairs = ((p_far, p), (s_far, s), (r0_far, r0), (r1_far, r1), (r2_far, r2))
    for copy in start_all(pairs, sems):
        copy.wait()
    decode_text_kernel(text_ref, p, s, r0, r1, out_ref, text_scr)
    count = count_ref[0]
    raw_scr[...] = r2[...] + filled(p[TEXT:, :] + s[TEXT:, :], 208)
    fill_patches(patch_scr, lambda cols: raw_scr[:, cols], count)

    def patches(side):
        for c in range(D // PAIR):
            cols = slice(c * PAIR, c * PAIR + PAIR)
            total = raw_scr[:, cols] + patch_conv_cols(patch_scr[:, cols], patch_ref, cols, side, -1)
            out_ref[TEXT:SEQ, cols] = total[0 : SEQ - TEXT].astype(BF16)

    by_grid(count, patches)


def decode(order, count, text_w, patch_w, part, other, res):
    return order(
        decode_kernel,
        (count, text_w, patch_w, part, other, *res),
        [smem()] + [vmem()] * 2 + [hbm()] * 5,
        (sds((SEQ, D), BF16),),
        whole_blocks((sds((SEQ, D), BF16),)),
        grid=(1,),
        scratch_shapes=PAGE_SCRATCH
        + [pltpu.VMEM(part.shape, F32)] * 2
        + [pltpu.VMEM((rows, D), F32) for _, rows in CHUNKS]
        + [pltpu.SemaphoreType.DMA((5,))],
        mib=18,
        name="decode",
    )[0]


def swap_tensor(x):
    return lax.ppermute(x, "tensor", [(0, 1), (1, 0)])


def swap_dp(x, bit, dp):
    return lax.ppermute(x, "dp", [(i, i ^ bit) for i in range(dp)])


def swap_core(parts, dp):
    return (parts[0], swap_dp(parts[1], 1, dp)) if len(parts) == 2 else parts


class Scatter:
    def __init__(self, order, dp, where, pair, bits, name, first, width):
        self.order, self.dp, self.where, self.bits, self.name = order, dp, where, bits, name
        self.window = (first, width)
        self.pair = pair
        self.left = list(range(1, dp.bit_length() - 1))
        self.extra = 0

    def step(self, *smalls):
        if len(self.pair) == 1:
            return
        bit = self.bits[0]
        self.bits = self.bits[1:]
        at = self.left.index(bit)
        if smalls:
            self.extra = smalls[0].shape[0]
        own, out = halve(
            self.order, self.where, self.pair, 2 ** len(self.left), 2**at, 1 + bit, *self.window,
            f"{self.name}_{bit}", smalls, self.extra,
        )
        self.window = (0, self.window[1])
        self.left.remove(bit)
        self.pair = (own, swap_dp(out, 2**bit, self.dp))

    def total(self):
        first, width = self.window
        whole = self.pair[0][:, first : first + width]
        return lax.psum_scatter(whole, "dp", scatter_dimension=0, tiled=True)


def whole_blocks(shapes):
    return [pl.BlockSpec(a.shape, lambda i, n=len(a.shape): (0,) * n) for a in shapes]


EARLY = 8
LATE = 24


def total_of(order, part, name):
    return add_blocks(order, *part.pair, name)


def add_blocks(order, *pair_name):
    *pair, name = pair_name
    shapes = (sds(pair[0].shape, F32),)
    return order(
        add_kernel, pair, whole_blocks(pair), shapes, whole_blocks(shapes), grid=(1,), name=name
    )[0]


def add_kernel(a, b, out):
    out[...] = a[...] + b[...]


def add_here(order, a, b, name):
    return order(
        add_kernel, (a, b), [vmem()] * 2, (sds(a.shape, F32),), [vmem()], name=name
    )[0]


def joint_kernel(where_ref, sum_ref, a_ref, b_ref, own_ref, out_ref):
    mine = where_ref[4]
    slab = a_ref.shape[0] // 2
    width = a_ref.shape[1]
    for ref, which in ((own_ref, mine), (out_ref, 1 - mine)):
        rows = pl.ds(pl.multiple_of(which * slab, 8), slab)
        ref[0:slab, 0:D] = sum_ref[rows, :]
        ref[0:slab, D : D + width] = a_ref[rows, :] + b_ref[rows, :]
        ref[slab:, 0:D] = sum_ref[2 * slab :, :]
        ref[slab:, D : D + width] = jnp.zeros((EARLY, width), F32)


def joint_step(order, dp, where, summed, part):
    rows, width = part.pair[0].shape
    shapes = (sds((rows // 2 + EARLY, D + width), F32),) * 2
    operands = (summed, *part.pair)
    own, out = order(
        joint_kernel, (where, *operands), [smem()] + whole_blocks(operands), shapes,
        whole_blocks(shapes), grid=(1,), name="joint_3",
    )
    return own, swap_dp(out, 8, dp)


def last_totals_kernel(
    both, b0, b1, joint, ob, ia, q_ref, k_ref, v_ref, o_ref, outer_ref, inner_ref, small_ref,
):
    slab = q_ref.shape[0]
    q_ref[...] = both[0:slab, 0:DL]
    k_ref[...] = both[0:slab, DL:D]
    both = b0[...] + b1[...]
    v_ref[...] = both[0:slab, 0:DL]
    o_ref[...] = both[0:slab, DL:D]
    small_ref[0:LATE, :] = both[slab:, 0:D]
    split = joint.shape[1] - D
    outer_ref[:, 0:split] = joint[0:slab, D : D + split]
    outer_ref[:, split:FL] = ob[...]
    inner_ref[:, 0:D] = ia[...]
    inner_ref[:, D:FL] = joint[0:slab, 0:D]
    small_ref[LATE : LATE + EARLY, :] = joint[slab:, 0:D]


def last_totals(order, total_a, part_b, *rest):
    *rest, slab = rest
    operands = [total_a, *part_b.pair, *rest]
    plain = sds((slab, DL), F32)
    wide = sds((slab, FL), F32)
    shapes = (plain,) * 4 + (wide, wide, sds((LATE + EARLY, D), F32))
    return order(
        last_totals_kernel, operands, whole_blocks(operands), shapes, whole_blocks(shapes),
        grid=(1,), name="last_totals",
    )


def gather_early_kernel(f0, f1, f2, out):
    sums = f0[...] + f1[...] + f2[...]
    out[...] = jnp.zeros(out.shape, F32)
    out[0:1, :] = sums[0:1, 0:D]
    out[1:2, :] = sums[0:1, D:FL]
    out[2:5, :] = sums[1:4, 0:D]


def gather_early(order, sums, into):
    (early,), moved = order(
        gather_early_kernel, sums, [vmem()] * 3, (sds((EARLY, D), F32),), [vmem()], into=into,
        name="gather_early",
    )
    return early, moved


def gather_late_kernel(taps, a0, a1, a2, bias, tab, out):
    out[...] = jnp.zeros(out.shape, F32)
    out[0:16, :] = taps[0:16, :]
    out[16:19, :] = (a0[...] + a1[...] + a2[...])[0:3]
    out[19:20, :] = bias[0:1, :]
    for h in range(HL):
        at = 256 * (h % 3)
        out[20 + h // 3 : 21 + h // 3, at : at + 256] = tab[h : h + 1, :]


def gather_late(order, *rest):
    return order(
        gather_late_kernel, rest, [vmem()] * 6, (sds((LATE, D), F32),), [vmem()],
        name="gather_late",
    )[0]


def finish_kernel(
    place_ref, own, core, other, both,
    text, patch, out_b, gain1, shift1, outer_b, gain2, shift2,
    query_b, value_b, inner_b, line, width, height,
):
    small = own[...] + core[...]
    slab = patch.shape[1]
    turn = lambda a: pltpu.roll(a, lax.rem(D - place_ref[0] * slab, D), 1)[:, 0:slab]
    shard = turn(small)
    taps = shard[0:16] + turn(other[...] + both[...])
    for dilate in range(3):
        for tap in range(3):
            text[dilate, tap] = taps[3 + (tap - 1) * (dilate + 1)]
    patch[...] = taps[7:16]
    rows = (16, 17, 18, LATE + 2, LATE + 3, LATE + 4)
    for i, ref in zip(rows, (out_b, gain1, shift1, outer_b, gain2, shift2)):
        ref[...] = shard[i]
    query_b[...] = small[19, 0:DL]
    value_b[...] = small[19, DL:D]
    inner_b[0:D] = small[LATE]
    inner_b[D:FL] = small[LATE + 1]
    for h in range(HL):
        row, at = 20 + h // 3, 256 * (h % 3)
        line[h : h + 1, :] = small[row : row + 1, at : at + 32]
        width[h : h + 1, :] = small[row : row + 1, at + 32 : at + 96]
        height[h : h + 1, :] = small[row : row + 1, at + 96 : at + 160]


def finish(order, place, own, core, other, both, slab):
    f = lambda *shape: sds(shape, F32)
    shapes = (f(3, 3, slab), f(9, slab)) + (f(slab),) * 6
    shapes += (f(DL), f(DL), f(FL), f(HL, 32), f(HL, 64), f(HL, 64))
    return order(
        finish_kernel, (place, own, core, other, both),
        [smem()] + whole_blocks((own, core, other, both)), shapes, whole_blocks(shapes), grid=(1,),
        name="finish",
    )


def swap_both(x, dp):
    pairs = [(2 * i + t, 2 * (i ^ 1) + (t ^ 1)) for i in range(dp) for t in range(2)]
    return lax.ppermute(x, ("dp", "tensor"), pairs)


def per_device(
    dp,
    page_tokens,
    patch_counts,
    token_boxes,
    text_weight,
    patch_weight,
    query_weight,
    query_bias,
    key_weight,
    value_weight,
    value_bias,
    out_weight,
    out_bias,
    line_table,
    width_table,
    height_table,
    norm1_gain,
    norm1_shift,
    inner_weight,
    inner_bias,
    outer_weight,
    outer_bias,
    norm2_gain,
    norm2_shift,
    cotangent,
):
    place = lax.axis_index("dp")
    half = lax.axis_index("tensor")
    core = place % 2
    bits = [(place // 2**i) % 2 for i in range(4)]
    where = jnp.stack([half] + bits).astype(jnp.int32)
    x = page_tokens.reshape(SEQ, D)
    cot = cotangent.reshape(SEQ, D)
    slab = D // dp if dp == 16 else None
    order = Order()

    z, m, o, u, r, wo_mine, ur = make_tables(
        order,
        where,
        jnp.concatenate([jnp.transpose(a) for a in (line_table, width_table, height_table)], axis=1),
        token_boxes.reshape(2, SEQ),
        out_weight,
    )
    wo_a = swap_tensor(wo_mine)
    row = lax.broadcasted_iota(jnp.int32, (8, 1), 0)
    bias = jnp.where(row == 0, query_bias[None, :], value_bias[None, :]).astype(F32)
    (q0, q1, q2, k, v), enc, enc_low, (o_far, ur_far, r_far) = encode(
        order, patch_counts, x, text_weight, patch_weight, bias,
        query_weight, key_weight, value_weight, (o, ur, r),
    )
    q = (q0, q1, q2)

    vec = jnp.zeros((8, 1), F32)
    for i, a in enumerate(
        (out_bias, norm1_gain, norm1_shift, outer_bias, norm2_gain, norm2_shift)
    ):
        vec = jnp.where(row == i, a[None, :].astype(F32), vec)
    bi = jnp.broadcast_to(inner_bias[None, :].astype(F32), (8, FL))
    probs, mix, mix_low, mix_other = ([None] * 3 for _ in range(4))
    xhat, rstd, hlow, act, slope, outer, outer_other = ([None] * 3 for _ in range(7))

    def attention_of(c, out):
        (p, a, low), far = attend(order, c, patch_counts, q[c], k, v, u, r, m, o, z, out)
        mix[c], mix_other[c] = a, swap_tensor(a)
        return (p, low), far

    def feed_of(c, out=()):
        got = feed(
            order, c, where, mix[c], mix_other[c], enc[c], vec, out_weight, wo_a, wo_b,
            inner_weight, bi, outer_weight, out,
        )
        far = None
        if out:
            got, far = got
        for keep, a in zip((xhat, rstd, hlow, act, slope, outer), got):
            keep[c] = a
        outer_other[c] = swap_tensor(got[5])
        return far

    near, enc = attention_of(ORDER[0], enc)
    wo_a = pass_on(order, wo_a)
    wo_b = swap_dp(wo_a, 1, dp)
    near, (probs[ORDER[0]], mix_low[ORDER[0]]) = attention_of(ORDER[1], near)
    near, (probs[ORDER[1]], mix_low[ORDER[1]]) = attention_of(ORDER[2], near)
    probs[ORDER[2]], mix_low[ORDER[2]] = feed_of(ORDER[0], near)
    enc_low = feed_of(ORDER[1], enc_low)
    *q_far, k_far, v_far = feed_of(ORDER[2], (q0, q1, q2, k, v))
    layer_out, inner_grad, outer_grad = None, None, None
    dres2, g2, g1, dhid, dhid_other, sums2 = ([None] * 3 for _ in range(6))
    for c in ORDER:
        got = feed_back(
            order, c, patch_counts, outer[c], outer_other[c], xhat[c], cot, vec, outer_weight,
            slope[c], inner_weight, layer_out,
        )
        layer_out = got[0]
        for keep, a in zip((dres2, g2, g1, dhid, sums2), got[1:]):
            keep[c] = a
        dhid_other[c] = swap_tensor(got[4])
        last = c == ORDER[2]
        inner_grad = chunk_grads(
            order, slab, where, hlow[c], g1[c], inner_grad, last, f"inner_grads_{c}"
        )
        outer_grad = chunk_grads(
            order, slab, where, g2[c], act[c], outer_grad, last, f"outer_grads_{c}"
        )
        if not last:
            inner_grad, outer_grad = inner_grad[0], outer_grad[0]
    scatter = functools.partial(Scatter, order, dp, where)
    x_first, z_first = (1, 2, 3), (2, 3, 1)
    inner_pair, outer_pair = swap_core(inner_grad, dp), swap_core(outer_grad, dp)
    inner = scatter(inner_pair, x_first, "inner", 0, D)
    inner_b = scatter(inner_pair, x_first, "inner_b", D, D)
    outer_a = scatter(outer_pair, x_first, "outer_a", 0, D)
    outer_b = scatter(outer_pair, z_first, "outer_b", D, D)
    early, (prob,) = gather_early(order, sums2, (probs[ORDER[0]],))
    carry = None
    dres1, g0, dq, sums1 = ([None] * 3 for _ in range(4))
    for c in ORDER:
        got = norm_one_back(
            order, c, dres2[c], dhid[c], dhid_other[c], xhat[c], rstd[c], vec, out_weight
        )
        dres1[c], g0[c], _, sums1[c] = got
        if c == ORDER[0]:
            inner.step()
            outer_b.step()
            inner_b.step(early)
        if c == ORDER[1]:
            outer_a.step()
            inner.step()
            outer_b.step()
        if c == ORDER[2]:
            inner_b.step()
            inner.step()
            outer_b.step()
        into = [probs[after] for after in ORDER[ORDER.index(c) + 1 :][:1]]
        if not into:
            into = [query_weight, key_weight, value_weight]
        got = attend_back(
            order, c, got[2], prob, q_far[c], k_far, v_far, ur_far, r_far, o_far, carry, into
        )
        got, into = got
        prob = into[0]
        dq[c], *carry = got
    weights = into
    dk, dv, dm, dz = carry
    if dp == 16:
        total_outer_b = total_of(order, outer_b, "outer_b_total")
        total_inner = total_of(order, inner, "inner_total")
    outer_a.step()
    if dp == 16:
        inner_b = total_of(order, inner_b, "inner_b_sum")
    operands = (enc_low, dq, dk, dv, g0, mix_low)
    if dp == 16:
        got = attention_grads(order, slab, where, *operands)
        first_pair, second_pair = swap_core(got[0:2], dp), swap_core(got[2:4], dp)
    else:
        first_pair = second_pair = plain_grads(order, *operands)
    rest = 0 if dp == 16 else SPLIT
    part_a = scatter(first_pair, x_first, "part_a", 0, SPLIT)
    part_b = scatter(second_pair, x_first, "part_b", rest, 4 * DL - SPLIT)
    part, bias_sums = project_back(order, dq, dk, dv, *weights)
    part_other = swap_tensor(part)
    part_a.step()
    tables = table_sums(order, dm, dz)
    taps = tap_sums(order, patch_counts, x, part, dres1)
    late = gather_late(order, taps, *sums1, bias_sums, tables)
    if dp == 16:
        joint = joint_step(order, dp, where, inner_b, outer_a)
    part_b.step(late)
    part_a.step()
    if dp == 16:
        joint = add_blocks(order, *joint, "joint_total")
    part_a.step()
    part_b.step()
    if dp == 16:
        total_a = total_of(order, part_a, "part_a_total")
    part_b.step()
    input_grad = decode(order, patch_counts, text_weight, patch_weight, part, part_other, dres1)
    if dp == 16:
        grad_q, grad_k, grad_v, grad_o, sum_outer, inner_total, small = last_totals(
            order, total_a, part_b, joint, total_outer_b, total_inner, slab
        )
    else:
        inner_total = jnp.concatenate([inner.total(), inner_b.total()], axis=1)
        sum_outer = jnp.concatenate([outer_a.total(), outer_b.total()], axis=1)
        both = jnp.concatenate([part_a.total(), part_b.total()], axis=1)
        grad_q, grad_k, grad_v, grad_o = jnp.split(both, 4, axis=1)
        small = jnp.concatenate([late, early], axis=0)
        bit = 2
        while bit < dp:
            small = small + swap_dp(small, bit, dp)
            bit *= 2
    small_others = (
        swap_dp(small, 1, dp), swap_tensor(small[0:16]), swap_both(small[0:16], dp)
    )
    small = finish(
        order, jnp.reshape(place, (1,)).astype(jnp.int32), small, *small_others, D // dp
    )
    text, patch, out_b, gain1, shift1, outer_b, gain2, shift2 = small[:8]
    query_b, value_b, inner_b, line, width, height = small[8:]
    return (
        layer_out.reshape(1, SEQ, D),
        input_grad.reshape(1, SEQ, D),
        text,
        patch,
        grad_q,
        query_b,
        grad_k,
        grad_v,
        value_b,
        jnp.transpose(grad_o),
        out_b,
        jnp.transpose(line),
        jnp.transpose(width),
        jnp.transpose(height),
        gain1,
        shift1,
        inner_total,
        inner_b,
        jnp.transpose(sum_outer),
        outer_b,
        gain2,
        shift2,
    )


def solution(mesh):
    placed = (
        P("dp", None, None),
        P("dp"),
        P("dp", None, None),
        P(),
        P(),
        P(None, "tensor"),
        P("tensor"),
        P(None, "tensor"),
        P(None, "tensor"),
        P("tensor"),
        P("tensor", None),
        P(),
        P(None, "tensor"),
        P(None, "tensor"),
        P(None, "tensor"),
        P(),
        P(),
        P(None, "tensor"),
        P("tensor"),
        P("tensor", None),
        P(),
        P(),
        P(),
        P("dp", None, None),
    )
    return jax.shard_map(
        functools.partial(per_device, mesh.shape["dp"]),
        mesh=mesh,
        in_specs=placed,
        out_specs=(
            P("dp", None, None),
            P("dp", None, None),
            P(None, None, "dp"),
            P(None, "dp"),
            P("dp", "tensor"),
            P("tensor"),
            P("dp", "tensor"),
            P("dp", "tensor"),
            P("tensor"),
            P("tensor", "dp"),
            P("dp"),
            P(None, "tensor"),
            P(None, "tensor"),
            P(None, "tensor"),
            P("dp"),
            P("dp"),
            P("dp", "tensor"),
            P("tensor"),
            P("tensor", "dp"),
            P("dp"),
            P("dp"),
            P("dp"),
        ),
        check_vma=False,
    )
```
